128 devices in a mesh: replica: 64 (over z, x_lo, y, core), group: 2 (over x_hi).
Axes of the slice: x: 4 (x_hi: 2, x_lo: 2; x = x_hi * 2 + x_lo), y: 4, z: 4, core: 2. Of those that a mesh axis runs over, the one named last changes fastest.
Arguments:
- tokens: bfloat16 [64, 512, 768], P('replica', 'group'), may hold values from -6 to 6
- cotangent: bfloat16 [64, 512, 768], P('replica', 'group'), may hold values from -6 to 6
- owner: int32 [35], replicated, may hold values from 0 to 63, as said below
- norm_gains: bfloat16 [2, 2, 768], P(None, None, 'replica'), may hold values from 0.5 to 1.5
- shifts: bfloat16 [2, 4, 768], P(None, None, 'replica'), may hold values from -3 to 3
- qkv_weight: bfloat16 [2, 768, 3, 768], P(None, 'replica', None, 'group'), may hold values from -0.3125 to 0.3125
- qv_bias: bfloat16 [2, 2, 2, 384], P(None, None, 'group', 'replica'), may hold values from -3 to 3
- out_weight: bfloat16 [2, 768, 768], P(None, 'group', 'replica'), may hold values from -0.625 to 0.625
- up_weight: bfloat16 [2, 768, 3072], P(None, 'replica', 'group'), may hold values from -0.21875 to 0.21875
- up_bias: bfloat16 [2, 2, 1536], P(None, 'group', 'replica'), may hold values from -3 to 3
- down_weight: bfloat16 [2, 3072, 768], P(None, 'group', 'replica'), may hold values from -0.15625 to 0.15625
Outputs:
- mixed_out: bfloat16 [64, 512, 768], P('replica', 'group')
- input_grad: bfloat16 [64, 512, 768], P('replica', 'group')
- norm_gains_grad: float32 [2, 2, 768], P(None, None, 'replica')
- shifts_grad: float32 [2, 4, 768], P(None, None, 'replica')
- qkv_weight_grad: float32 [2, 768, 3, 768], P(None, 'replica', None, 'group')
- qv_bias_grad: float32 [2, 2, 2, 384], P(None, None, 'group', 'replica')
- out_weight_grad: float32 [2, 768, 768], P(None, 'group', 'replica')
- up_weight_grad: float32 [2, 768, 3072], P(None, 'replica', 'group')
- up_bias_grad: float32 [2, 2, 1536], P(None, 'group', 'replica')
- down_weight_grad: float32 [2, 3072, 768], P(None, 'group', 'replica')
The draws below stay inside these ranges and needn't reach their ends.
Inputs may be any that keep to these rules, and one draw needn't show every extreme that they name: `owner`: 35 different slots; slots 0 and 63 hold an image in every draw.
All inputs are finite; a program needn't handle non-finite values.
Results may differ from the reference program's by a relative error of at most 0.028.
Values may be sent and summed in bfloat16 or wider, within the bound.
No kernel may reach another device: no remote copies, remote signals or barrier semaphores. Data moves between devices by JAX's collectives and lax.ppermute only.
A program may use at most 192 MiB of HBM per device.

```python
import math
import jax
import jax.numpy as jnp
from jax import lax

HEAD = 64
D = 768
FF = 3072
LEN = 512
LAYERS = 2
IMAGES = 35
SLOTS = 64
N_REPLICA = 64
N_GROUP = 2


def draw_owner(key, part):
    key = jax.random.fold_in(key, 7)
    first_key, second_key = jax.random.split(key)
    middle = 1 + jax.random.permutation(first_key, N_REPLICA - 2)[:IMAGES - 2]
    chosen = jnp.concatenate([jnp.array([0, N_REPLICA - 1], jnp.int32), middle.astype(jnp.int32)])
    return jax.random.permutation(second_key, chosen).astype(jnp.int32)


def block_scale(rng, dims, cuts, least, top_value):
    level = 1.0
    for position, shards_of in cuts:
        draws = jax.random.uniform(jax.random.fold_in(jax.random.fold_in(rng, 6), position), (shards_of,), jnp.float32, least / len(cuts), top_value / len(cuts))
        level = level * jnp.repeat(jnp.exp(draws), dims[position] // shards_of).reshape((-1,) + (1,) * (len(dims) - 1 - position))
    return level


def noise(rng, extent, scale, reach, shards=(), kind=jnp.bfloat16):
    values = jax.random.normal(rng, extent, jnp.float32) * scale
    if len(shards) > 0:
        values = block_scale(rng, extent, shards, -0.22, 0.18) * values
    return jnp.clip(values, min=-reach, max=reach).astype(kind)


def setup_inputs(seed: int = 0) -> dict:
    keys = jax.random.split(jax.random.key(seed), 12)
    tokens = noise(keys[0], (SLOTS, LEN, D), 1.0, 6.0, ((0, 64), (1, 2)))
    cotangent = noise(keys[1], (SLOTS, LEN, D), 1.0, 6.0, ((0, 64), (1, 2)))
    owner = draw_owner(jax.random.fold_in(keys[11], 71), 0)
    norm_gains = jnp.clip(1.0 + 0.1 * jax.random.normal(keys[3], (LAYERS, 2, D), jnp.float32), 0.5, 1.5).astype(jnp.bfloat16)
    shifts = noise(keys[4], (LAYERS, 4, D), 0.5, 3.0, ((2, 64),))
    qkv_weight = noise(keys[5], (LAYERS, D, 3, D), (D // 2) ** -0.5, 0.3125, ((1, 64), (3, 2)))
    qv_bias = noise(keys[6], (LAYERS, 2, N_GROUP, D // N_GROUP), 0.5, 3.0, ((2, 2), (3, 64)))
    out_weight = noise(keys[7], (LAYERS, D, D), (D // 8) ** -0.5, 0.625, ((1, 2), (2, 64)))
    up_weight = noise(keys[8], (LAYERS, D, FF), D ** -0.5, 0.21875, ((1, 64), (2, 2)))
    up_bias = noise(keys[9], (LAYERS, N_GROUP, FF // N_GROUP), 0.5, 3.0, ((1, 2), (2, 64)))
    down_weight = noise(keys[10], (LAYERS, FF, D), (FF // 2) ** -0.5, 0.15625, ((1, 2), (2, 64)))
    return {"tokens": tokens, "cotangent": cotangent, "owner": owner, "norm_gains": norm_gains, "shifts": shifts, "qkv_weight": qkv_weight, "qv_bias": qv_bias, "out_weight": out_weight, "up_weight": up_weight, "up_bias": up_bias, "down_weight": down_weight}


@jax.custom_vjp
def low(v):
    return lax.optimization_barrier(v.astype(jnp.bfloat16)).astype(jnp.float32)

@jax.custom_vjp
def low_back(v):
    return v

def low_keep(v):
    return (low(v), None)

def low_pass(kept, grad):
    return (grad,)

def back_keep(v):
    return (v, None)

def back_low(kept, grad):
    return (low(grad),)
low.defvjp(low_keep, low_pass)
low_back.defvjp(back_keep, back_low)
highest = lax.Precision.HIGHEST
epsilon = 1e-06

def norm_rows(values, gain_row, shift_row):
    average = lax.optimization_barrier(jnp.mean(values, axis=-1, keepdims=True))
    centred = values - average
    spread = lax.optimization_barrier(jnp.mean(centred * centred, axis=-1, keepdims=True))
    return centred * lax.rsqrt(spread + epsilon) * gain_row + shift_row

def layer_forward(stream, params):
    gains, shifts, qkv_w, qv_b, out_w, up_w, up_b, down_w = params
    length = stream.shape[0]
    features = stream.shape[1]
    head_count = features // HEAD
    scaling = 1.0 / math.sqrt(HEAD)
    first_rows = low(norm_rows(stream, gains[0], shifts[0]))
    projected = jnp.dot(first_rows, qkv_w.reshape(features, 3 * features), precision=highest).reshape(length, 3, features)
    biases = qv_b.reshape(2, features)
    queries = low_back(low(projected[:, 0] + biases[0])).reshape(length, head_count, HEAD)
    key_rows = low_back(low(projected[:, 1])).reshape(length, head_count, HEAD)
    value_rows = low_back(low(projected[:, 2] + biases[1])).reshape(length, head_count, HEAD)
    scores = low_back(jnp.einsum('qhd,khd->hqk', queries, key_rows, precision=highest) * scaling)
    highest_score = lax.optimization_barrier(jnp.max(scores, axis=-1, keepdims=True))
    log_total = highest_score + jnp.log(lax.optimization_barrier(jnp.sum(jnp.exp(scores - highest_score), axis=-1, keepdims=True)))
    attn_probs = low(jnp.exp(scores - log_total))
    attended = jnp.einsum('hqk,khd->qhd', attn_probs, value_rows, precision=highest).reshape(length, features)
    attended = low_back(low(attended))
    middle = stream + low_back(jnp.dot(attended, out_w, precision=highest)) + shifts[1]
    second = low(norm_rows(middle, gains[1], shifts[2]))
    up_act = low_back(jnp.dot(second, up_w, precision=highest) + up_b.reshape(-1))
    hidden = low(jax.nn.gelu(up_act, approximate=False))
    return middle + low_back(jnp.dot(hidden, down_w, precision=highest)) + shifts[3]

def forward(pictures, params):

    def per_image(carried, picture):
        values = picture
        for number in range(LAYERS):
            values = layer_forward(values, tuple((array[number] for array in params)))
        return (carried, values)
    _, outputs = lax.scan(jax.checkpoint(per_image), jnp.zeros((), jnp.float32), pictures)
    return outputs

def reference(tokens, cotangent, owner, norm_gains, shifts, qkv_weight, qv_bias, out_weight, up_weight, up_bias, down_weight):
    params = tuple((array.astype(jnp.float32) for array in (norm_gains, shifts, qkv_weight, qv_bias, out_weight, up_weight, up_bias, down_weight)))
    pictures = tokens.astype(jnp.float32)[owner]
    cotangent_img = cotangent.astype(jnp.float32)[owner]
    outputs, pullback = jax.vjp(forward, pictures, params)
    picture_grads, param_grads = pullback(cotangent_img)
    blank = jnp.zeros((N_REPLICA, LEN, D), jnp.float32)
    mixed_out = blank.at[owner].set(outputs).astype(jnp.bfloat16)
    input_grad = blank.at[owner].set(picture_grads).astype(jnp.bfloat16)
    return (mixed_out, input_grad, param_grads[0], param_grads[1], param_grads[2], param_grads[3], param_grads[4], param_grads[5], param_grads[6], param_grads[7])
```

```python
import math

import jax
import jax.numpy as jnp
from jax import lax
from jax.sharding import Mesh
from jax.sharding import PartitionSpec as P

HEAD = 64
LAYERS = 2
WIDTH = 768
HALF = WIDTH // 2
UNITS = 1536
COLS = 1152
ROWS = 12
F32 = jnp.float32
BF16 = jnp.bfloat16
epsilon = 1e-06

SIZES = (4, 2, 4, 2, 2)
AXES = ("z", "xl", "y", "c", "xh")
REPLICA = ("z", "xl", "y", "c")

RING = {"z": (0, 1, 2, 3), "y": (0, 1, 2, 3), "x": (0, 2, 1, 3)}
NAMES = {"z": "z", "y": "y", "x": ("xl", "xh")}


def hop(values, axis, steps):
    ring = RING[axis]
    return lax.ppermute(
        values, NAMES[axis], [(ring[i], ring[(i + steps) % 4]) for i in range(4)]
    )


def slot_of(axis, offset):
    if axis == "x":
        slot = (lax.axis_index("xl") + 2 * lax.axis_index("xh") + offset) % 4
        return (slot % 2) * 2 + slot // 2
    return (lax.axis_index(axis) + offset) % 4


def put(out, values, place):
    return lax.dynamic_update_slice(out, values[None], (place,) + (0,) * values.ndim)


def take(values, place):
    return lax.dynamic_index_in_dim(values, place, 0, keepdims=False)


def ring_gather(values, axis, direct):
    left, right = hop(values, axis, 1), hop(values, axis, -1)
    if direct:
        across = hop(values, axis, 2)
    else:
        cut = values.shape[0] // 2
        across = jnp.concatenate([hop(left[:cut], axis, 1), hop(right[cut:], axis, -1)])
    out = jnp.zeros((4,) + values.shape, values.dtype)
    for offset, block in ((0, values), (3, left), (1, right), (2, across)):
        out = put(out, block, slot_of(axis, offset))
    return out


def plus(first, *others):
    total = first.astype(F32)
    for other in others:
        total = total + other.astype(F32)
    return total.astype(BF16)


def ring_reduce(values, axis, direct):
    mine, to_right, across, to_left = (take(values, slot_of(axis, n)) for n in range(4))
    if direct:
        return plus(mine, hop(to_right, axis, 1), hop(to_left, axis, -1), hop(across, axis, 2))
    cut = mine.shape[0] // 2
    first = hop(across[:cut], axis, 1)
    second = hop(across[cut:], axis, -1)
    to_right = jnp.concatenate([plus(to_right[:cut], first), to_right[cut:]])
    to_left = jnp.concatenate([to_left[:cut], plus(to_left[cut:], second)])
    return plus(mine, hop(to_right, axis, 1), hop(to_left, axis, -1))


def gather_chips(slab):
    both = ring_gather(slab[:2], "x", True)
    third = ring_gather(slab[2], "y", True)
    first = ring_gather(both[:, 0], "y", False)
    pair = ring_gather(jnp.concatenate([both[:, 1], third]), "z", False)
    first = ring_gather(first, "z", False)
    second = ring_gather(pair[:, :4], "y", False)
    third = ring_gather(pair[:, 4:], "x", False)
    return (
        jnp.swapaxes(first, 1, 2),
        jnp.moveaxis(second, 0, 2),
        jnp.swapaxes(third, 0, 1),
    )


def reduce_chips(first, second, third):
    first = ring_reduce(jnp.swapaxes(first, 1, 2), "z", False)
    second = ring_reduce(jnp.moveaxis(second, 2, 0), "y", False)
    third = ring_reduce(jnp.swapaxes(third, 0, 1), "x", False)
    first = ring_reduce(first, "y", False)
    pair = ring_reduce(jnp.concatenate([second, third], axis=1), "z", False)
    both = ring_reduce(jnp.stack([first, pair[:4]], axis=1), "x", True)
    third = ring_reduce(pair[4:], "y", True)
    return jnp.concatenate([both, third[None]])


def turn(values, step):
    pairs = [
        (y * 4 + c * 2 + h, ((y + step) % 4) * 4 + h * 2 + c)
        for y in range(4)
        for c in range(2)
        for h in range(2)
    ]
    return lax.ppermute(values, ("y", "c", "xh"), pairs)


def swap(values):
    return lax.ppermute(values, ("c", "xh"), [(0, 0), (1, 2), (2, 1), (3, 3)])


def trade(values):
    return lax.ppermute(values, "c", [(0, 1), (1, 0)])


def total_of(part):
    part = part.astype(BF16)
    return part.astype(F32) + trade(part).astype(F32)


def fetch_weights(qkv_w, out_w, up_w, down_w):
    packed = jnp.concatenate(
        [
            qkv_w.reshape(LAYERS, ROWS, 3 * HALF),
            jnp.swapaxes(out_w, 1, 2),
            up_w,
            jnp.swapaxes(down_w, 1, 2),
        ],
        axis=2,
    ).reshape(LAYERS, ROWS, 4, COLS)
    packed = jnp.moveaxis(packed, 2, 0)
    slab = jnp.zeros((4, LAYERS, ROWS, COLS), BF16)
    y = lax.axis_index("y")
    for step in range(4):
        slab = put(slab, turn(take(packed, (y + step) % 4), step), (y - step) % 4)
    slab = jnp.moveaxis(slab, 0, 1).reshape(LAYERS, 3, 16, COLS)
    parts = gather_chips(jnp.moveaxis(slab, 1, 0))

    def rows(number, group, low, high):
        return jnp.stack(
            [part[:, :, group, number, :, low:high] for part in parts], axis=2
        ).reshape(WIDTH, high - low)

    layers = []
    for number in range(LAYERS):
        layers.append(
            (
                rows(number, 0, 0, COLS),
                rows(number, 1, 0, HALF),
                jnp.concatenate(
                    [rows(number, 1, HALF, COLS), rows(number, 2, 0, WIDTH)], axis=1
                ),
                jnp.concatenate(
                    [rows(number, 2, WIDTH, COLS), rows(number, 3, 0, COLS)], axis=1
                ),
            )
        )
    return layers


def return_weights(grads):
    parts = [[], [], []]
    for qkv_g, out_g, up_g, down_g in grads:
        whole = jnp.stack(
            [
                qkv_g,
                jnp.concatenate([out_g, up_g[:, :WIDTH]], axis=1),
                jnp.concatenate([up_g[:, WIDTH:], down_g[:, :HALF]], axis=1),
                down_g[:, HALF:],
            ]
        ).reshape(4, 4, 4, 3, 16, COLS)
        for number in range(3):
            parts[number].append(jnp.moveaxis(whole[:, :, :, number], 0, 2))
    slab = reduce_chips(*(jnp.stack(part, axis=3) for part in parts))
    slab = jnp.moveaxis(slab, 0, 1).reshape(LAYERS, 4, ROWS, COLS)
    slab = jnp.moveaxis(slab, 1, 0)
    out = jnp.zeros((4, LAYERS, ROWS, COLS), BF16)
    y = lax.axis_index("y")
    for step in range(4):
        out = put(out, turn(take(slab, (y + step) % 4), step), (y - step) % 4)
    out = jnp.moveaxis(out, 0, 2).reshape(LAYERS, ROWS, 4 * COLS).astype(F32)
    return (
        out[:, :, :COLS].reshape(LAYERS, ROWS, 3, HALF),
        jnp.swapaxes(out[:, :, COLS : COLS + HALF], 1, 2),
        out[:, :, COLS + HALF : COLS + HALF + UNITS],
        jnp.swapaxes(out[:, :, COLS + HALF + UNITS :], 1, 2),
    )


def fetch_small(gains, shifts, qv_b, up_b):
    packed = jnp.concatenate(
        [
            gains.reshape(LAYERS, 24),
            shifts.reshape(LAYERS, 48),
            qv_b.reshape(LAYERS, 12),
            up_b.reshape(LAYERS, 24),
            jnp.zeros((LAYERS, 20), BF16),
        ],
        axis=1,
    )
    copies = jnp.broadcast_to(packed[None], (128, LAYERS, 128))
    every = lax.all_to_all(copies, AXES, split_axis=0, concat_axis=0, tiled=True)
    every = every.reshape(4, 2, 4, 2, 2, LAYERS, 128).astype(F32)
    shared = every[:, :, :, :, 0, :, :72].reshape(4, 2, 4, 2, LAYERS, 6, ROWS)
    shared = shared.transpose(4, 5, 0, 1, 3, 2, 6).reshape(LAYERS, 6, WIDTH)
    halves = lax.dynamic_index_in_dim(every, lax.axis_index("c"), 4, keepdims=False)
    halves = halves.reshape(64, LAYERS, 128)
    qv = halves[:, :, 72:84].reshape(64, LAYERS, 2, 6).transpose(1, 2, 0, 3)
    up = halves[:, :, 84:108].transpose(1, 0, 2)
    return shared, qv.reshape(LAYERS, 2, HALF), up.reshape(LAYERS, UNITS)


def return_small(shared, qv, up):
    shared = 0.5 * jnp.stack(shared).reshape(LAYERS, 6, 4, 2, 2, 4, ROWS)
    shared = shared.transpose(2, 3, 5, 4, 0, 1, 6).reshape(64, LAYERS, 72)
    qv = jnp.stack(qv).reshape(LAYERS, 2, 64, 6).transpose(2, 0, 1, 3).reshape(64, LAYERS, 12)
    up = jnp.stack(up).reshape(LAYERS, 64, 24).transpose(1, 0, 2)
    core = lax.axis_index("c")
    chunks = jnp.stack(
        [
            jnp.concatenate(
                [
                    shared,
                    jnp.where(core == half, qv, 0.0),
                    jnp.where(core == half, up, 0.0),
                    jnp.zeros((64, LAYERS, 20), F32),
                ],
                axis=2,
            )
            for half in range(2)
        ],
        axis=1,
    ).reshape(128, LAYERS, 128)
    mine = jnp.sum(
        lax.all_to_all(chunks, AXES, split_axis=0, concat_axis=0, tiled=True), axis=0
    )
    return (
        mine[:, :24].reshape(LAYERS, 2, ROWS),
        mine[:, 24:72].reshape(LAYERS, 4, ROWS),
        mine[:, 72:84].reshape(LAYERS, 2, 1, 6),
        mine[:, 84:108].reshape(LAYERS, 1, 24),
    )


def norm_parts(values):
    average = jnp.mean(values, axis=-1, keepdims=True)
    centred = values - average
    spread = jnp.mean(centred * centred, axis=-1, keepdims=True)
    inverse = lax.rsqrt(spread + epsilon)
    return centred * inverse, inverse


def norm_back(values, gain_row, upstream):
    normal, inverse = norm_parts(values)
    gain_grad = jnp.sum(upstream * normal, axis=0)
    shift_grad = jnp.sum(upstream, axis=0)
    scaled = upstream * gain_row
    back = inverse * (
        scaled
        - jnp.mean(scaled, axis=-1, keepdims=True)
        - normal * jnp.mean(scaled * normal, axis=-1, keepdims=True)
    )
    return back, gain_grad, shift_grad


def dot(a, b):
    return jnp.dot(a, b, preferred_element_type=F32)


def dot_rows(a, b):
    return lax.dot_general(a, b, (((1,), (1,)), ((), ())), preferred_element_type=F32)


def dot_columns(a, b):
    return lax.dot_general(a, b, (((0,), (0,)), ((), ())), preferred_element_type=F32)


def gelu_parts(up_act):
    cumulative = 0.5 * (1.0 + lax.erf(up_act * (1.0 / math.sqrt(2.0))))
    density = jnp.exp(-0.5 * up_act * up_act) * (1.0 / math.sqrt(2.0 * math.pi))
    return cumulative, density


def heads_of(values):
    return jnp.moveaxis(values.reshape(values.shape[0], -1, HEAD), 1, 0)


def columns_of(values):
    return jnp.moveaxis(values, 0, 1).reshape(values.shape[1], -1)


def layer_ahead(stream, weights, shared, qv_b, up_b):
    qkv_w, out_w, up_w, down_w = weights
    scaling = 1.0 / math.sqrt(HEAD)
    first = (norm_parts(stream)[0] * shared[0] + shared[2]).astype(BF16)
    bias = jnp.concatenate([qv_b[0], jnp.zeros((HALF,), F32), qv_b[1]])
    qkv = (dot(first, qkv_w) + bias).astype(BF16)
    heads = heads_of(qkv)
    count = HALF // HEAD
    queries, keys, values = heads[:count], heads[count : 2 * count], heads[2 * count :]
    scores = jnp.einsum("hqd,hkd->hqk", queries, keys, preferred_element_type=F32) * scaling
    top = jnp.max(scores, axis=-1, keepdims=True)
    log_total = top + jnp.log(jnp.sum(jnp.exp(scores - top), axis=-1, keepdims=True))
    probs = jnp.exp(scores - log_total).astype(BF16)
    attended = columns_of(
        jnp.einsum("hqk,hkd->hqd", probs, values, preferred_element_type=F32).astype(BF16)
    )
    middle = stream + total_of(dot_rows(attended, out_w)) + shared[3]
    second = (norm_parts(middle)[0] * shared[1] + shared[4]).astype(BF16)
    up_act = dot(second, up_w) + up_b
    hidden = (up_act * gelu_parts(up_act)[0]).astype(BF16)
    block_out = middle + total_of(dot_rows(hidden, down_w)) + shared[5]
    return block_out, (stream, first, queries, keys, values, log_total, attended, middle, second, up_act, hidden)


def layer_back(upstream, stored, weights, shared):
    qkv_w, out_w, up_w, down_w = weights
    stream, first, queries, keys, values, log_total, attended, middle, second, up_act, hidden = stored
    scaling = 1.0 / math.sqrt(HEAD)
    down_in = upstream.astype(BF16)
    down_bias_g = jnp.sum(upstream, axis=0)
    down_g = dot_columns(down_in, hidden).astype(BF16)
    hidden_g = dot(down_in, down_w)
    cumulative, density = gelu_parts(up_act)
    up_in = (hidden_g * (cumulative + up_act * density)).astype(BF16)
    up_g = dot_columns(second, up_in).astype(BF16)
    up_bias_g = jnp.sum(up_in.astype(F32), axis=0)
    back, gain_two, shift_two = norm_back(middle, shared[1], total_of(dot_rows(up_in, up_w)))
    middle_g = upstream + back
    out_in = middle_g.astype(BF16)
    out_bias_g = jnp.sum(middle_g, axis=0)
    out_g = dot_columns(out_in, attended).astype(BF16)
    attended_g = heads_of(dot(out_in, out_w).astype(BF16))
    scores = jnp.einsum("hqd,hkd->hqk", queries, keys, preferred_element_type=F32) * scaling
    probs = jnp.exp(scores - log_total)
    prob_g = jnp.einsum("hqd,hkd->hqk", attended_g, values, preferred_element_type=F32)
    value_g = jnp.einsum(
        "hqk,hqd->hkd", probs.astype(BF16), attended_g, preferred_element_type=F32
    ).astype(BF16)
    row_delta = jnp.sum(probs * prob_g, axis=-1, keepdims=True)
    score_g = (probs * (prob_g - row_delta)).astype(BF16)
    query_g = (
        jnp.einsum("hqk,hkd->hqd", score_g, keys, preferred_element_type=F32) * scaling
    ).astype(BF16)
    key_g = (
        jnp.einsum("hqk,hqd->hkd", score_g, queries, preferred_element_type=F32) * scaling
    ).astype(BF16)
    proj_g = columns_of(jnp.concatenate([query_g, key_g, value_g]))
    qkv_g = dot_columns(first, proj_g).astype(BF16)
    proj_sums = jnp.sum(proj_g.astype(F32), axis=0)
    qv_g = jnp.stack([proj_sums[:HALF], proj_sums[2 * HALF :]])
    back, gain_one, shift_one = norm_back(stream, shared[0], total_of(dot_rows(proj_g, qkv_w)))
    stream_g = middle_g + back
    shared_g = jnp.stack([gain_one, gain_two, shift_one, out_bias_g, shift_two, down_bias_g])
    return stream_g, (qkv_g, out_g, up_g, down_g), shared_g, qv_g, up_bias_g


def whole_image(rows):
    rows = swap(rows)
    other = trade(rows)
    core = lax.axis_index("c")
    out = put(jnp.zeros((2,) + rows.shape, rows.dtype), rows, core)
    return put(out, other, 1 - core).reshape(-1, WIDTH)


def image_half(values):
    return swap(take(values.reshape(2, -1, WIDTH), lax.axis_index("c")))[None]


def body(
    tokens,
    cotangent,
    owner,
    norm_gains,
    shifts,
    qkv_weight,
    qv_bias,
    out_weight,
    up_weight,
    up_bias,
    down_weight,
):
    z, xl, y, xh = (lax.axis_index(name) for name in ("z", "xl", "y", "xh"))
    image_no = ((z * 2 + xl) * 4 + y) * 2 + xh
    live_flag = jnp.sum((owner == image_no).astype(F32))
    position = lax.broadcasted_iota(jnp.int32, (WIDTH, WIDTH), 1)
    lead, rest = position // 96, position % 96
    natural = lead * 96 + ((rest % 48) // ROWS) * 24 + (rest // 48) * ROWS + rest % ROWS
    reorder = (lax.broadcasted_iota(jnp.int32, (WIDTH, WIDTH), 0) == natural).astype(BF16)
    weights = fetch_weights(qkv_weight, out_weight, up_weight, down_weight)
    shared, qv_b, up_b = fetch_small(norm_gains, shifts, qv_bias, up_bias)
    stream = dot(whole_image(tokens[0]), reorder)
    upstream = dot(whole_image(cotangent[0]), reorder) * live_flag
    stored = []
    for number in range(LAYERS):
        stream, kept = layer_ahead(stream, weights[number], shared[number], qv_b[number], up_b[number])
        stored.append(kept)
    mixed_out = image_half(dot_rows((stream * live_flag).astype(BF16), reorder).astype(BF16))
    grads, shared_g, qv_g, up_g = ([None] * LAYERS for _ in range(4))
    for number in reversed(range(LAYERS)):
        upstream, grads[number], shared_g[number], qv_g[number], up_g[number] = layer_back(
            upstream, stored[number], weights[number], shared[number]
        )
    input_grad = image_half(dot_rows(upstream.astype(BF16), reorder).astype(BF16))
    qkv_g, out_g, up_w_g, down_g = return_weights(grads)
    gains_g, shifts_g, qv_bias_g, up_bias_g = return_small(shared_g, qv_g, up_g)
    return (
        mixed_out,
        input_grad,
        gains_g,
        shifts_g,
        qkv_g,
        qv_bias_g,
        out_g,
        up_w_g,
        up_bias_g,
        down_g,
    )


def solution(mesh):
    parts = Mesh(mesh.devices.reshape(SIZES), AXES)
    return jax.shard_map(
        body,
        mesh=parts,
        in_specs=(
            P(REPLICA, "xh", None),
            P(REPLICA, "xh", None),
            P(),
            P(None, None, REPLICA),
            P(None, None, REPLICA),
            P(None, REPLICA, None, "xh"),
            P(None, None, "xh", REPLICA),
            P(None, "xh", REPLICA),
            P(None, REPLICA, "xh"),
            P(None, "xh", REPLICA),
            P(None, "xh", REPLICA),
        ),
        out_specs=(
            P(REPLICA, "xh", None),
            P(REPLICA, "xh", None),
            P(None, None, REPLICA),
            P(None, None, REPLICA),
            P(None, REPLICA, None, "xh"),
            P(None, None, "xh", REPLICA),
            P(None, "xh", REPLICA),
            P(None, REPLICA, "xh"),
            P(None, "xh", REPLICA),
            P(None, "xh", REPLICA),
        ),
        check_vma=False,
    )
```

```python
import math

import jax
import jax.numpy as jnp
from jax import lax
from jax.sharding import Mesh
from jax.sharding import PartitionSpec as P

HEAD = 64
LAYERS = 2
WIDTH = 768
HALF = WIDTH // 2
UNITS = 1536
COLS = 1152
ROWS = 12
F32 = jnp.float32
BF16 = jnp.bfloat16
epsilon = 1e-06

SIZES = (4, 2, 4, 2, 2)
AXES = ("z", "xl", "y", "c", "xh")
REPLICA = ("z", "xl", "y", "c")

RING = {"z": (0, 1, 2, 3), "y": (0, 1, 2, 3), "x": (0, 2, 1, 3)}
NAMES = {"z": "z", "y": "y", "x": ("xl", "xh")}


def hop(values, axis, steps):
    ring = RING[axis]
    return lax.ppermute(
        values, NAMES[axis], [(ring[i], ring[(i + steps) % 4]) for i in range(4)]
    )


def slot_of(axis, offset):
    if axis == "x":
        slot = (lax.axis_index("xl") + 2 * lax.axis_index("xh") + offset) % 4
        return (slot % 2) * 2 + slot // 2
    return (lax.axis_index(axis) + offset) % 4


def put(out, values, place):
    return lax.dynamic_update_slice(out, values[None], (place,) + (0,) * values.ndim)


def take(values, place):
    return lax.dynamic_index_in_dim(values, place, 0, keepdims=False)


def round_hop(values, axis):
    ring = RING[axis]
    pairs = []
    for core in range(2):
        for i in range(4):
            src, dst = ring[i], ring[(i + 1 - 2 * core) % 4]
            if axis == "x":
                spot = lambda at: (at // 2) * 4 + core * 2 + at % 2
            else:
                spot = lambda at: at * 2 + core
            pairs.append((spot(src), spot(dst)))
    names = ("xl", "c", "xh") if axis == "x" else (axis, "c")
    return lax.ppermute(values, names, pairs)


def core_slot(axis, offset):
    return slot_of(axis, offset * (1 - 2 * lax.axis_index("c")))


def together(values):
    return list(lax.optimization_barrier(tuple(values)))


def plus(first, *others):
    total = first.astype(F32)
    for other in others:
        total = total + other.astype(F32)
    return total.astype(BF16)


def assemble(pieces):
    out = jnp.zeros((4,) + pieces[0][1].shape, pieces[0][1].dtype)
    for place, block in pieces:
        out = put(out, block, place)
    return out


def gather_direct(arrays, axes):
    arrays = together(arrays)
    moved = [[hop(v, axis, n) for n in (1, -1, 2)] for v, axis in zip(arrays, axes)]
    return [
        assemble([(slot_of(axis, n), b) for n, b in zip((0, 3, 1, 2), [v] + parts)])
        for v, axis, parts in zip(arrays, axes, moved)
    ]


def gather_round(arrays, axes):
    arrays = together(arrays)
    pieces = [[(core_slot(axis, 0), v)] for v, axis in zip(arrays, axes)]
    for step in range(1, 4):
        arrays = [round_hop(v, axis) for v, axis in zip(arrays, axes)]
        for k, axis in enumerate(axes):
            pieces[k].append((core_slot(axis, -step), arrays[k]))
    return [assemble(found) for found in pieces]


def reduce_direct(arrays, axes):
    arrays = together(arrays)
    out = []
    for v, axis in zip(arrays, axes):
        mine, after, across, before = (take(v, slot_of(axis, n)) for n in range(4))
        out.append((mine, hop(after, axis, 1), hop(before, axis, -1), hop(across, axis, 2)))
    return [plus(*found) for found in out]


def reduce_round(arrays, axes):
    arrays = together(arrays)
    moving = [take(v, core_slot(axis, 3)) for v, axis in zip(arrays, axes)]
    for offset in (2, 1, 0):
        moving = [round_hop(m, axis) for m, axis in zip(moving, axes)]
        moving = [
            plus(take(v, core_slot(axis, offset)), m)
            for v, m, axis in zip(arrays, moving, axes)
        ]
    return moving


def gather_chips(slab):
    both, third = gather_direct([slab[:2], slab[2]], ["x", "y"])
    first, pair = gather_direct(
        [both[:, 0], jnp.concatenate([both[:, 1], third])], ["y", "z"]
    )
    first, second, third = gather_round([first, pair[:, :4], pair[:, 4:]], ["z", "y", "x"])
    return (
        jnp.swapaxes(first, 1, 2),
        jnp.moveaxis(second, 0, 2),
        jnp.swapaxes(third, 0, 1),
    )


def reduce_chips(first, second, third):
    first, second, third = reduce_round(
        [jnp.swapaxes(first, 1, 2), jnp.moveaxis(second, 2, 0), jnp.swapaxes(third, 0, 1)],
        ["z", "y", "x"],
    )
    first, pair = reduce_direct([first, jnp.concatenate([second, third], axis=1)], ["y", "z"])
    both, third = reduce_direct([jnp.stack([first, pair[:4]], axis=1), pair[4:]], ["x", "y"])
    return jnp.concatenate([both, third[None]])


def turn(values, step):
    pairs = [
        (y * 4 + c * 2 + h, ((y + step) % 4) * 4 + h * 2 + c)
        for y in range(4)
        for c in range(2)
        for h in range(2)
    ]
    return lax.ppermute(values, ("y", "c", "xh"), pairs)


def swap(values):
    return lax.ppermute(values, ("c", "xh"), [(0, 0), (1, 2), (2, 1), (3, 3)])


def trade(values):
    return lax.ppermute(values, "c", [(0, 1), (1, 0)])


def total_of(part):
    part = part.astype(BF16)
    return part.astype(F32) + trade(part).astype(F32)


def fetch_weights(qkv_w, out_w, up_w, down_w):
    packed = jnp.concatenate(
        [
            qkv_w.reshape(LAYERS, ROWS, 3 * HALF),
            jnp.swapaxes(out_w, 1, 2),
            up_w,
            jnp.swapaxes(down_w, 1, 2),
        ],
        axis=2,
    ).reshape(LAYERS, ROWS, 4, COLS)
    packed = jnp.moveaxis(packed, 2, 0)
    slab = jnp.zeros((4, LAYERS, ROWS, COLS), BF16)
    y = lax.axis_index("y")
    for step in range(4):
        slab = put(slab, turn(take(packed, (y + step) % 4), step), (y - step) % 4)
    slab = jnp.moveaxis(slab, 0, 1).reshape(LAYERS, 3, 16, COLS)
    parts = gather_chips(jnp.moveaxis(slab, 1, 0))

    def rows(number, group, low, high):
        return jnp.stack(
            [part[:, :, group, number, :, low:high] for part in parts], axis=2
        ).reshape(WIDTH, high - low)

    layers = []
    for number in range(LAYERS):
        layers.append(
            (
                rows(number, 0, 0, COLS),
                rows(number, 1, 0, HALF),
                jnp.concatenate(
                    [rows(number, 1, HALF, COLS), rows(number, 2, 0, WIDTH)], axis=1
                ),
                jnp.concatenate(
                    [rows(number, 2, WIDTH, COLS), rows(number, 3, 0, COLS)], axis=1
                ),
            )
        )
    return layers


def return_weights(grads):
    parts = [[], [], []]
    for qkv_g, out_g, up_g, down_g in grads:
        whole = jnp.stack(
            [
                qkv_g,
                jnp.concatenate([out_g, up_g[:, :WIDTH]], axis=1),
                jnp.concatenate([up_g[:, WIDTH:], down_g[:, :HALF]], axis=1),
                down_g[:, HALF:],
            ]
        ).reshape(4, 4, 4, 3, 16, COLS)
        for number in range(3):
            parts[number].append(jnp.moveaxis(whole[:, :, :, number], 0, 2))
    slab = reduce_chips(*(jnp.stack(part, axis=3) for part in parts))
    slab = jnp.moveaxis(slab, 0, 1).reshape(LAYERS, 4, ROWS, COLS)
    slab = jnp.moveaxis(slab, 1, 0)
    out = jnp.zeros((4, LAYERS, ROWS, COLS), BF16)
    y = lax.axis_index("y")
    for step in range(4):
        out = put(out, turn(take(slab, (y + step) % 4), step), (y - step) % 4)
    out = jnp.moveaxis(out, 0, 2).reshape(LAYERS, ROWS, 4 * COLS).astype(F32)
    return (
        out[:, :, :COLS].reshape(LAYERS, ROWS, 3, HALF),
        jnp.swapaxes(out[:, :, COLS : COLS + HALF], 1, 2),
        out[:, :, COLS + HALF : COLS + HALF + UNITS],
        jnp.swapaxes(out[:, :, COLS + HALF + UNITS :], 1, 2),
    )


def small_maps():
    core = lax.axis_index("c")

    def grid(columns):
        return (
            lax.broadcasted_iota(jnp.int32, (128, columns), 0),
            lax.broadcasted_iota(jnp.int32, (128, columns), 1),
        )

    device, f = grid(WIDTH)
    owner = (f // 96) * 8 + ((f % 48) // ROWS) * 2 + (f % 96) // 48
    whole = device // 2 == owner
    first = device == owner * 2
    device, f = grid(HALF)
    qv = device == (f // 6) * 2 + core
    device, f = grid(UNITS)
    up = device == (f // 24) * 2 + core

    def pick(rows, columns, period):
        row = lax.broadcasted_iota(jnp.int32, (rows, columns), 0)
        return (row == lax.broadcasted_iota(jnp.int32, (rows, columns), 1) % period).astype(F32)

    return (
        tuple(m.astype(BF16) for m in (first, whole, qv, up)),
        (pick(16, WIDTH, ROWS), pick(16, HALF, 6), pick(32, UNITS, 24)),
    )


def fetch_small(gains, shifts, qv_b, up_b, maps):
    (first, _, qv_map, up_map), (pick, qv_pick, up_pick) = maps

    def widen(values, width):
        return jnp.pad(values, ((0, 0),) * (values.ndim - 1) + ((0, width - values.shape[-1]),))

    packed = jnp.concatenate(
        [
            widen(jnp.concatenate([gains, shifts], axis=1), 16).reshape(-1),
            widen(qv_b.reshape(LAYERS, 2, 6), 16).reshape(-1),
            widen(up_b.reshape(LAYERS, 24), 32).reshape(-1),
            jnp.zeros((64,), BF16),
        ]
    )
    copies = jnp.broadcast_to(packed.reshape(1, 3, 128), (128, 3, 128))
    every = lax.all_to_all(copies, AXES, split_axis=0, concat_axis=0, tiled=True)
    every = every.reshape(128, 384)
    shared = dot_columns(every[:, :192], first).reshape(LAYERS, 6, 16, WIDTH)
    qv = dot_columns(every[:, 192:256], qv_map).reshape(LAYERS, 2, 16, HALF)
    up = dot_columns(every[:, 256:320], up_map).reshape(LAYERS, 1, 32, UNITS)
    return (
        jnp.sum(shared * pick, axis=2),
        jnp.sum(qv * qv_pick, axis=2),
        jnp.sum(up * up_pick, axis=2),
    )


def return_small(shared, qv, up, maps):
    (_, whole, qv_map, up_map), (pick, qv_pick, up_pick) = maps

    def spread(rows, table):
        rows = jnp.concatenate(rows)[:, None, :] * table
        return rows.reshape(-1, rows.shape[-1]).astype(BF16)

    chunks = jnp.concatenate(
        [
            0.5 * dot_rows(whole, spread(shared, pick)),
            dot_rows(qv_map, spread(qv, qv_pick)),
            dot_rows(up_map, spread(up, up_pick)),
            jnp.zeros((128, 64), F32),
        ],
        axis=1,
    ).reshape(128, 3, 128)
    mine = lax.all_to_all(chunks, AXES, split_axis=0, concat_axis=0, tiled=True)
    mine = jnp.sum(mine, axis=0).reshape(384)
    shared = mine[:192].reshape(LAYERS, 6, 16)[:, :, :ROWS]
    return (
        shared[:, :2],
        shared[:, 2:],
        mine[192:256].reshape(LAYERS, 2, 1, 16)[:, :, :, :6],
        mine[256:320].reshape(LAYERS, 1, 32)[:, :, :24],
    )


def norm_parts(values):
    average = jnp.mean(values, axis=-1, keepdims=True)
    centred = values - average
    spread = jnp.mean(centred * centred, axis=-1, keepdims=True)
    inverse = lax.rsqrt(spread + epsilon)
    return centred * inverse, inverse


def norm_back(values, gain_row, upstream):
    normal, inverse = norm_parts(values)
    gain_grad = jnp.sum(upstream * normal, axis=0, keepdims=True)
    shift_grad = jnp.sum(upstream, axis=0, keepdims=True)
    scaled = upstream * gain_row
    back = inverse * (
        scaled
        - jnp.mean(scaled, axis=-1, keepdims=True)
        - normal * jnp.mean(scaled * normal, axis=-1, keepdims=True)
    )
    return back, gain_grad, shift_grad


def dot(a, b):
    return jnp.dot(a, b, preferred_element_type=F32)


def dot_rows(a, b):
    return lax.dot_general(a, b, (((1,), (1,)), ((), ())), preferred_element_type=F32)


def dot_columns(a, b):
    return lax.dot_general(a, b, (((0,), (0,)), ((), ())), preferred_element_type=F32)


def gelu_parts(up_act):
    cumulative = 0.5 * (1.0 + lax.erf(up_act * (1.0 / math.sqrt(2.0))))
    density = jnp.exp(-0.5 * up_act * up_act) * (1.0 / math.sqrt(2.0 * math.pi))
    return cumulative, density


def heads_of(values):
    return jnp.moveaxis(values.reshape(values.shape[0], -1, HEAD), 1, 0)


def columns_of(values):
    return jnp.moveaxis(values, 0, 1).reshape(values.shape[1], -1)


def layer_ahead(stream, weights, shared, qv_b, up_b):
    qkv_w, out_w, up_w, down_w = weights
    scaling = 1.0 / math.sqrt(HEAD)
    first = (norm_parts(stream)[0] * shared[0:1] + shared[2:3]).astype(BF16)
    bias = jnp.concatenate([qv_b[:1], jnp.zeros((1, HALF), F32), qv_b[1:]], axis=1)
    qkv = (dot(first, qkv_w) + bias).astype(BF16)
    heads = heads_of(qkv)
    count = HALF // HEAD
    queries, keys, values = heads[:count], heads[count : 2 * count], heads[2 * count :]
    scores = jnp.einsum("hqd,hkd->hqk", queries, keys, preferred_element_type=F32) * scaling
    top = jnp.max(scores, axis=-1, keepdims=True)
    log_total = top + jnp.log(jnp.sum(jnp.exp(scores - top), axis=-1, keepdims=True))
    probs = jnp.exp(scores - log_total).astype(BF16)
    attended = columns_of(
        jnp.einsum("hqk,hkd->hqd", probs, values, preferred_element_type=F32).astype(BF16)
    )
    middle = stream + total_of(dot_rows(attended, out_w)) + shared[3:4]
    second = (norm_parts(middle)[0] * shared[1:2] + shared[4:5]).astype(BF16)
    up_act = dot(second, up_w) + up_b
    hidden = (up_act * gelu_parts(up_act)[0]).astype(BF16)
    block_out = middle + total_of(dot_rows(hidden, down_w)) + shared[5:6]
    return block_out, (stream, first, queries, keys, values, log_total, attended, middle, second, up_act, hidden)


def layer_back(upstream, stored, weights, shared):
    qkv_w, out_w, up_w, down_w = weights
    stream, first, queries, keys, values, log_total, attended, middle, second, up_act, hidden = stored
    scaling = 1.0 / math.sqrt(HEAD)
    down_in = upstream.astype(BF16)
    down_bias_g = jnp.sum(upstream, axis=0, keepdims=True)
    down_g = dot_columns(down_in, hidden).astype(BF16)
    hidden_g = dot(down_in, down_w)
    cumulative, density = gelu_parts(up_act)
    up_in = (hidden_g * (cumulative + up_act * density)).astype(BF16)
    up_g = dot_columns(second, up_in).astype(BF16)
    up_bias_g = jnp.sum(up_in.astype(F32), axis=0, keepdims=True)
    back, gain_two, shift_two = norm_back(middle, shared[1:2], total_of(dot_rows(up_in, up_w)))
    middle_g = upstream + back
    out_in = middle_g.astype(BF16)
    out_bias_g = jnp.sum(middle_g, axis=0, keepdims=True)
    out_g = dot_columns(out_in, attended).astype(BF16)
    attended_g = heads_of(dot(out_in, out_w).astype(BF16))
    scores = jnp.einsum("hqd,hkd->hqk", queries, keys, preferred_element_type=F32) * scaling
    probs = jnp.exp(scores - log_total)
    prob_g = jnp.einsum("hqd,hkd->hqk", attended_g, values, preferred_element_type=F32)
    value_g = jnp.einsum(
        "hqk,hqd->hkd", probs.astype(BF16), attended_g, preferred_element_type=F32
    ).astype(BF16)
    row_delta = jnp.sum(probs * prob_g, axis=-1, keepdims=True)
    score_g = (probs * (prob_g - row_delta)).astype(BF16)
    query_g = (
        jnp.einsum("hqk,hkd->hqd", score_g, keys, preferred_element_type=F32) * scaling
    ).astype(BF16)
    key_g = (
        jnp.einsum("hqk,hqd->hkd", score_g, queries, preferred_element_type=F32) * scaling
    ).astype(BF16)
    proj_g = columns_of(jnp.concatenate([query_g, key_g, value_g]))
    qkv_g = dot_columns(first, proj_g).astype(BF16)
    proj_sums = jnp.sum(proj_g.astype(F32), axis=0, keepdims=True)
    qv_g = jnp.concatenate([proj_sums[:, :HALF], proj_sums[:, 2 * HALF :]])
    back, gain_one, shift_one = norm_back(stream, shared[0:1], total_of(dot_rows(proj_g, qkv_w)))
    stream_g = middle_g + back
    shared_g = jnp.concatenate([gain_one, gain_two, shift_one, out_bias_g, shift_two, down_bias_g])
    return stream_g, (qkv_g, out_g, up_g, down_g), shared_g, qv_g, up_bias_g


def whole_image(rows):
    rows = swap(rows)
    other = trade(rows)
    core = lax.axis_index("c")
    out = put(jnp.zeros((2,) + rows.shape, rows.dtype), rows, core)
    return put(out, other, 1 - core).reshape(-1, WIDTH)


def image_half(values):
    return swap(take(values.reshape(2, -1, WIDTH), lax.axis_index("c")))[None]


def body(
    tokens,
    cotangent,
    owner,
    norm_gains,
    shifts,
    qkv_weight,
    qv_bias,
    out_weight,
    up_weight,
    up_bias,
    down_weight,
):
    z, xl, y, xh = (lax.axis_index(name) for name in ("z", "xl", "y", "xh"))
    image_no = ((z * 2 + xl) * 4 + y) * 2 + xh
    live_flag = jnp.sum((owner == image_no).astype(F32))
    position = lax.broadcasted_iota(jnp.int32, (WIDTH, WIDTH), 1)
    lead, rest = position // 96, position % 96
    natural = lead * 96 + ((rest % 48) // ROWS) * 24 + (rest // 48) * ROWS + rest % ROWS
    reorder = (lax.broadcasted_iota(jnp.int32, (WIDTH, WIDTH), 0) == natural).astype(BF16)
    maps = small_maps()
    weights = fetch_weights(qkv_weight, out_weight, up_weight, down_weight)
    shared, qv_b, up_b = fetch_small(norm_gains, shifts, qv_bias, up_bias, maps)
    stream = dot(whole_image(tokens[0]), reorder)
    upstream = dot(whole_image(cotangent[0]), reorder) * live_flag
    stored = []
    for number in range(LAYERS):
        stream, kept = layer_ahead(stream, weights[number], shared[number], qv_b[number], up_b[number])
        stored.append(kept)
    mixed_out = image_half(dot_rows((stream * live_flag).astype(BF16), reorder).astype(BF16))
    grads, shared_g, qv_g, up_g = ([None] * LAYERS for _ in range(4))
    for number in reversed(range(LAYERS)):
        upstream, grads[number], shared_g[number], qv_g[number], up_g[number] = layer_back(
            upstream, stored[number], weights[number], shared[number]
        )
    input_grad = image_half(dot_rows(upstream.astype(BF16), reorder).astype(BF16))
    qkv_g, out_g, up_w_g, down_g = return_weights(grads)
    gains_g, shifts_g, qv_bias_g, up_bias_g = return_small(shared_g, qv_g, up_g, maps)
    return (
        mixed_out,
        input_grad,
        gains_g,
        shifts_g,
        qkv_g,
        qv_bias_g,
        out_g,
        up_w_g,
        up_bias_g,
        down_g,
    )


def solution(mesh):
    parts = Mesh(mesh.devices.reshape(SIZES), AXES)
    return jax.shard_map(
        body,
        mesh=parts,
        in_specs=(
            P(REPLICA, "xh", None),
            P(REPLICA, "xh", None),
            P(),
            P(None, None, REPLICA),
            P(None, None, REPLICA),
            P(None, REPLICA, None, "xh"),
            P(None, None, "xh", REPLICA),
            P(None, "xh", REPLICA),
            P(None, REPLICA, "xh"),
            P(None, "xh", REPLICA),
            P(None, "xh", REPLICA),
        ),
        out_specs=(
            P(REPLICA, "xh", None),
            P(REPLICA, "xh", None),
            P(None, None, REPLICA),
            P(None, None, REPLICA),
            P(None, REPLICA, None, "xh"),
            P(None, None, "xh", REPLICA),
            P(None, "xh", REPLICA),
            P(None, REPLICA, "xh"),
            P(None, "xh", REPLICA),
            P(None, "xh", REPLICA),
        ),
        check_vma=False,
    )
```

```python
import math

import jax
import jax.numpy as jnp
from jax import lax
from jax.experimental import pallas as pl
from jax.experimental.pallas import tpu as pltpu
from jax.sharding import Mesh
from jax.sharding import PartitionSpec as P

HEAD = 64
LAYERS = 2
WIDTH = 768
HALF = WIDTH // 2
UNITS = 1536
COLS = 1152
ROWS = 12
F32 = jnp.float32
BF16 = jnp.bfloat16
epsilon = 1e-06

SIZES = (4, 2, 4, 2, 2)
AXES = ("z", "xl", "y", "c", "xh")
REPLICA = ("z", "xl", "y", "c")

RING = {"z": (0, 1, 2, 3), "y": (0, 1, 2, 3), "x": (0, 2, 1, 3)}
NAMES = {"z": "z", "y": "y", "x": ("xl", "xh")}


def hop(values, axis, steps):
    ring = RING[axis]
    return lax.ppermute(
        values, NAMES[axis], [(ring[i], ring[(i + steps) % 4]) for i in range(4)]
    )


def slot_of(axis, offset):
    if axis == "x":
        slot = (lax.axis_index("xl") + 2 * lax.axis_index("xh") + offset) % 4
        return (slot % 2) * 2 + slot // 2
    return (lax.axis_index(axis) + offset) % 4


def put(out, values, place):
    return lax.dynamic_update_slice(out, values[None], (place,) + (0,) * values.ndim)


def take(values, place):
    return lax.dynamic_index_in_dim(values, place, 0, keepdims=False)


def round_hop(values, axis):
    ring = RING[axis]
    pairs = []
    for core in range(2):
        for i in range(4):
            src, dst = ring[i], ring[(i + 1 - 2 * core) % 4]
            if axis == "x":
                spot = lambda at: (at // 2) * 4 + core * 2 + at % 2
            else:
                spot = lambda at: at * 2 + core
            pairs.append((spot(src), spot(dst)))
    names = ("xl", "c", "xh") if axis == "x" else (axis, "c")
    return lax.ppermute(values, names, pairs)


def core_slot(axis, offset):
    return slot_of(axis, offset * (1 - 2 * lax.axis_index("c")))


def together(values):
    return list(lax.optimization_barrier(tuple(values)))


def plus(first, *others):
    total = first.astype(F32)
    for other in others:
        total = total + other.astype(F32)
    return total.astype(BF16)


def assemble(pieces):
    out = jnp.zeros((4,) + pieces[0][1].shape, pieces[0][1].dtype)
    for place, block in pieces:
        out = put(out, block, place)
    return out


def gather_round(arrays, axes):
    pieces = [[(core_slot(axis, 0), v)] for v, axis in zip(arrays, axes)]
    for step in range(1, 4):
        arrays = [round_hop(v, axis) for v, axis in zip(arrays, axes)]
        for k, axis in enumerate(axes):
            pieces[k].append((core_slot(axis, -step), arrays[k]))
    return [assemble(found) for found in pieces]


def reduce_round(arrays, axes):
    moving = [take(v, core_slot(axis, 3)) for v, axis in zip(arrays, axes)]
    for offset in (2, 1, 0):
        moving = [round_hop(m, axis) for m, axis in zip(moving, axes)]
        moving = [
            plus(take(v, core_slot(axis, offset)), m)
            for v, m, axis in zip(arrays, moving, axes)
        ]
    return moving


PHASES = (("x", "y", "z"), ("y", "z", "x"), ("z", "x", "y"))


def gather_chips(slab):
    parts = together([slab[0], slab[1], slab[2]])
    parts = together(gather_round(parts, PHASES[0]))
    parts = together(gather_round(parts, PHASES[1]))
    layers = []
    for number in range(LAYERS):
        found = [part[:, :, number] for part in parts]
        if layers:
            found = together(found + layers[-1])[:3]
        layers.append(together(gather_round(found, PHASES[2])))
    return [
        (jnp.swapaxes(first, 1, 2), jnp.swapaxes(second, 0, 1), jnp.swapaxes(third, 0, 2))
        for first, second, third in layers
    ]


def reduce_layer(first, second, third):
    parts = together(
        [jnp.swapaxes(first, 1, 2), jnp.swapaxes(second, 0, 1), jnp.swapaxes(third, 0, 2)]
    )
    return reduce_round(parts, PHASES[2])


def reduce_chips(layers):
    parts = together([jnp.stack(found, axis=2) for found in zip(*layers)])
    parts = together(reduce_round(parts, PHASES[1]))
    return jnp.stack(reduce_round(parts, PHASES[0]))


def turn(values, step):
    pairs = [
        (y * 4 + c * 2 + h, ((y + step) % 4) * 4 + h * 2 + c)
        for y in range(4)
        for c in range(2)
        for h in range(2)
    ]
    return lax.ppermute(values, ("y", "c", "xh"), pairs)


def swap(values):
    return lax.ppermute(values, ("c", "xh"), [(0, 0), (1, 2), (2, 1), (3, 3)])


def trade(values):
    return lax.ppermute(values, "c", [(0, 1), (1, 0)])


def fetch_weights(qkv_w, out_w, up_w, down_w):
    packed = jnp.concatenate(
        [
            qkv_w.reshape(LAYERS, ROWS, 3 * HALF),
            jnp.swapaxes(out_w, 1, 2),
            up_w,
            jnp.swapaxes(down_w, 1, 2),
        ],
        axis=2,
    ).reshape(LAYERS, ROWS, 4, COLS)
    packed = jnp.moveaxis(packed, 2, 0)
    slab = jnp.zeros((4, LAYERS, ROWS, COLS), BF16)
    y = lax.axis_index("y")
    for step in range(4):
        slab = put(slab, turn(take(packed, (y + step) % 4), step), (y - step) % 4)
    slab = jnp.moveaxis(slab, 0, 1).reshape(LAYERS, 3, 16, COLS)
    layers = []
    for parts in gather_chips(jnp.moveaxis(slab, 1, 0)):

        def rows(group, low, high):
            return jnp.stack(
                [part[:, :, group, :, low:high] for part in parts], axis=2
            ).reshape(WIDTH, high - low)

        layers.append(
            (
                rows(0, 0, COLS),
                rows(1, 0, HALF),
                jnp.concatenate([rows(1, HALF, COLS), rows(2, 0, WIDTH)], axis=1),
                jnp.concatenate([rows(2, WIDTH, COLS), rows(3, 0, COLS)], axis=1),
            )
        )
    return layers


def reduce_grads(qkv_g, out_g, up_g, down_g):
    whole = jnp.stack(
        [
            qkv_g,
            jnp.concatenate([out_g, up_g[:, :WIDTH]], axis=1),
            jnp.concatenate([up_g[:, WIDTH:], down_g[:, :HALF]], axis=1),
            down_g[:, HALF:],
        ]
    ).reshape(4, 4, 4, 3, 16, COLS)
    return reduce_layer(*(jnp.moveaxis(whole[:, :, :, k], 0, 2) for k in range(3)))


def return_weights(layers):
    slab = reduce_chips(layers)
    slab = jnp.moveaxis(slab, 0, 1).reshape(LAYERS, 4, ROWS, COLS)
    slab = jnp.moveaxis(slab, 1, 0)
    out = jnp.zeros((4, LAYERS, ROWS, COLS), BF16)
    y = lax.axis_index("y")
    for step in range(4):
        out = put(out, turn(take(slab, (y + step) % 4), step), (y - step) % 4)
    out = jnp.moveaxis(out, 0, 2).reshape(LAYERS, ROWS, 4 * COLS).astype(F32)
    return (
        out[:, :, :COLS].reshape(LAYERS, ROWS, 3, HALF),
        jnp.swapaxes(out[:, :, COLS : COLS + HALF], 1, 2),
        out[:, :, COLS + HALF : COLS + HALF + UNITS],
        jnp.swapaxes(out[:, :, COLS + HALF + UNITS :], 1, 2),
    )


def small_maps():
    core = lax.axis_index("c")

    def grid(columns):
        return (
            lax.broadcasted_iota(jnp.int32, (128, columns), 0),
            lax.broadcasted_iota(jnp.int32, (128, columns), 1),
        )

    device, f = grid(WIDTH)
    owner = (f // 96) * 8 + ((f % 48) // ROWS) * 2 + (f % 96) // 48
    whole = device // 2 == owner
    first = device == owner * 2
    device, f = grid(HALF)
    qv = device == (f // 6) * 2 + core
    device, f = grid(UNITS)
    up = device == (f // 24) * 2 + core

    def pick(rows, columns, period):
        row = lax.broadcasted_iota(jnp.int32, (rows, columns), 0)
        return (row == lax.broadcasted_iota(jnp.int32, (rows, columns), 1) % period).astype(F32)

    return (
        tuple(m.astype(BF16) for m in (first, whole, qv, up)),
        (pick(16, WIDTH, ROWS), pick(16, HALF, 6), pick(32, UNITS, 24)),
    )


def pack_small(gains, shifts, qv_b, up_b):

    def widen(values, width):
        return jnp.pad(values, ((0, 0),) * (values.ndim - 1) + ((0, width - values.shape[-1]),))

    return jnp.concatenate(
        [
            widen(jnp.concatenate([gains, shifts], axis=1), 16).reshape(-1),
            widen(qv_b.reshape(LAYERS, 2, 6), 16).reshape(-1),
            widen(up_b.reshape(LAYERS, 24), 32).reshape(-1),
            jnp.zeros((64,), BF16),
        ]
    )


def fetch_small(packed, maps):
    (first, _, qv_map, up_map), (pick, qv_pick, up_pick) = maps
    copies = jnp.broadcast_to(packed.reshape(1, 3, 128), (128, 3, 128))
    every = lax.all_to_all(copies, AXES, split_axis=0, concat_axis=0, tiled=True)
    every = every.reshape(128, 384)
    shared = dot_columns(every[:, :192], first).reshape(LAYERS, 6, 16, WIDTH)
    qv = dot_columns(every[:, 192:256], qv_map).reshape(LAYERS, 2, 16, HALF)
    up = dot_columns(every[:, 256:320], up_map).reshape(LAYERS, 1, 32, UNITS)
    return (
        jnp.sum(shared * pick, axis=2),
        jnp.sum(qv * qv_pick, axis=2),
        jnp.sum(up * up_pick, axis=2),
    )


def return_small(shared, qv, up, maps):
    (_, whole, qv_map, up_map), (pick, qv_pick, up_pick) = maps

    def spread(rows, table):
        rows = jnp.concatenate(rows)[:, None, :] * table
        return rows.reshape(-1, rows.shape[-1]).astype(BF16)

    chunks = jnp.concatenate(
        [
            0.5 * dot_rows(whole, spread(shared, pick)),
            dot_rows(qv_map, spread(qv, qv_pick)),
            dot_rows(up_map, spread(up, up_pick)),
            jnp.zeros((128, 64), F32),
        ],
        axis=1,
    ).reshape(128, 3, 128)
    mine = lax.all_to_all(chunks, AXES, split_axis=0, concat_axis=0, tiled=True)
    mine = jnp.sum(mine, axis=0).reshape(384)
    shared = mine[:192].reshape(LAYERS, 6, 16)[:, :, :ROWS]
    return (
        shared[:, :2],
        shared[:, 2:],
        mine[192:256].reshape(LAYERS, 2, 1, 16)[:, :, :, :6],
        mine[256:320].reshape(LAYERS, 1, 32)[:, :, :24],
    )


def norm_parts(values):
    average = jnp.mean(values, axis=-1, keepdims=True)
    centred = values - average
    spread = jnp.mean(centred * centred, axis=-1, keepdims=True)
    inverse = lax.rsqrt(spread + epsilon)
    return centred * inverse, inverse


def dot(a, b):
    return jnp.dot(a, b, preferred_element_type=F32)


def dot_rows(a, b):
    return lax.dot_general(a, b, (((1,), (1,)), ((), ())), preferred_element_type=F32)


def dot_columns(a, b):
    return lax.dot_general(a, b, (((0,), (0,)), ((), ())), preferred_element_type=F32)


def gelu_parts(up_act):
    cumulative = 0.5 * (1.0 + lax.erf(up_act * (1.0 / math.sqrt(2.0))))
    density = jnp.exp(-0.5 * up_act * up_act) * (1.0 / math.sqrt(2.0 * math.pi))
    return cumulative, density


CHUNK = 128
PAIR = 2 * HEAD


def call(kernel, flops, outs, *args):
    return pl.pallas_call(
        kernel,
        cost_estimate=pl.CostEstimate(
            flops=flops * 10**9,
            bytes_accessed=8 * 2**20,
            transcendentals=2**20,
        ),
        out_shape=[jax.ShapeDtypeStruct(shape, kind) for shape, kind in outs],
        compiler_params=pltpu.CompilerParams(vmem_limit_bytes=50 * 2**20),
    )(*args)


def chunks_of(ref):
    return [pl.ds(start, CHUNK) for start in range(0, ref.shape[0], CHUNK)]


def pair_masks():
    lane = lax.broadcasted_iota(jnp.int32, (1, PAIR), 1)
    return (lane < HEAD).astype(BF16), (lane >= HEAD).astype(BF16)


def attention_ahead(x_ref, rows_ref, qkv_w, bias, out_w, first, qkv, attended, part):
    for rows in chunks_of(x_ref):
        normal = norm_parts(x_ref[rows, :])[0]
        first[rows, :] = (normal * rows_ref[0:1, :] + rows_ref[2:3, :]).astype(BF16)
    qkv[...] = (dot(first[...], qkv_w[...]) + bias[...]).astype(BF16)
    masks = pair_masks()
    for low in range(0, HALF, PAIR):
        query = qkv[:, low : low + PAIR]
        key = qkv[:, HALF + low : HALF + low + PAIR]
        value = qkv[:, 2 * HALF + low : 2 * HALF + low + PAIR]
        total = jnp.zeros((query.shape[0], PAIR), F32)
        for mask in masks:
            scores = dot_rows(query * (mask * 0.125).astype(BF16), key)
            weight = jnp.exp(scores - jnp.max(scores, axis=-1, keepdims=True))
            inverse = 1.0 / jnp.sum(weight, axis=-1, keepdims=True)
            total = total + dot((weight * inverse).astype(BF16), value * mask)
        attended[:, low : low + PAIR] = total.astype(BF16)
    part[...] = dot_rows(attended[...], out_w[...]).astype(BF16)


def units_ahead(
    x_ref, own, other, rows_ref, up_w, up_b, down_w, middle, second, hidden, slope, part
):
    for rows in chunks_of(x_ref):
        value = x_ref[rows, :] + (own[rows, :].astype(F32) + other[rows, :].astype(F32))
        value = value + rows_ref[3:4, :]
        middle[rows, :] = value
        normal = norm_parts(value)[0]
        second[rows, :] = (normal * rows_ref[1:2, :] + rows_ref[4:5, :]).astype(BF16)
    for low in range(0, UNITS, HALF):
        cols = slice(low, low + HALF)
        up_act = dot(second[...], up_w[:, cols]) + up_b[:, cols]
        cumulative, density = gelu_parts(up_act)
        hidden[:, cols] = (up_act * cumulative).astype(BF16)
        slope[:, cols] = (cumulative + up_act * density).astype(BF16)
    part[...] = dot_rows(hidden[...], down_w[...]).astype(BF16)


def units_back(g_ref, slope, up_w, down_w, down_in, up_in, part, g_sum, up_sum):
    total = jnp.zeros((1, WIDTH), F32)
    for rows in chunks_of(g_ref):
        value = g_ref[rows, :]
        total = total + jnp.sum(value, axis=0, keepdims=True)
        down_in[rows, :] = value.astype(BF16)
    g_sum[...] = total
    for low in range(0, UNITS, HALF):
        cols = slice(low, low + HALF)
        grad = dot(down_in[...], down_w[:, cols]) * slope[:, cols].astype(F32)
        grad = grad.astype(BF16)
        up_in[:, cols] = grad
        up_sum[:, cols] = jnp.sum(grad.astype(F32), axis=0, keepdims=True)
    part[...] = dot_rows(up_in[...], up_w[...]).astype(BF16)


def norm_chunk(values, gain_row, upstream):
    normal, inverse = norm_parts(values)
    gain_grad = jnp.sum(upstream * normal, axis=0, keepdims=True)
    shift_grad = jnp.sum(upstream, axis=0, keepdims=True)
    scaled = upstream * gain_row
    back = inverse * (
        scaled
        - jnp.mean(scaled, axis=-1, keepdims=True)
        - normal * jnp.mean(scaled * normal, axis=-1, keepdims=True)
    )
    return back, gain_grad, shift_grad


def attention_back(
    g_ref, own, other, middle, rows_ref, qkv_w, out_w, qkv,
    middle_g, out_in, proj_g, part, sums, proj_sum, attended_g,
):
    totals = [jnp.zeros((1, WIDTH), F32)] * 3
    for rows in chunks_of(g_ref):
        grad = own[rows, :].astype(F32) + other[rows, :].astype(F32)
        back, gain, shift = norm_chunk(middle[rows, :], rows_ref[1:2, :], grad)
        value = g_ref[rows, :] + back
        middle_g[rows, :] = value
        out_in[rows, :] = value.astype(BF16)
        bias = jnp.sum(value, axis=0, keepdims=True)
        totals = [t + v for t, v in zip(totals, (gain, shift, bias))]
    for k in range(3):
        sums[k : k + 1, :] = totals[k]
    attended_g[...] = dot(out_in[...], out_w[...]).astype(BF16)
    masks = pair_masks()
    for low in range(0, HALF, PAIR):
        spots = [slice(k * HALF + low, k * HALF + low + PAIR) for k in range(3)]
        query, key, value = (qkv[:, spot] for spot in spots)
        grad = attended_g[:, low : low + PAIR]
        found = [jnp.zeros((query.shape[0], PAIR), F32)] * 3
        for mask in masks:
            scaled = (mask * 0.125).astype(BF16)
            scores = dot_rows(key, query * scaled)
            weight = jnp.exp(scores - jnp.max(scores, axis=0, keepdims=True))
            probs = weight * (1.0 / jnp.sum(weight, axis=0, keepdims=True))
            prob_g = dot_rows(value, grad * mask)
            delta = jnp.sum(probs * prob_g, axis=0, keepdims=True)
            score_g = (probs * (prob_g - delta)).astype(BF16)
            found[0] = found[0] + dot_columns(score_g, key * scaled)
            found[1] = found[1] + dot(score_g, query * scaled)
            found[2] = found[2] + dot(probs.astype(BF16), grad * mask)
        for spot, values in zip(spots, found):
            values = values.astype(BF16)
            proj_g[:, spot] = values
            proj_sum[:, spot] = jnp.sum(values.astype(F32), axis=0, keepdims=True)
    part[...] = dot_rows(proj_g[...], qkv_w[...]).astype(BF16)


def stream_back(middle_g, own, other, x_ref, rows_ref, stream_g, sums):
    totals = [jnp.zeros((1, WIDTH), F32)] * 2
    for rows in chunks_of(x_ref):
        grad = own[rows, :].astype(F32) + other[rows, :].astype(F32)
        back, gain, shift = norm_chunk(x_ref[rows, :], rows_ref[0:1, :], grad)
        stream_g[rows, :] = middle_g[rows, :] + back
        totals = [t + v for t, v in zip(totals, (gain, shift))]
    for k in range(2):
        sums[k : k + 1, :] = totals[k]


def layer_ahead(stream, weights, shared, qv_b, up_b):
    qkv_w, out_w, up_w, down_w = weights
    length = stream.shape[0]
    bias = jnp.concatenate([qv_b[:1], jnp.zeros((1, HALF), F32), qv_b[1:]], axis=1)
    narrow, wide = ((length, WIDTH), BF16), ((length, UNITS), BF16)
    first, qkv, attended, part = call(
        attention_ahead,
        2,
        [narrow, ((length, COLS), BF16), ((length, HALF), BF16), narrow],
        stream, shared, qkv_w, bias, out_w,
    )
    middle, second, hidden, slope, down_part = call(
        units_ahead,
        4,
        [((length, WIDTH), F32), narrow, wide, wide, narrow],
        stream, part, trade(part), shared, up_w, up_b, down_w,
    )
    down_out = down_part.astype(F32) + trade(down_part).astype(F32)
    block_out = middle + down_out + shared[5:6]
    return block_out, (stream, first, qkv, attended, middle, second, hidden, slope)


def layer_back(upstream, stored, weights, shared):
    qkv_w, out_w, up_w, down_w = weights
    stream, first, qkv, attended, middle, second, hidden, slope = stored
    length = stream.shape[0]
    narrow, wide = ((length, WIDTH), BF16), ((length, UNITS), BF16)
    down_in, up_in, part, down_bias_g, up_bias_g = call(
        units_back,
        4,
        [narrow, wide, narrow, ((1, WIDTH), F32), ((1, UNITS), F32)],
        upstream, slope, up_w, down_w,
    )
    other = trade(part)
    down_g = dot_columns(down_in, hidden).astype(BF16)
    up_g = dot_columns(second, up_in).astype(BF16)
    middle_g, out_in, proj_g, part, middle_sums, proj_sums, _ = call(
        attention_back,
        5,
        [
            ((length, WIDTH), F32), narrow, ((length, COLS), BF16), narrow,
            ((3, WIDTH), F32), ((1, COLS), F32), ((length, HALF), BF16),
        ],
        upstream, part, other, middle, shared, qkv_w, out_w, qkv,
    )
    other = trade(part)
    out_g = dot_columns(out_in, attended).astype(BF16)
    qkv_g = dot_columns(first, proj_g).astype(BF16)
    stream_g, stream_sums = call(
        stream_back,
        1,
        [((length, WIDTH), F32), ((2, WIDTH), F32)],
        middle_g, part, other, stream, shared,
    )
    qv_g = jnp.concatenate([proj_sums[:, :HALF], proj_sums[:, 2 * HALF :]])
    shared_g = jnp.concatenate(
        [
            stream_sums[:1], middle_sums[:1], stream_sums[1:],
            middle_sums[2:], middle_sums[1:2], down_bias_g,
        ]
    )
    return stream_g, (qkv_g, out_g, up_g, down_g), shared_g, qv_g, up_bias_g


def whole_image(rows):
    rows = swap(rows)
    other = trade(rows)
    core = lax.axis_index("c")
    out = put(jnp.zeros((2,) + rows.shape, rows.dtype), rows, core)
    return put(out, other, 1 - core).reshape(-1, WIDTH)


def image_half(values):
    return swap(take(values.reshape(2, -1, WIDTH), lax.axis_index("c")))[None]


def body(
    tokens,
    cotangent,
    owner,
    norm_gains,
    shifts,
    qkv_weight,
    qv_bias,
    out_weight,
    up_weight,
    up_bias,
    down_weight,
):
    z, xl, y, xh = (lax.axis_index(name) for name in ("z", "xl", "y", "xh"))
    image_no = ((z * 2 + xl) * 4 + y) * 2 + xh
    live_flag = jnp.sum((owner == image_no).astype(F32))
    position = lax.broadcasted_iota(jnp.int32, (WIDTH, WIDTH), 1)
    lead, rest = position // 96, position % 96
    natural = lead * 96 + ((rest % 48) // ROWS) * 24 + (rest // 48) * ROWS + rest % ROWS
    reorder = (lax.broadcasted_iota(jnp.int32, (WIDTH, WIDTH), 0) == natural).astype(BF16)
    maps = small_maps()
    weights = fetch_weights(qkv_weight, out_weight, up_weight, down_weight)
    packed = pack_small(norm_gains, shifts, qv_bias, up_bias)
    shared, qv_b, up_b = fetch_small(packed, maps)
    stream = dot(whole_image(tokens[0]), reorder)
    cotangent, _ = lax.optimization_barrier((cotangent, weights[0][0]))
    upstream = dot(whole_image(cotangent[0]), reorder) * live_flag
    stored = []
    for number in range(LAYERS):
        stream, kept = layer_ahead(stream, weights[number], shared[number], qv_b[number], up_b[number])
        stored.append(kept)
    mixed_out = image_half(dot_rows((stream * live_flag).astype(BF16), reorder).astype(BF16))
    grads, shared_g, qv_g, up_g = ([None] * LAYERS for _ in range(4))
    for number in reversed(range(LAYERS)):
        upstream, pieces, shared_g[number], qv_g[number], up_g[number] = layer_back(
            upstream, stored[number], weights[number], shared[number]
        )
        grads[number] = reduce_grads(*pieces)
        upstream, mixed_out = lax.optimization_barrier((upstream, mixed_out))
    input_grad = image_half(dot_rows(upstream.astype(BF16), reorder).astype(BF16))
    qkv_g, out_g, up_w_g, down_g = return_weights(grads)
    gains_g, shifts_g, qv_bias_g, up_bias_g = return_small(shared_g, qv_g, up_g, maps)
    return (
        mixed_out,
        input_grad,
        gains_g,
        shifts_g,
        qkv_g,
        qv_bias_g,
        out_g,
        up_w_g,
        up_bias_g,
        down_g,
    )


def solution(mesh):
    parts = Mesh(mesh.devices.reshape(SIZES), AXES)
    return jax.shard_map(
        body,
        mesh=parts,
        in_specs=(
            P(REPLICA, "xh", None),
            P(REPLICA, "xh", None),
            P(),
            P(None, None, REPLICA),
            P(None, None, REPLICA),
            P(None, REPLICA, None, "xh"),
            P(None, None, "xh", REPLICA),
            P(None, "xh", REPLICA),
            P(None, REPLICA, "xh"),
            P(None, "xh", REPLICA),
            P(None, "xh", REPLICA),
        ),
        out_specs=(
            P(REPLICA, "xh", None),
            P(REPLICA, "xh", None),
            P(None, None, REPLICA),
            P(None, None, REPLICA),
            P(None, REPLICA, None, "xh"),
            P(None, None, "xh", REPLICA),
            P(None, "xh", REPLICA),
            P(None, REPLICA, "xh"),
            P(None, "xh", REPLICA),
            P(None, "xh", REPLICA),
        ),
        check_vma=False,
    )
```

```python
import math

import jax
import jax.numpy as jnp
from jax import lax
from jax.experimental import pallas as pl
from jax.experimental.pallas import tpu as pltpu
from jax.sharding import Mesh
from jax.sharding import PartitionSpec as P

HEAD = 64
LAYERS = 2
WIDTH = 768
HALF = WIDTH // 2
UNITS = 1536
COLS = 1152
ROWS = 12
F32 = jnp.float32
BF16 = jnp.bfloat16
epsilon = 1e-06

SIZES = (4, 2, 4, 2, 2)
AXES = ("z", "xl", "y", "c", "xh")
REPLICA = ("z", "xl", "y", "c")

RING = {"z": (0, 1, 2, 3), "y": (0, 1, 2, 3), "x": (0, 2, 1, 3)}
NAMES = {"z": "z", "y": "y", "x": ("xl", "xh")}


def hop(values, axis, steps):
    ring = RING[axis]
    return lax.ppermute(
        values, NAMES[axis], [(ring[i], ring[(i + steps) % 4]) for i in range(4)]
    )


def slot_of(axis, offset):
    if axis == "x":
        slot = (lax.axis_index("xl") + 2 * lax.axis_index("xh") + offset) % 4
        return (slot % 2) * 2 + slot // 2
    return (lax.axis_index(axis) + offset) % 4


def put(out, values, place):
    return lax.dynamic_update_slice(out, values[None], (place,) + (0,) * values.ndim)


def take(values, place):
    return lax.dynamic_index_in_dim(values, place, 0, keepdims=False)


def round_hop(values, axis):
    ring = RING[axis]
    pairs = []
    for core in range(2):
        for i in range(4):
            src, dst = ring[i], ring[(i + 1 - 2 * core) % 4]
            if axis == "x":
                spot = lambda at: (at // 2) * 4 + core * 2 + at % 2
            else:
                spot = lambda at: at * 2 + core
            pairs.append((spot(src), spot(dst)))
    names = ("xl", "c", "xh") if axis == "x" else (axis, "c")
    return lax.ppermute(values, names, pairs)


def core_slot(axis, offset):
    return slot_of(axis, offset * (1 - 2 * lax.axis_index("c")))


def together(values):
    return list(lax.optimization_barrier(tuple(values)))


def plus(first, *others):
    total = first.astype(F32)
    for other in others:
        total = total + other.astype(F32)
    return total.astype(BF16)


def assemble(pieces):
    out = jnp.zeros((4,) + pieces[0][1].shape, pieces[0][1].dtype)
    for place, block in pieces:
        out = put(out, block, place)
    return out


def blocks_round(arrays, axes):
    found = [[v] for v in arrays]
    for _ in range(1, 4):
        arrays = [round_hop(v, axis) for v, axis in zip(arrays, axes)]
        for blocks, v in zip(found, arrays):
            blocks.append(v)
    return found


def slots_round(axis):
    return [core_slot(axis, -step) for step in range(4)]


def gather_round(arrays, axes):
    return [
        assemble(list(zip(slots_round(axis), blocks)))
        for axis, blocks in zip(axes, blocks_round(arrays, axes))
    ]


def reduce_round(arrays, axes):
    moving = [take(v, core_slot(axis, 3)) for v, axis in zip(arrays, axes)]
    for offset in (2, 1, 0):
        moving = [round_hop(m, axis) for m, axis in zip(moving, axes)]
        moving = [
            plus(take(v, core_slot(axis, offset)), m)
            for v, m, axis in zip(arrays, moving, axes)
        ]
    return moving


PHASES = (("x", "y", "z"), ("y", "z", "x"), ("z", "x", "y"))


SEGMENTS = (
    ((0, 0, 0, COLS),),
    ((1, 0, 0, HALF), (2, 0, HALF, WIDTH)),
    ((2, WIDTH, 0, WIDTH), (3, 0, WIDTH, HALF)),
    ((3, HALF, 0, COLS),),
)
SHAPES = (COLS, HALF, UNITS, UNITS)


def lay_out(slots, *refs):
    blocks, weights, sem = refs[:12], refs[12:16], refs[16]

    def z_last(block, slot, y, weight, low, start, width):
        return [
            (
                block.at[y, :, :, pl.ds(start, width)],
                weight.at[slot, :, 0, :, pl.ds(low, width)],
            )
        ]

    def x_last(block, slot, y, weight, low, start, width):
        return [
            (
                block.at[:, y, :, pl.ds(start, width)],
                weight.at[:, slot, 1, :, pl.ds(low, width)],
            )
        ]

    def y_last(block, slot, y, weight, low, start, width):
        return [
            (
                block.at[x, :, :, pl.ds(start, width)],
                weight.at[:, x, 2, :, pl.ds(low, width)],
            )
            for x in range(4)
        ]

    def each(act):
        for number in range(12):
            slot, block = slots[number], blocks[number]
            for y in range(4):
                pairs = []
                for which, low, start, width in SEGMENTS[y]:
                    kind = (z_last, x_last, y_last)[number // 4]
                    pairs += kind(block, slot, y, weights[which], low, start, width)

                def go(pairs=pairs, number=number, y=y):
                    for index, (src, dst) in enumerate(pairs):
                        act(pltpu.make_async_copy(src, dst, sem.at[number, y, index]))

                if number < 8:
                    go()
                else:
                    pl.when(slot == y)(go)

    each(lambda copy: copy.start())
    each(lambda copy: copy.wait())


def gather_chips(slab):
    parts = together([slab[0], slab[1], slab[2]])
    parts = together(gather_round(parts, PHASES[0]))
    parts = together(gather_round(parts, PHASES[1]))
    slots = jnp.stack(sum([slots_round(axis) for axis in PHASES[2]], [])).astype(jnp.int32)
    layers, last = [], []
    for number in range(LAYERS):
        found = together([part[:, :, number] for part in parts] + last)[:3]
        found = blocks_round(found, PHASES[2])
        last = [blocks[3] for blocks in found]
        weights = pl.pallas_call(
            lay_out,
            in_specs=[pl.BlockSpec(memory_space=pltpu.SMEM)]
            + [pl.BlockSpec(memory_space=pl.ANY)] * 12,
            out_specs=[pl.BlockSpec(memory_space=pl.ANY)] * 4,
            out_shape=[jax.ShapeDtypeStruct((4, 4, 3, 16, n), BF16) for n in SHAPES],
            scratch_shapes=[pltpu.SemaphoreType.DMA((12, 4, 8))],
        )(slots, *sum(found, []))
        layers.append(tuple(w.reshape(WIDTH, w.shape[-1]) for w in weights))
    return layers


def reduce_layer(first, second, third):
    parts = together(
        [jnp.swapaxes(first, 1, 2), jnp.swapaxes(second, 0, 1), jnp.swapaxes(third, 0, 2)]
    )
    return reduce_round(parts, PHASES[2])


def reduce_direct(arrays, axes):
    out = []
    for v, axis in zip(arrays, axes):
        mine, after, across, before = (take(v, slot_of(axis, n)) for n in range(4))
        out.append((mine, hop(after, axis, 1), hop(before, axis, -1), hop(across, axis, 2)))
    return [plus(*found) for found in out]


def reduce_chips(layers):
    parts = together([jnp.stack(found, axis=2) for found in zip(*layers)])
    parts = together(reduce_round(parts, PHASES[1]))
    return jnp.stack(reduce_direct(parts, PHASES[0]))


def turn(values, step):
    pairs = [
        (y * 4 + c * 2 + h, ((y + step) % 4) * 4 + h * 2 + c)
        for y in range(4)
        for c in range(2)
        for h in range(2)
    ]
    return lax.ppermute(values, ("y", "c", "xh"), pairs)


def swap(values):
    return lax.ppermute(values, ("c", "xh"), [(0, 0), (1, 2), (2, 1), (3, 3)])


def trade(values):
    return lax.ppermute(values, "c", [(0, 1), (1, 0)])


def fetch_weights(qkv_w, out_w, up_w, down_w):
    packed = jnp.concatenate(
        [
            qkv_w.reshape(LAYERS, ROWS, 3 * HALF),
            jnp.swapaxes(out_w, 1, 2),
            up_w,
            jnp.swapaxes(down_w, 1, 2),
        ],
        axis=2,
    ).reshape(LAYERS, ROWS, 4, COLS)
    packed = jnp.moveaxis(packed, 2, 0)
    slab = jnp.zeros((4, LAYERS, ROWS, COLS), BF16)
    y = lax.axis_index("y")
    for step in range(4):
        slab = put(slab, turn(take(packed, (y + step) % 4), step), (y - step) % 4)
    slab = jnp.moveaxis(slab, 0, 1).reshape(LAYERS, 3, 16, COLS)
    return gather_chips(jnp.moveaxis(slab, 1, 0))


def reduce_grads(qkv_g, out_g, up_g, down_g):
    whole = jnp.stack(
        [
            qkv_g,
            jnp.concatenate([out_g, up_g[:, :WIDTH]], axis=1),
            jnp.concatenate([up_g[:, WIDTH:], down_g[:, :HALF]], axis=1),
            down_g[:, HALF:],
        ]
    ).reshape(4, 4, 4, 3, 16, COLS)
    return reduce_layer(*(jnp.moveaxis(whole[:, :, :, k], 0, 2) for k in range(3)))


def return_weights(layers):
    slab = reduce_chips(layers)
    slab = jnp.moveaxis(slab, 0, 1).reshape(LAYERS, 4, ROWS, COLS)
    slab = jnp.moveaxis(slab, 1, 0)
    out = jnp.zeros((4, LAYERS, ROWS, COLS), BF16)
    y = lax.axis_index("y")
    for step in range(4):
        out = put(out, turn(take(slab, (y + step) % 4), step), (y - step) % 4)
    out = jnp.moveaxis(out, 0, 2).reshape(LAYERS, ROWS, 4 * COLS).astype(F32)
    return (
        out[:, :, :COLS].reshape(LAYERS, ROWS, 3, HALF),
        jnp.swapaxes(out[:, :, COLS : COLS + HALF], 1, 2),
        out[:, :, COLS + HALF : COLS + HALF + UNITS],
        jnp.swapaxes(out[:, :, COLS + HALF + UNITS :], 1, 2),
    )


def small_maps():
    core = lax.axis_index("c")

    def grid(columns):
        return (
            lax.broadcasted_iota(jnp.int32, (128, columns), 0),
            lax.broadcasted_iota(jnp.int32, (128, columns), 1),
        )

    device, f = grid(WIDTH)
    owner = (f // 96) * 8 + ((f % 48) // ROWS) * 2 + (f % 96) // 48
    whole = device // 2 == owner
    first = device == owner * 2
    device, f = grid(HALF)
    qv = device == (f // 6) * 2 + core
    device, f = grid(UNITS)
    up = device == (f // 24) * 2 + core

    def pick(rows, columns, period):
        row = lax.broadcasted_iota(jnp.int32, (rows, columns), 0)
        return (row == lax.broadcasted_iota(jnp.int32, (rows, columns), 1) % period).astype(F32)

    return (
        tuple(m.astype(BF16) for m in (first, whole, qv, up)),
        (pick(16, WIDTH, ROWS), pick(16, HALF, 6), pick(32, UNITS, 24)),
    )


def pack_small(gains, shifts, qv_b, up_b):

    def widen(values, width):
        return jnp.pad(values, ((0, 0),) * (values.ndim - 1) + ((0, width - values.shape[-1]),))

    return jnp.concatenate(
        [
            widen(jnp.concatenate([gains, shifts], axis=1), 16).reshape(-1),
            widen(qv_b.reshape(LAYERS, 2, 6), 16).reshape(-1),
            widen(up_b.reshape(LAYERS, 24), 32).reshape(-1),
            jnp.zeros((64,), BF16),
        ]
    )


def fetch_small(packed, maps):
    (first, _, qv_map, up_map), (pick, qv_pick, up_pick) = maps
    copies = jnp.broadcast_to(packed.reshape(1, 3, 128), (128, 3, 128))
    every = lax.all_to_all(copies, AXES, split_axis=0, concat_axis=0, tiled=True)
    every = every.reshape(128, 384)
    shared = dot_columns(every[:, :192], first).reshape(LAYERS, 6, 16, WIDTH)
    qv = dot_columns(every[:, 192:256], qv_map).reshape(LAYERS, 2, 16, HALF)
    up = dot_columns(every[:, 256:320], up_map).reshape(LAYERS, 1, 32, UNITS)
    return (
        jnp.sum(shared * pick, axis=2),
        jnp.sum(qv * qv_pick, axis=2),
        jnp.sum(up * up_pick, axis=2),
    )


def return_small(shared, qv, up, maps):
    (_, whole, qv_map, up_map), (pick, qv_pick, up_pick) = maps

    def spread(rows, table):
        rows = jnp.concatenate(rows)[:, None, :] * table
        return rows.reshape(-1, rows.shape[-1]).astype(BF16)

    chunks = jnp.concatenate(
        [
            0.5 * dot_rows(whole, spread(shared, pick)),
            dot_rows(qv_map, spread(qv, qv_pick)),
            dot_rows(up_map, spread(up, up_pick)),
            jnp.zeros((128, 64), F32),
        ],
        axis=1,
    ).reshape(128, 3, 128)
    mine = lax.all_to_all(chunks, AXES, split_axis=0, concat_axis=0, tiled=True)
    mine = jnp.sum(mine, axis=0).reshape(384)
    shared = mine[:192].reshape(LAYERS, 6, 16)[:, :, :ROWS]
    return (
        shared[:, :2],
        shared[:, 2:],
        mine[192:256].reshape(LAYERS, 2, 1, 16)[:, :, :, :6],
        mine[256:320].reshape(LAYERS, 1, 32)[:, :, :24],
    )


def norm_parts(values):
    average = jnp.mean(values, axis=-1, keepdims=True)
    centred = values - average
    spread = jnp.mean(centred * centred, axis=-1, keepdims=True)
    inverse = lax.rsqrt(spread + epsilon)
    return centred * inverse, inverse


def dot(a, b):
    return jnp.dot(a, b, preferred_element_type=F32)


def dot_rows(a, b):
    return lax.dot_general(a, b, (((1,), (1,)), ((), ())), preferred_element_type=F32)


def dot_columns(a, b):
    return lax.dot_general(a, b, (((0,), (0,)), ((), ())), preferred_element_type=F32)


def gelu_parts(up_act):
    cumulative = 0.5 * (1.0 + lax.erf(up_act * (1.0 / math.sqrt(2.0))))
    density = jnp.exp(-0.5 * up_act * up_act) * (1.0 / math.sqrt(2.0 * math.pi))
    return cumulative, density


CHUNK = 128
PAIR = 2 * HEAD


def call(kernel, flops, outs, *args):
    return pl.pallas_call(
        kernel,
        cost_estimate=pl.CostEstimate(
            flops=flops * 10**9,
            bytes_accessed=8 * 2**20,
            transcendentals=2**20,
        ),
        out_shape=[jax.ShapeDtypeStruct(shape, kind) for shape, kind in outs],
        compiler_params=pltpu.CompilerParams(vmem_limit_bytes=50 * 2**20),
    )(*args)


def chunks_of(ref):
    return [pl.ds(start, CHUNK) for start in range(0, ref.shape[0], CHUNK)]


def pair_masks():
    lane = lax.broadcasted_iota(jnp.int32, (1, PAIR), 1)
    return (lane < HEAD).astype(BF16), (lane >= HEAD).astype(BF16)


def attention_ahead(x_ref, rows_ref, qkv_w, bias, out_w, first, qkv, attended, part):
    for rows in chunks_of(x_ref):
        normal = norm_parts(x_ref[rows, :])[0]
        first[rows, :] = (normal * rows_ref[0:1, :] + rows_ref[2:3, :]).astype(BF16)
    qkv[...] = (dot(first[...], qkv_w[...]) + bias[...]).astype(BF16)
    masks = pair_masks()
    for low in range(0, HALF, PAIR):
        query = qkv[:, low : low + PAIR]
        key = qkv[:, HALF + low : HALF + low + PAIR]
        value = qkv[:, 2 * HALF + low : 2 * HALF + low + PAIR]
        total = jnp.zeros((query.shape[0], PAIR), F32)
        for mask in masks:
            scores = dot_rows(query * (mask * 0.125).astype(BF16), key)
            weight = jnp.exp(scores - jnp.max(scores, axis=-1, keepdims=True))
            inverse = 1.0 / jnp.sum(weight, axis=-1, keepdims=True)
            total = total + dot((weight * inverse).astype(BF16), value * mask)
        attended[:, low : low + PAIR] = total.astype(BF16)
    part[...] = dot_rows(attended[...], out_w[...]).astype(BF16)


def units_ahead(
    x_ref, own, other, rows_ref, up_w, up_b, down_w, middle, second, hidden, slope, part
):
    for rows in chunks_of(x_ref):
        value = x_ref[rows, :] + (own[rows, :].astype(F32) + other[rows, :].astype(F32))
        value = value + rows_ref[3:4, :]
        middle[rows, :] = value
        normal = norm_parts(value)[0]
        second[rows, :] = (normal * rows_ref[1:2, :] + rows_ref[4:5, :]).astype(BF16)
    for low in range(0, UNITS, HALF):
        cols = slice(low, low + HALF)
        up_act = dot(second[...], up_w[:, cols]) + up_b[:, cols]
        cumulative, density = gelu_parts(up_act)
        hidden[:, cols] = (up_act * cumulative).astype(BF16)
        slope[:, cols] = (cumulative + up_act * density).astype(BF16)
    part[...] = dot_rows(hidden[...], down_w[...]).astype(BF16)


def units_back(g_ref, slope, up_w, down_w, down_in, up_in, part, g_sum, up_sum):
    total = jnp.zeros((1, WIDTH), F32)
    for rows in chunks_of(g_ref):
        value = g_ref[rows, :]
        total = total + jnp.sum(value, axis=0, keepdims=True)
        down_in[rows, :] = value.astype(BF16)
    g_sum[...] = total
    for low in range(0, UNITS, HALF):
        cols = slice(low, low + HALF)
        grad = dot(down_in[...], down_w[:, cols]) * slope[:, cols].astype(F32)
        grad = grad.astype(BF16)
        up_in[:, cols] = grad
        up_sum[:, cols] = jnp.sum(grad.astype(F32), axis=0, keepdims=True)
    part[...] = dot_rows(up_in[...], up_w[...]).astype(BF16)


def norm_chunk(values, gain_row, upstream):
    normal, inverse = norm_parts(values)
    gain_grad = jnp.sum(upstream * normal, axis=0, keepdims=True)
    shift_grad = jnp.sum(upstream, axis=0, keepdims=True)
    scaled = upstream * gain_row
    back = inverse * (
        scaled
        - jnp.mean(scaled, axis=-1, keepdims=True)
        - normal * jnp.mean(scaled * normal, axis=-1, keepdims=True)
    )
    return back, gain_grad, shift_grad


def attention_back(
    g_ref, own, other, middle, rows_ref, qkv_w, out_w, qkv,
    middle_g, out_in, proj_g, part, sums, proj_sum, attended_g,
):
    totals = [jnp.zeros((1, WIDTH), F32)] * 3
    for rows in chunks_of(g_ref):
        grad = own[rows, :].astype(F32) + other[rows, :].astype(F32)
        back, gain, shift = norm_chunk(middle[rows, :], rows_ref[1:2, :], grad)
        value = g_ref[rows, :] + back
        middle_g[rows, :] = value
        out_in[rows, :] = value.astype(BF16)
        bias = jnp.sum(value, axis=0, keepdims=True)
        totals = [t + v for t, v in zip(totals, (gain, shift, bias))]
    for k in range(3):
        sums[k : k + 1, :] = totals[k]
    attended_g[...] = dot(out_in[...], out_w[...]).astype(BF16)
    masks = pair_masks()
    for low in range(0, HALF, PAIR):
        spots = [slice(k * HALF + low, k * HALF + low + PAIR) for k in range(3)]
        query, key, value = (qkv[:, spot] for spot in spots)
        grad = attended_g[:, low : low + PAIR]
        found = [jnp.zeros((query.shape[0], PAIR), F32)] * 3
        for mask in masks:
            scaled = (mask * 0.125).astype(BF16)
            scores = dot_rows(key, query * scaled)
            weight = jnp.exp(scores - jnp.max(scores, axis=0, keepdims=True))
            probs = weight * (1.0 / jnp.sum(weight, axis=0, keepdims=True))
            prob_g = dot_rows(value, grad * mask)
            delta = jnp.sum(probs * prob_g, axis=0, keepdims=True)
            score_g = (probs * (prob_g - delta)).astype(BF16)
            found[0] = found[0] + dot_columns(score_g, key * scaled)
            found[1] = found[1] + dot(score_g, query * scaled)
            found[2] = found[2] + dot(probs.astype(BF16), grad * mask)
        for spot, values in zip(spots, found):
            values = values.astype(BF16)
            proj_g[:, spot] = values
            proj_sum[:, spot] = jnp.sum(values.astype(F32), axis=0, keepdims=True)
    part[...] = dot_rows(proj_g[...], qkv_w[...]).astype(BF16)


def stream_back(middle_g, own, other, x_ref, rows_ref, stream_g, sums):
    totals = [jnp.zeros((1, WIDTH), F32)] * 2
    for rows in chunks_of(x_ref):
        grad = own[rows, :].astype(F32) + other[rows, :].astype(F32)
        back, gain, shift = norm_chunk(x_ref[rows, :], rows_ref[0:1, :], grad)
        stream_g[rows, :] = middle_g[rows, :] + back
        totals = [t + v for t, v in zip(totals, (gain, shift))]
    for k in range(2):
        sums[k : k + 1, :] = totals[k]


def layer_ahead(stream, weights, shared, qv_b, up_b):
    qkv_w, out_w, up_w, down_w = weights
    length = stream.shape[0]
    bias = jnp.concatenate([qv_b[:1], jnp.zeros((1, HALF), F32), qv_b[1:]], axis=1)
    narrow, wide = ((length, WIDTH), BF16), ((length, UNITS), BF16)
    first, qkv, attended, part = call(
        attention_ahead,
        2,
        [narrow, ((length, COLS), BF16), ((length, HALF), BF16), narrow],
        stream, shared, qkv_w, bias, out_w,
    )
    middle, second, hidden, slope, down_part = call(
        units_ahead,
        4,
        [((length, WIDTH), F32), narrow, wide, wide, narrow],
        stream, part, trade(part), shared, up_w, up_b, down_w,
    )
    down_out = down_part.astype(F32) + trade(down_part).astype(F32)
    block_out = middle + down_out + shared[5:6]
    return block_out, (stream, first, qkv, attended, middle, second, hidden, slope)


def layer_back(upstream, stored, weights, shared):
    qkv_w, out_w, up_w, down_w = weights
    stream, first, qkv, attended, middle, second, hidden, slope = stored
    length = stream.shape[0]
    narrow, wide = ((length, WIDTH), BF16), ((length, UNITS), BF16)
    down_in, up_in, part, down_bias_g, up_bias_g = call(
        units_back,
        4,
        [narrow, wide, narrow, ((1, WIDTH), F32), ((1, UNITS), F32)],
        upstream, slope, up_w, down_w,
    )
    other = trade(part)
    down_g = dot_columns(down_in, hidden).astype(BF16)
    up_g = dot_columns(second, up_in).astype(BF16)
    middle_g, out_in, proj_g, part, middle_sums, proj_sums, _ = call(
        attention_back,
        5,
        [
            ((length, WIDTH), F32), narrow, ((length, COLS), BF16), narrow,
            ((3, WIDTH), F32), ((1, COLS), F32), ((length, HALF), BF16),
        ],
        upstream, part, other, middle, shared, qkv_w, out_w, qkv,
    )
    other = trade(part)
    out_g = dot_columns(out_in, attended).astype(BF16)
    qkv_g = dot_columns(first, proj_g).astype(BF16)
    stream_g, stream_sums = call(
        stream_back,
        1,
        [((length, WIDTH), F32), ((2, WIDTH), F32)],
        middle_g, part, other, stream, shared,
    )
    qv_g = jnp.concatenate([proj_sums[:, :HALF], proj_sums[:, 2 * HALF :]])
    shared_g = jnp.concatenate(
        [
            stream_sums[:1], middle_sums[:1], stream_sums[1:],
            middle_sums[2:], middle_sums[1:2], down_bias_g,
        ]
    )
    return stream_g, (qkv_g, out_g, up_g, down_g), shared_g, qv_g, up_bias_g


def whole_image(rows):
    rows = swap(rows)
    other = trade(rows)
    core = lax.axis_index("c")
    out = put(jnp.zeros((2,) + rows.shape, rows.dtype), rows, core)
    return put(out, other, 1 - core).reshape(-1, WIDTH)


def image_half(values):
    return swap(take(values.reshape(2, -1, WIDTH), lax.axis_index("c")))[None]


def body(
    tokens,
    cotangent,
    owner,
    norm_gains,
    shifts,
    qkv_weight,
    qv_bias,
    out_weight,
    up_weight,
    up_bias,
    down_weight,
):
    z, xl, y, xh = (lax.axis_index(name) for name in ("z", "xl", "y", "xh"))
    image_no = ((z * 2 + xl) * 4 + y) * 2 + xh
    live_flag = jnp.sum((owner == image_no).astype(F32))
    position = lax.broadcasted_iota(jnp.int32, (WIDTH, WIDTH), 1)
    lead, rest = position // 96, position % 96
    natural = lead * 96 + ((rest % 48) // ROWS) * 24 + (rest // 48) * ROWS + rest % ROWS
    reorder = (lax.broadcasted_iota(jnp.int32, (WIDTH, WIDTH), 0) == natural).astype(BF16)
    maps = small_maps()
    weights = fetch_weights(qkv_weight, out_weight, up_weight, down_weight)
    packed = pack_small(norm_gains, shifts, qv_bias, up_bias)
    shared, qv_b, up_b = fetch_small(packed, maps)
    stream = dot(whole_image(tokens[0]), reorder)
    cotangent, _ = lax.optimization_barrier((cotangent, weights[0][0]))
    upstream = dot(whole_image(cotangent[0]), reorder) * live_flag
    stored = []
    for number in range(LAYERS):
        stream, kept = layer_ahead(stream, weights[number], shared[number], qv_b[number], up_b[number])
        stored.append(kept)
    mixed_out = image_half(dot_rows((stream * live_flag).astype(BF16), reorder).astype(BF16))
    grads, shared_g, qv_g, up_g = ([None] * LAYERS for _ in range(4))
    for number in reversed(range(LAYERS)):
        upstream, pieces, shared_g[number], qv_g[number], up_g[number] = layer_back(
            upstream, stored[number], weights[number], shared[number]
        )
        grads[number] = reduce_grads(*pieces)
        upstream, mixed_out = lax.optimization_barrier((upstream, mixed_out))
    input_grad = image_half(dot_rows(upstream.astype(BF16), reorder).astype(BF16))
    qkv_g, out_g, up_w_g, down_g = return_weights(grads)
    gains_g, shifts_g, qv_bias_g, up_bias_g = return_small(shared_g, qv_g, up_g, maps)
    return (
        mixed_out,
        input_grad,
        gains_g,
        shifts_g,
        qkv_g,
        qv_bias_g,
        out_g,
        up_w_g,
        up_bias_g,
        down_g,
    )


def solution(mesh):
    parts = Mesh(mesh.devices.reshape(SIZES), AXES)
    return jax.shard_map(
        body,
        mesh=parts,
        in_specs=(
            P(REPLICA, "xh", None),
            P(REPLICA, "xh", None),
            P(),
            P(None, None, REPLICA),
            P(None, None, REPLICA),
            P(None, REPLICA, None, "xh"),
            P(None, None, "xh", REPLICA),
            P(None, "xh", REPLICA),
            P(None, REPLICA, "xh"),
            P(None, "xh", REPLICA),
            P(None, "xh", REPLICA),
        ),
        out_specs=(
            P(REPLICA, "xh", None),
            P(REPLICA, "xh", None),
            P(None, None, REPLICA),
            P(None, None, REPLICA),
            P(None, REPLICA, None, "xh"),
            P(None, None, "xh", REPLICA),
            P(None, "xh", REPLICA),
            P(None, REPLICA, "xh"),
            P(None, "xh", REPLICA),
            P(None, "xh", REPLICA),
        ),
        check_vma=False,
    )
```

```python
import math

import jax
import jax.numpy as jnp
from jax import lax
from jax.experimental import pallas as pl
from jax.experimental.pallas import tpu as pltpu
from jax.sharding import Mesh
from jax.sharding import PartitionSpec as P

HEAD = 64
LAYERS = 2
WIDTH = 768
HALF = WIDTH // 2
UNITS = 1536
COLS = 1152
ROWS = 12
F32 = jnp.float32
BF16 = jnp.bfloat16
epsilon = 1e-06

SIZES = (4, 2, 4, 2, 2)
AXES = ("z", "xl", "y", "c", "xh")
REPLICA = ("z", "xl", "y", "c")

RING = {"z": (0, 1, 2, 3), "y": (0, 1, 2, 3), "x": (0, 2, 1, 3)}
NAMES = {"z": "z", "y": "y", "x": ("xl", "xh")}


def hop(values, axis, steps):
    ring = RING[axis]
    return lax.ppermute(
        values, NAMES[axis], [(ring[i], ring[(i + steps) % 4]) for i in range(4)]
    )


def slot_of(axis, offset):
    if axis == "x":
        slot = (lax.axis_index("xl") + 2 * lax.axis_index("xh") + offset) % 4
        return (slot % 2) * 2 + slot // 2
    return (lax.axis_index(axis) + offset) % 4


def put(out, values, place):
    return lax.dynamic_update_slice(out, values[None], (place,) + (0,) * values.ndim)


def take(values, place):
    return lax.dynamic_index_in_dim(values, place, 0, keepdims=False)


def round_hop(values, axis):
    ring = RING[axis]
    pairs = []
    for core in range(2):
        for i in range(4):
            src, dst = ring[i], ring[(i + 1 - 2 * core) % 4]
            if axis == "x":
                spot = lambda at: (at // 2) * 4 + core * 2 + at % 2
            else:
                spot = lambda at: at * 2 + core
            pairs.append((spot(src), spot(dst)))
    names = ("xl", "c", "xh") if axis == "x" else (axis, "c")
    return lax.ppermute(values, names, pairs)


def core_slot(axis, offset):
    return slot_of(axis, offset * (1 - 2 * lax.axis_index("c")))


def together(values):
    return list(lax.optimization_barrier(tuple(values)))


def plus(first, *others):
    total = first.astype(F32)
    for other in others:
        total = total + other.astype(F32)
    return total.astype(BF16)


def assemble(pieces):
    out = jnp.zeros((4,) + pieces[0][1].shape, pieces[0][1].dtype)
    for place, block in pieces:
        out = put(out, block, place)
    return out


def blocks_round(arrays, axes):
    found = [[v] for v in arrays]
    for _ in range(1, 4):
        arrays = [round_hop(v, axis) for v, axis in zip(arrays, axes)]
        for blocks, v in zip(found, arrays):
            blocks.append(v)
    return found


def slots_round(axis):
    return [core_slot(axis, -step) for step in range(4)]


def gather_round(arrays, axes):
    return [
        assemble(list(zip(slots_round(axis), blocks)))
        for axis, blocks in zip(axes, blocks_round(arrays, axes))
    ]


def reduce_round(arrays, axes):
    moving = [take(v, core_slot(axis, 3)) for v, axis in zip(arrays, axes)]
    for offset in (2, 1, 0):
        moving = [round_hop(m, axis) for m, axis in zip(moving, axes)]
        moving = [
            plus(take(v, core_slot(axis, offset)), m)
            for v, m, axis in zip(arrays, moving, axes)
        ]
    return moving


PHASES = (("x", "y", "z"), ("y", "z", "x"), ("z", "x", "y"))


SEGMENTS = (
    ((0, 0, 0, COLS),),
    ((1, 0, 0, HALF), (2, 0, HALF, WIDTH)),
    ((2, WIDTH, 0, WIDTH), (3, 0, WIDTH, HALF)),
    ((3, HALF, 0, COLS),),
)
SHAPES = (COLS, HALF, UNITS, UNITS)


def lay_out(slots, *refs):
    blocks, weights = refs[:12], refs[12:]
    for number, block in enumerate(blocks):
        slot = slots[number]
        for y in range(4):

            def go(block=block, slot=slot, y=y, part=number // 4):
                for which, low, start, width in SEGMENTS[y]:
                    weight, to = weights[which], slice(low, low + width)
                    come = slice(start, start + width)
                    if part == 0:
                        weight[slot, :, 0, :, to] = block[y, :, :, come]
                    elif part == 1:
                        weight[:, slot, 1, :, to] = block[:, y, :, come]
                    else:
                        for x in range(4):
                            weight[:, x, 2, :, to] = block[x, :, :, come]

            if number < 8:
                go()
            else:
                pl.when(slot == y)(go)


def gather_chips(slab):
    parts = together([slab[0], slab[1], slab[2]])
    parts = together(gather_round(parts, PHASES[0]))
    parts = together(gather_round(parts, PHASES[1]))
    slots = jnp.stack(sum([slots_round(axis) for axis in PHASES[2]], [])).astype(jnp.int32)
    layers, last = [], []
    for number in range(LAYERS):
        found = together([part[:, :, number] for part in parts] + last)[:3]
        found = blocks_round(found, PHASES[2])
        last = [blocks[3] for blocks in found]
        weights = pl.pallas_call(
            lay_out,
            in_specs=[pl.BlockSpec(memory_space=pltpu.SMEM)]
            + [pl.BlockSpec(memory_space=pltpu.VMEM)] * 12,
            out_specs=[pl.BlockSpec(memory_space=pltpu.VMEM)] * 4,
            out_shape=[jax.ShapeDtypeStruct((4, 4, 3, 16, n), BF16) for n in SHAPES],
            compiler_params=pltpu.CompilerParams(vmem_limit_bytes=40 * 2**20),
        )(slots, *sum(found, []))
        layers.append(tuple(w.reshape(WIDTH, w.shape[-1]) for w in weights))
    return layers


def reduce_layer(first, second, third):
    parts = together(
        [jnp.swapaxes(first, 1, 2), jnp.swapaxes(second, 0, 1), jnp.swapaxes(third, 0, 2)]
    )
    return reduce_round(parts, PHASES[2])


def reduce_direct(arrays, axes):
    out = []
    for v, axis in zip(arrays, axes):
        mine, after, across, before = (take(v, slot_of(axis, n)) for n in range(4))
        out.append((mine, hop(after, axis, 1), hop(before, axis, -1), hop(across, axis, 2)))
    return [plus(*found) for found in out]


def reduce_chips(layers):
    parts = together([jnp.stack(found, axis=2) for found in zip(*layers)])
    parts = together(reduce_round(parts, PHASES[1]))
    return jnp.stack(reduce_direct(parts, PHASES[0]))


def turn(values, step):
    pairs = [
        (y * 4 + c * 2 + h, ((y + step) % 4) * 4 + h * 2 + c)
        for y in range(4)
        for c in range(2)
        for h in range(2)
    ]
    return lax.ppermute(values, ("y", "c", "xh"), pairs)


def swap(values):
    return lax.ppermute(values, ("c", "xh"), [(0, 0), (1, 2), (2, 1), (3, 3)])


def trade(values):
    return lax.ppermute(values, "c", [(0, 1), (1, 0)])


SMALL = 384
PLANE = ("z", "xl", "xh")


def with_row(values, small):
    row = jnp.zeros((4, LAYERS, 1, COLS), BF16)
    row = lax.dynamic_update_slice(row, small.astype(BF16)[:, None, None, :], (0, 0, 0, 0))
    return jnp.concatenate([values, row], axis=2)


def turn_all(values):
    out = jnp.zeros_like(values)
    y = lax.axis_index("y")
    for step in range(4):
        out = put(out, turn(take(values, (y + step) % 4), step), (y - step) % 4)
    return out


def fetch_weights(qkv_w, out_w, up_w, down_w, small):
    packed = jnp.concatenate(
        [
            qkv_w.reshape(LAYERS, ROWS, 3 * HALF),
            jnp.swapaxes(out_w, 1, 2),
            up_w,
            jnp.swapaxes(down_w, 1, 2),
        ],
        axis=2,
    ).reshape(LAYERS, ROWS, 4, COLS)
    packed = with_row(jnp.moveaxis(packed, 2, 0), jnp.broadcast_to(small, (4, SMALL)))
    slab = turn_all(packed)
    small = slab[:, 0, ROWS, :SMALL]
    slab = jnp.moveaxis(slab[:, :, :ROWS], 0, 1).reshape(LAYERS, 3, 16, COLS)
    return gather_chips(jnp.moveaxis(slab, 1, 0)), small


def reduce_grads(qkv_g, out_g, up_g, down_g):
    whole = jnp.stack(
        [
            qkv_g,
            jnp.concatenate([out_g, up_g[:, :WIDTH]], axis=1),
            jnp.concatenate([up_g[:, WIDTH:], down_g[:, :HALF]], axis=1),
            down_g[:, HALF:],
        ]
    ).reshape(4, 4, 4, 3, 16, COLS)
    return reduce_layer(*(jnp.moveaxis(whole[:, :, :, k], 0, 2) for k in range(3)))


def return_weights(layers, small):
    slab = reduce_chips(layers)
    slab = jnp.moveaxis(slab, 0, 1).reshape(LAYERS, 4, ROWS, COLS)
    out = turn_all(with_row(jnp.moveaxis(slab, 1, 0), small))
    small = jnp.sum(out[:, 0, ROWS, :SMALL].astype(F32), axis=0)
    out = jnp.moveaxis(out[:, :, :ROWS], 0, 2).reshape(LAYERS, ROWS, 4 * COLS).astype(F32)
    return (
        out[:, :, :COLS].reshape(LAYERS, ROWS, 3, HALF),
        jnp.swapaxes(out[:, :, COLS : COLS + HALF], 1, 2),
        out[:, :, COLS + HALF : COLS + HALF + UNITS],
        jnp.swapaxes(out[:, :, COLS + HALF + UNITS :], 1, 2),
    ), small


def small_maps():
    def table(columns, shard):
        f = lax.broadcasted_iota(jnp.int32, (64, columns), 1)
        return (lax.broadcasted_iota(jnp.int32, (64, columns), 0) == shard(f)).astype(BF16)

    def ordered(r):
        return (r // 8) * 8 + (r % 2) * 4 + (r % 8) // 2

    def pick(rows, columns, period):
        row = lax.broadcasted_iota(jnp.int32, (rows, columns), 0)
        return (row == lax.broadcasted_iota(jnp.int32, (rows, columns), 1) % period).astype(F32)

    return (
        (
            table(WIDTH, lambda f: f // ROWS),
            table(HALF, lambda f: ordered(f // 6)),
            table(UNITS, lambda f: ordered(f // 24)),
        ),
        (pick(16, WIDTH, ROWS), pick(16, HALF, 6), pick(32, UNITS, 24)),
    )


def pack_small(gains, shifts, qv_b, up_b):

    def widen(values, width):
        return jnp.pad(values, ((0, 0),) * (values.ndim - 1) + ((0, width - values.shape[-1]),))

    return jnp.concatenate(
        [
            widen(jnp.concatenate([gains, shifts], axis=1), 16).reshape(-1),
            widen(qv_b.reshape(LAYERS, 2, 6), 16).reshape(-1),
            widen(up_b.reshape(LAYERS, 24), 32).reshape(-1),
            jnp.zeros((64,), BF16),
        ]
    )


def fetch_small(packed, maps):
    (first, qv_map, up_map), (pick, qv_pick, up_pick) = maps
    copies = jnp.broadcast_to(packed.reshape(1, 12, 128), (16, 12, 128))
    every = lax.all_to_all(copies, PLANE, split_axis=0, concat_axis=0, tiled=True)
    every = every.reshape(64, SMALL)
    shared = dot_columns(every[:, :192], first).reshape(LAYERS, 6, 16, WIDTH)
    qv = dot_columns(every[:, 192:256], qv_map).reshape(LAYERS, 2, 16, HALF)
    up = dot_columns(every[:, 256:320], up_map).reshape(LAYERS, 1, 32, UNITS)
    return (
        jnp.sum(shared * pick, axis=2),
        jnp.sum(qv * qv_pick, axis=2),
        jnp.sum(up * up_pick, axis=2),
    )


def return_small(shared, qv, up, maps):
    (first, qv_map, up_map), (pick, qv_pick, up_pick) = maps

    def spread(rows, table):
        rows = jnp.concatenate(rows)[:, None, :] * table
        return rows.reshape(-1, rows.shape[-1]).astype(BF16)

    chunks = jnp.concatenate(
        [
            dot_rows(first, spread(shared, pick)),
            dot_rows(qv_map, spread(qv, qv_pick)),
            dot_rows(up_map, spread(up, up_pick)),
            jnp.zeros((64, 64), F32),
        ],
        axis=1,
    ).reshape(16, 12, 128)
    mine = lax.all_to_all(chunks, PLANE, split_axis=0, concat_axis=0, tiled=True)
    return jnp.sum(mine, axis=0).reshape(4, SMALL)


def unpack_small(mine):
    shared = mine[:192].reshape(LAYERS, 6, 16)[:, :, :ROWS]
    return (
        shared[:, :2],
        shared[:, 2:],
        mine[192:256].reshape(LAYERS, 2, 1, 16)[:, :, :, :6],
        mine[256:320].reshape(LAYERS, 1, 32)[:, :, :24],
    )


def norm_parts(values):
    average = jnp.mean(values, axis=-1, keepdims=True)
    centred = values - average
    spread = jnp.mean(centred * centred, axis=-1, keepdims=True)
    inverse = lax.rsqrt(spread + epsilon)
    return centred * inverse, inverse


def dot(a, b):
    return jnp.dot(a, b, preferred_element_type=F32)


def dot_rows(a, b):
    return lax.dot_general(a, b, (((1,), (1,)), ((), ())), preferred_element_type=F32)


def dot_columns(a, b):
    return lax.dot_general(a, b, (((0,), (0,)), ((), ())), preferred_element_type=F32)


def gelu_parts(up_act):
    cumulative = 0.5 * (1.0 + lax.erf(up_act * (1.0 / math.sqrt(2.0))))
    density = jnp.exp(-0.5 * up_act * up_act) * (1.0 / math.sqrt(2.0 * math.pi))
    return cumulative, density


CHUNK = 128
PAIR = 2 * HEAD


def call(kernel, flops, outs, *args):
    return pl.pallas_call(
        kernel,
        cost_estimate=pl.CostEstimate(
            flops=flops * 10**9,
            bytes_accessed=8 * 2**20,
            transcendentals=2**20,
        ),
        out_shape=[jax.ShapeDtypeStruct(shape, kind) for shape, kind in outs],
        compiler_params=pltpu.CompilerParams(vmem_limit_bytes=50 * 2**20),
    )(*args)


def chunks_of(ref):
    return [pl.ds(start, CHUNK) for start in range(0, ref.shape[0], CHUNK)]


def pair_masks():
    lane = lax.broadcasted_iota(jnp.int32, (1, PAIR), 1)
    return (lane < HEAD).astype(BF16), (lane >= HEAD).astype(BF16)


def attention_ahead(x_ref, rows_ref, qkv_w, bias, out_w, first, qkv, attended, part):
    for rows in chunks_of(x_ref):
        normal = norm_parts(x_ref[rows, :])[0]
        first[rows, :] = (normal * rows_ref[0:1, :] + rows_ref[2:3, :]).astype(BF16)
    qkv[...] = (dot(first[...], qkv_w[...]) + bias[...]).astype(BF16)
    masks = pair_masks()
    for low in range(0, HALF, PAIR):
        query = qkv[:, low : low + PAIR]
        key = qkv[:, HALF + low : HALF + low + PAIR]
        value = qkv[:, 2 * HALF + low : 2 * HALF + low + PAIR]
        total = jnp.zeros((query.shape[0], PAIR), F32)
        for mask in masks:
            scores = dot_rows(query * (mask * 0.125).astype(BF16), key)
            weight = jnp.exp(scores - jnp.max(scores, axis=-1, keepdims=True))
            inverse = 1.0 / jnp.sum(weight, axis=-1, keepdims=True)
            total = total + dot((weight * inverse).astype(BF16), value * mask)
        attended[:, low : low + PAIR] = total.astype(BF16)
    part[...] = dot_rows(attended[...], out_w[...]).astype(BF16)


def units_ahead(
    x_ref, own, other, rows_ref, up_w, up_b, down_w, middle, second, hidden, slope, part
):
    for rows in chunks_of(x_ref):
        value = x_ref[rows, :] + (own[rows, :].astype(F32) + other[rows, :].astype(F32))
        value = value + rows_ref[3:4, :]
        middle[rows, :] = value
        normal = norm_parts(value)[0]
        second[rows, :] = (normal * rows_ref[1:2, :] + rows_ref[4:5, :]).astype(BF16)
    for low in range(0, UNITS, HALF):
        cols = slice(low, low + HALF)
        up_act = dot(second[...], up_w[:, cols]) + up_b[:, cols]
        cumulative, density = gelu_parts(up_act)
        hidden[:, cols] = (up_act * cumulative).astype(BF16)
        slope[:, cols] = (cumulative + up_act * density).astype(BF16)
    part[...] = dot_rows(hidden[...], down_w[...]).astype(BF16)


def units_back(g_ref, slope, up_w, down_w, down_in, up_in, part, g_sum, up_sum):
    total = jnp.zeros((1, WIDTH), F32)
    for rows in chunks_of(g_ref):
        value = g_ref[rows, :]
        total = total + jnp.sum(value, axis=0, keepdims=True)
        down_in[rows, :] = value.astype(BF16)
    g_sum[...] = total
    for low in range(0, UNITS, HALF):
        cols = slice(low, low + HALF)
        grad = dot(down_in[...], down_w[:, cols]) * slope[:, cols].astype(F32)
        grad = grad.astype(BF16)
        up_in[:, cols] = grad
        up_sum[:, cols] = jnp.sum(grad.astype(F32), axis=0, keepdims=True)
    part[...] = dot_rows(up_in[...], up_w[...]).astype(BF16)


def norm_chunk(values, gain_row, upstream):
    normal, inverse = norm_parts(values)
    gain_grad = jnp.sum(upstream * normal, axis=0, keepdims=True)
    shift_grad = jnp.sum(upstream, axis=0, keepdims=True)
    scaled = upstream * gain_row
    back = inverse * (
        scaled
        - jnp.mean(scaled, axis=-1, keepdims=True)
        - normal * jnp.mean(scaled * normal, axis=-1, keepdims=True)
    )
    return back, gain_grad, shift_grad


def attention_back(
    g_ref, own, other, middle, rows_ref, qkv_w, out_w, qkv,
    middle_g, out_in, proj_g, part, sums, proj_sum, attended_g,
):
    totals = [jnp.zeros((1, WIDTH), F32)] * 3
    for rows in chunks_of(g_ref):
        grad = own[rows, :].astype(F32) + other[rows, :].astype(F32)
        back, gain, shift = norm_chunk(middle[rows, :], rows_ref[1:2, :], grad)
        value = g_ref[rows, :] + back
        middle_g[rows, :] = value
        out_in[rows, :] = value.astype(BF16)
        bias = jnp.sum(value, axis=0, keepdims=True)
        totals = [t + v for t, v in zip(totals, (gain, shift, bias))]
    for k in range(3):
        sums[k : k + 1, :] = totals[k]
    attended_g[...] = dot(out_in[...], out_w[...]).astype(BF16)
    masks = pair_masks()
    for low in range(0, HALF, PAIR):
        spots = [slice(k * HALF + low, k * HALF + low + PAIR) for k in range(3)]
        query, key, value = (qkv[:, spot] for spot in spots)
        grad = attended_g[:, low : low + PAIR]
        found = [jnp.zeros((query.shape[0], PAIR), F32)] * 3
        for mask in masks:
            scaled = (mask * 0.125).astype(BF16)
            scores = dot_rows(key, query * scaled)
            weight = jnp.exp(scores - jnp.max(scores, axis=0, keepdims=True))
            probs = weight * (1.0 / jnp.sum(weight, axis=0, keepdims=True))
            prob_g = dot_rows(value, grad * mask)
            delta = jnp.sum(probs * prob_g, axis=0, keepdims=True)
            score_g = (probs * (prob_g - delta)).astype(BF16)
            found[0] = found[0] + dot_columns(score_g, key * scaled)
            found[1] = found[1] + dot(score_g, query * scaled)
            found[2] = found[2] + dot(probs.astype(BF16), grad * mask)
        for spot, values in zip(spots, found):
            values = values.astype(BF16)
            proj_g[:, spot] = values
            proj_sum[:, spot] = jnp.sum(values.astype(F32), axis=0, keepdims=True)
    part[...] = dot_rows(proj_g[...], qkv_w[...]).astype(BF16)


def stream_back(middle_g, own, other, x_ref, rows_ref, stream_g, sums):
    totals = [jnp.zeros((1, WIDTH), F32)] * 2
    for rows in chunks_of(x_ref):
        grad = own[rows, :].astype(F32) + other[rows, :].astype(F32)
        back, gain, shift = norm_chunk(x_ref[rows, :], rows_ref[0:1, :], grad)
        stream_g[rows, :] = middle_g[rows, :] + back
        totals = [t + v for t, v in zip(totals, (gain, shift))]
    for k in range(2):
        sums[k : k + 1, :] = totals[k]


def layer_ahead(stream, weights, shared, qv_b, up_b):
    qkv_w, out_w, up_w, down_w = weights
    length = stream.shape[0]
    bias = jnp.concatenate([qv_b[:1], jnp.zeros((1, HALF), F32), qv_b[1:]], axis=1)
    narrow, wide = ((length, WIDTH), BF16), ((length, UNITS), BF16)
    first, qkv, attended, part = call(
        attention_ahead,
        2,
        [narrow, ((length, COLS), BF16), ((length, HALF), BF16), narrow],
        stream, shared, qkv_w, bias, out_w,
    )
    middle, second, hidden, slope, down_part = call(
        units_ahead,
        4,
        [((length, WIDTH), F32), narrow, wide, wide, narrow],
        stream, part, trade(part), shared, up_w, up_b, down_w,
    )
    down_out = down_part.astype(F32) + trade(down_part).astype(F32)
    block_out = middle + down_out + shared[5:6]
    return block_out, (stream, first, qkv, attended, middle, second, hidden, slope)


def layer_back(upstream, stored, weights, shared):
    qkv_w, out_w, up_w, down_w = weights
    stream, first, qkv, attended, middle, second, hidden, slope = stored
    length = stream.shape[0]
    narrow, wide = ((length, WIDTH), BF16), ((length, UNITS), BF16)
    down_in, up_in, part, down_bias_g, up_bias_g = call(
        units_back,
        4,
        [narrow, wide, narrow, ((1, WIDTH), F32), ((1, UNITS), F32)],
        upstream, slope, up_w, down_w,
    )
    other = trade(part)
    down_g = dot_columns(down_in, hidden).astype(BF16)
    up_g = dot_columns(second, up_in).astype(BF16)
    middle_g, out_in, proj_g, part, middle_sums, proj_sums, _ = call(
        attention_back,
        5,
        [
            ((length, WIDTH), F32), narrow, ((length, COLS), BF16), narrow,
            ((3, WIDTH), F32), ((1, COLS), F32), ((length, HALF), BF16),
        ],
        upstream, part, other, middle, shared, qkv_w, out_w, qkv,
    )
    other = trade(part)
    out_g = dot_columns(out_in, attended).astype(BF16)
    qkv_g = dot_columns(first, proj_g).astype(BF16)
    stream_g, stream_sums = call(
        stream_back,
        1,
        [((length, WIDTH), F32), ((2, WIDTH), F32)],
        middle_g, part, other, stream, shared,
    )
    qv_g = jnp.concatenate([proj_sums[:, :HALF], proj_sums[:, 2 * HALF :]])
    shared_g = jnp.concatenate(
        [
            stream_sums[:1], middle_sums[:1], stream_sums[1:],
            middle_sums[2:], middle_sums[1:2], down_bias_g,
        ]
    )
    return stream_g, (qkv_g, out_g, up_g, down_g), shared_g, qv_g, up_bias_g


def whole_image(rows):
    rows = swap(rows)
    other = trade(rows)
    core = lax.axis_index("c")
    out = put(jnp.zeros((2,) + rows.shape, rows.dtype), rows, core)
    return put(out, other, 1 - core).reshape(-1, WIDTH)


def image_half(values):
    return swap(take(values.reshape(2, -1, WIDTH), lax.axis_index("c")))[None]


def body(
    tokens,
    cotangent,
    owner,
    norm_gains,
    shifts,
    qkv_weight,
    qv_bias,
    out_weight,
    up_weight,
    up_bias,
    down_weight,
):
    z, xl, y, xh = (lax.axis_index(name) for name in ("z", "xl", "y", "xh"))
    image_no = ((z * 2 + xl) * 4 + y) * 2 + xh
    live_flag = jnp.sum((owner == image_no).astype(F32))
    position = lax.broadcasted_iota(jnp.int32, (WIDTH, WIDTH), 1)
    lead, rest = position // 96, position % 96
    natural = lead * 96 + ((rest % 48) // ROWS) * 24 + (rest // 48) * ROWS + rest % ROWS
    reorder = (lax.broadcasted_iota(jnp.int32, (WIDTH, WIDTH), 0) == natural).astype(BF16)
    maps = small_maps()
    packed = pack_small(norm_gains, shifts, qv_bias, up_bias)
    weights, packed = fetch_weights(qkv_weight, out_weight, up_weight, down_weight, packed)
    shared, qv_b, up_b = fetch_small(packed, maps)
    stream = dot(whole_image(tokens[0]), reorder)
    cotangent, _ = lax.optimization_barrier((cotangent, weights[0][0]))
    upstream = dot(whole_image(cotangent[0]), reorder) * live_flag
    stored = []
    for number in range(LAYERS):
        stream, kept = layer_ahead(stream, weights[number], shared[number], qv_b[number], up_b[number])
        stored.append(kept)
    mixed_out = image_half(dot_rows((stream * live_flag).astype(BF16), reorder).astype(BF16))
    grads, shared_g, qv_g, up_g = ([None] * LAYERS for _ in range(4))
    for number in reversed(range(LAYERS)):
        upstream, pieces, shared_g[number], qv_g[number], up_g[number] = layer_back(
            upstream, stored[number], weights[number], shared[number]
        )
        grads[number] = reduce_grads(*pieces)
        upstream, mixed_out = lax.optimization_barrier((upstream, mixed_out))
    input_grad = image_half(dot_rows(upstream.astype(BF16), reorder).astype(BF16))
    (qkv_g, out_g, up_w_g, down_g), small = return_weights(
        grads, return_small(shared_g, qv_g, up_g, maps)
    )
    gains_g, shifts_g, qv_bias_g, up_bias_g = unpack_small(small)
    return (
        mixed_out,
        input_grad,
        gains_g,
        shifts_g,
        qkv_g,
        qv_bias_g,
        out_g,
        up_w_g,
        up_bias_g,
        down_g,
    )


def solution(mesh):
    parts = Mesh(mesh.devices.reshape(SIZES), AXES)
    return jax.shard_map(
        body,
        mesh=parts,
        in_specs=(
            P(REPLICA, "xh", None),
            P(REPLICA, "xh", None),
            P(),
            P(None, None, REPLICA),
            P(None, None, REPLICA),
            P(None, REPLICA, None, "xh"),
            P(None, None, "xh", REPLICA),
            P(None, "xh", REPLICA),
            P(None, REPLICA, "xh"),
            P(None, "xh", REPLICA),
            P(None, "xh", REPLICA),
        ),
        out_specs=(
            P(REPLICA, "xh", None),
            P(REPLICA, "xh", None),
            P(None, None, REPLICA),
            P(None, None, REPLICA),
            P(None, REPLICA, None, "xh"),
            P(None, None, "xh", REPLICA),
            P(None, "xh", REPLICA),
            P(None, REPLICA, "xh"),
            P(None, "xh", REPLICA),
            P(None, "xh", REPLICA),
        ),
        check_vma=False,
    )
```

```python
import math

import jax
import jax.numpy as jnp
from jax import lax
from jax.experimental import pallas as pl
from jax.experimental.pallas import tpu as pltpu
from jax.sharding import Mesh
from jax.sharding import PartitionSpec as P

HEAD = 64
LAYERS = 2
WIDTH = 768
HALF = WIDTH // 2
UNITS = 1536
COLS = 1152
ROWS = 12
F32 = jnp.float32
BF16 = jnp.bfloat16
epsilon = 1e-06

SIZES = (4, 2, 4, 2, 2)
AXES = ("z", "xl", "y", "c", "xh")
REPLICA = ("z", "xl", "y", "c")

RING = {"z": (0, 1, 2, 3), "y": (0, 1, 2, 3), "x": (0, 2, 1, 3)}
NAMES = {"z": "z", "y": "y", "x": ("xl", "xh")}


def hop(values, axis, steps):
    ring = RING[axis]
    return lax.ppermute(
        values, NAMES[axis], [(ring[i], ring[(i + steps) % 4]) for i in range(4)]
    )


def slot_of(axis, offset):
    if axis == "x":
        slot = (lax.axis_index("xl") + 2 * lax.axis_index("xh") + offset) % 4
        return (slot % 2) * 2 + slot // 2
    return (lax.axis_index(axis) + offset) % 4


def put(out, values, place):
    return lax.dynamic_update_slice(out, values[None], (place,) + (0,) * values.ndim)


def take(values, place):
    return lax.dynamic_index_in_dim(values, place, 0, keepdims=False)


def round_hop(values, axis):
    ring = RING[axis]
    pairs = []
    for core in range(2):
        for i in range(4):
            src, dst = ring[i], ring[(i + 1 - 2 * core) % 4]
            if axis == "x":
                spot = lambda at: (at // 2) * 4 + core * 2 + at % 2
            else:
                spot = lambda at: at * 2 + core
            pairs.append((spot(src), spot(dst)))
    names = ("xl", "c", "xh") if axis == "x" else (axis, "c")
    return lax.ppermute(values, names, pairs)


def core_slot(axis, offset):
    return slot_of(axis, offset * (1 - 2 * lax.axis_index("c")))


def together(values):
    return list(lax.optimization_barrier(tuple(values)))


def plus(first, *others):
    total = first.astype(F32)
    for other in others:
        total = total + other.astype(F32)
    return total.astype(BF16)


def assemble(pieces):
    out = jnp.zeros((4,) + pieces[0][1].shape, pieces[0][1].dtype)
    for place, block in pieces:
        out = put(out, block, place)
    return out


def after(values, *others):
    tied = lax.optimization_barrier((tuple(values), others))
    return list(tied[0])


def blocks_round(arrays, axes):
    found = [[v] for v in arrays]
    for _ in range(1, 4):
        arrays = [round_hop(v, axis) for v, axis in zip(arrays, axes)]
        for blocks, v in zip(found, arrays):
            blocks.append(v)
    return found


def slots_round(axis):
    return [core_slot(axis, -step) for step in range(4)]


def gather_round(arrays, axes):
    return [
        assemble(list(zip(slots_round(axis), blocks)))
        for axis, blocks in zip(axes, blocks_round(arrays, axes))
    ]


def reduce_first(arrays, axes):
    moving = [take(v, core_slot(axis, 3)) for v, axis in zip(arrays, axes)]
    return [round_hop(m, axis) for m, axis in zip(moving, axes)]


def reduce_add(arrays, moving, axes, offset):
    return [
        plus(take(v, core_slot(axis, offset)), m) for v, m, axis in zip(arrays, moving, axes)
    ]


def reduce_next(arrays, moving, axes, offset):
    moving = reduce_add(arrays, moving, axes, offset)
    return [round_hop(m, axis) for m, axis in zip(moving, axes)]


PHASES = (("x", "y", "z"), ("y", "z", "x"), ("z", "x", "y"))


SEGMENTS = (
    ((0, 0, 0, COLS),),
    ((1, 0, 0, HALF), (2, 0, HALF, WIDTH)),
    ((2, WIDTH, 0, WIDTH), (3, 0, WIDTH, HALF)),
    ((3, HALF, 0, COLS),),
)
SHAPES = (COLS, HALF, UNITS, UNITS)


def lay_out(slots, *refs):
    blocks, weights = refs[:12], refs[12:]
    for number, block in enumerate(blocks):
        slot = slots[number]
        for y in range(4):

            def go(block=block, slot=slot, y=y, part=number // 4):
                for which, low, start, width in SEGMENTS[y]:
                    weight, to = weights[which], slice(low, low + width)
                    come = slice(start, start + width)
                    if part == 0:
                        weight[slot, :, 0, :, to] = block[y, :, :, come]
                    elif part == 1:
                        weight[:, slot, 1, :, to] = block[:, y, :, come]
                    else:
                        for x in range(4):
                            weight[:, x, 2, :, to] = block[x, :, :, come]

            if number < 8:
                go()
            else:
                pl.when(slot == y)(go)


def gather_chips(slab, small):
    parts = together([slab[0], slab[1], slab[2]])
    parts = together(gather_round(parts, PHASES[0]))
    parts = together(gather_round(parts, PHASES[1]))
    slots = jnp.stack(sum([slots_round(axis) for axis in PHASES[2]], [])).astype(jnp.int32)
    layers, last = [], []
    for number in range(LAYERS):
        found = together([part[:, :, number] for part in parts] + last)[:3]
        found = blocks_round(found, PHASES[2])
        last = [blocks[3] for blocks in found]
        if number == 0:
            (small,) = after([small], *(blocks[1] for blocks in found))
        weights = pl.pallas_call(
            lay_out,
            in_specs=[pl.BlockSpec(memory_space=pltpu.SMEM)]
            + [pl.BlockSpec(memory_space=pltpu.VMEM)] * 12,
            out_specs=[pl.BlockSpec(memory_space=pltpu.VMEM)] * 4,
            out_shape=[jax.ShapeDtypeStruct((4, 4, 3, 16, n), BF16) for n in SHAPES],
            compiler_params=pltpu.CompilerParams(vmem_limit_bytes=40 * 2**20),
        )(slots, *sum(found, []))
        layers.append(tuple(w.reshape(WIDTH, w.shape[-1]) for w in weights))
    return layers, small


def ring_order(first, second, third):
    return together(
        [jnp.swapaxes(first, 1, 2), jnp.swapaxes(second, 0, 1), jnp.swapaxes(third, 0, 2)]
    )


def reduce_direct(arrays, axes):
    out = []
    for v, axis in zip(arrays, axes):
        mine, after, across, before = (take(v, slot_of(axis, n)) for n in range(4))
        out.append((mine, hop(after, axis, 1), hop(before, axis, -1), hop(across, axis, 2)))
    return [plus(*found) for found in out]


def reduce_chips(layers, stream_g, small):
    axes = PHASES[1]
    parts = together([jnp.stack(found, axis=2) for found in zip(*layers)])
    moving = reduce_first(parts, axes)
    (stream_g,) = after([stream_g], *moving)
    moving = reduce_next(parts, moving, axes, 2)
    small = after(small, *moving)
    moving = reduce_next(parts, moving, axes, 1)
    parts = together(reduce_add(parts, moving, axes, 0))
    return jnp.stack(reduce_direct(parts, PHASES[0])), stream_g, small


def turn(values, step):
    pairs = [
        (y * 4 + c * 2 + h, ((y + step) % 4) * 4 + h * 2 + c)
        for y in range(4)
        for c in range(2)
        for h in range(2)
    ]
    return lax.ppermute(values, ("y", "c", "xh"), pairs)


def swap(values):
    return lax.ppermute(values, ("c", "xh"), [(0, 0), (1, 2), (2, 1), (3, 3)])


def trade(values):
    return lax.ppermute(values, "c", [(0, 1), (1, 0)])


def fetch_weights(qkv_w, out_w, up_w, down_w, small):
    packed = jnp.concatenate(
        [
            qkv_w.reshape(LAYERS, ROWS, 3 * HALF),
            jnp.swapaxes(out_w, 1, 2),
            up_w,
            jnp.swapaxes(down_w, 1, 2),
        ],
        axis=2,
    ).reshape(LAYERS, ROWS, 4, COLS)
    packed = jnp.moveaxis(packed, 2, 0)
    slab = jnp.zeros((4, LAYERS, ROWS, COLS), BF16)
    y = lax.axis_index("y")
    for step in range(4):
        slab = put(slab, turn(take(packed, (y + step) % 4), step), (y - step) % 4)
    slab = jnp.moveaxis(slab, 0, 1).reshape(LAYERS, 3, 16, COLS)
    return gather_chips(jnp.moveaxis(slab, 1, 0), small)


def grad_parts(qkv_g, out_g, up_g, down_g):
    whole = jnp.stack(
        [
            qkv_g,
            jnp.concatenate([out_g, up_g[:, :WIDTH]], axis=1),
            jnp.concatenate([up_g[:, WIDTH:], down_g[:, :HALF]], axis=1),
            down_g[:, HALF:],
        ]
    ).reshape(4, 4, 4, 3, 16, COLS)
    return ring_order(*(jnp.moveaxis(whole[:, :, :, k], 0, 2) for k in range(3)))


def return_weights(layers, stream_g, small):
    slab, stream_g, small = reduce_chips(layers, stream_g, small)
    slab = jnp.moveaxis(slab, 0, 1).reshape(LAYERS, 4, ROWS, COLS)
    slab = jnp.moveaxis(slab, 1, 0)
    out = jnp.zeros((4, LAYERS, ROWS, COLS), BF16)
    y = lax.axis_index("y")
    for step in range(4):
        out = put(out, turn(take(slab, (y + step) % 4), step), (y - step) % 4)
    out = jnp.moveaxis(out, 0, 2).reshape(LAYERS, ROWS, 4 * COLS).astype(F32)
    grads = (
        out[:, :, :COLS].reshape(LAYERS, ROWS, 3, HALF),
        jnp.swapaxes(out[:, :, COLS : COLS + HALF], 1, 2),
        out[:, :, COLS + HALF : COLS + HALF + UNITS],
        jnp.swapaxes(out[:, :, COLS + HALF + UNITS :], 1, 2),
    )
    return grads, stream_g, small


def small_maps():
    core = lax.axis_index("c")

    def grid(columns):
        return (
            lax.broadcasted_iota(jnp.int32, (128, columns), 0),
            lax.broadcasted_iota(jnp.int32, (128, columns), 1),
        )

    device, f = grid(WIDTH)
    owner = (f // 96) * 8 + ((f % 48) // ROWS) * 2 + (f % 96) // 48
    whole = device // 2 == owner
    first = device == owner * 2
    device, f = grid(HALF)
    qv = device == (f // 6) * 2 + core
    device, f = grid(UNITS)
    up = device == (f // 24) * 2 + core

    def pick(rows, columns, period):
        row = lax.broadcasted_iota(jnp.int32, (rows, columns), 0)
        return (row == lax.broadcasted_iota(jnp.int32, (rows, columns), 1) % period).astype(F32)

    return (
        tuple(m.astype(BF16) for m in (first, whole, qv, up)),
        (pick(16, WIDTH, ROWS), pick(16, HALF, 6), pick(32, UNITS, 24)),
    )


def pack_small(gains, shifts, qv_b, up_b):

    def widen(values, width):
        return jnp.pad(values, ((0, 0),) * (values.ndim - 1) + ((0, width - values.shape[-1]),))

    return jnp.concatenate(
        [
            widen(jnp.concatenate([gains, shifts], axis=1), 16).reshape(-1),
            widen(qv_b.reshape(LAYERS, 2, 6), 16).reshape(-1),
            widen(up_b.reshape(LAYERS, 24), 32).reshape(-1),
            jnp.zeros((64,), BF16),
        ]
    )


def fetch_small(packed, maps):
    (first, _, qv_map, up_map), (pick, qv_pick, up_pick) = maps
    copies = jnp.broadcast_to(packed.reshape(1, 3, 128), (128, 3, 128))
    every = lax.all_to_all(copies, AXES, split_axis=0, concat_axis=0, tiled=True)
    every = every.reshape(128, 384)
    shared = dot_columns(every[:, :192], first).reshape(LAYERS, 6, 16, WIDTH)
    qv = dot_columns(every[:, 192:256], qv_map).reshape(LAYERS, 2, 16, HALF)
    up = dot_columns(every[:, 256:320], up_map).reshape(LAYERS, 1, 32, UNITS)
    return (
        jnp.sum(shared * pick, axis=2),
        jnp.sum(qv * qv_pick, axis=2),
        jnp.sum(up * up_pick, axis=2),
    )


def return_small(shared, qv, up, maps):
    (_, whole, qv_map, up_map), (pick, qv_pick, up_pick) = maps

    def spread(rows, table):
        rows = jnp.concatenate(rows)[:, None, :] * table
        return rows.reshape(-1, rows.shape[-1]).astype(BF16)

    chunks = jnp.concatenate(
        [
            0.5 * dot_rows(whole, spread(shared, pick)),
            dot_rows(qv_map, spread(qv, qv_pick)),
            dot_rows(up_map, spread(up, up_pick)),
            jnp.zeros((128, 64), F32),
        ],
        axis=1,
    ).reshape(128, 3, 128)
    mine = lax.all_to_all(chunks, AXES, split_axis=0, concat_axis=0, tiled=True)
    mine = jnp.sum(mine, axis=0).reshape(384)
    shared = mine[:192].reshape(LAYERS, 6, 16)[:, :, :ROWS]
    return (
        shared[:, :2],
        shared[:, 2:],
        mine[192:256].reshape(LAYERS, 2, 1, 16)[:, :, :, :6],
        mine[256:320].reshape(LAYERS, 1, 32)[:, :, :24],
    )


def norm_parts(values):
    average = jnp.mean(values, axis=-1, keepdims=True)
    centred = values - average
    spread = jnp.mean(centred * centred, axis=-1, keepdims=True)
    inverse = lax.rsqrt(spread + epsilon)
    return centred * inverse, inverse


def dot(a, b):
    return jnp.dot(a, b, preferred_element_type=F32)


def dot_rows(a, b):
    return lax.dot_general(a, b, (((1,), (1,)), ((), ())), preferred_element_type=F32)


def dot_columns(a, b):
    return lax.dot_general(a, b, (((0,), (0,)), ((), ())), preferred_element_type=F32)


def gelu_parts(up_act):
    cumulative = 0.5 * (1.0 + lax.erf(up_act * (1.0 / math.sqrt(2.0))))
    density = jnp.exp(-0.5 * up_act * up_act) * (1.0 / math.sqrt(2.0 * math.pi))
    return cumulative, density


CHUNK = 128
PAIR = 2 * HEAD


def call(kernel, flops, outs, *args):
    return pl.pallas_call(
        kernel,
        cost_estimate=pl.CostEstimate(
            flops=flops * 10**9,
            bytes_accessed=8 * 2**20,
            transcendentals=2**20,
        ),
        out_shape=[jax.ShapeDtypeStruct(shape, kind) for shape, kind in outs],
        compiler_params=pltpu.CompilerParams(vmem_limit_bytes=50 * 2**20),
    )(*args)


def chunks_of(ref):
    return [pl.ds(start, CHUNK) for start in range(0, ref.shape[0], CHUNK)]


def pair_masks():
    lane = lax.broadcasted_iota(jnp.int32, (1, PAIR), 1)
    return (lane < HEAD).astype(BF16), (lane >= HEAD).astype(BF16)


def attention_ahead(x_ref, rows_ref, qkv_w, bias, out_w, first, qkv, attended, part):
    for rows in chunks_of(x_ref):
        normal = norm_parts(x_ref[rows, :])[0]
        first[rows, :] = (normal * rows_ref[0:1, :] + rows_ref[2:3, :]).astype(BF16)
    qkv[...] = (dot(first[...], qkv_w[...]) + bias[...]).astype(BF16)
    masks = pair_masks()
    for low in range(0, HALF, PAIR):
        query = qkv[:, low : low + PAIR]
        key = qkv[:, HALF + low : HALF + low + PAIR]
        value = qkv[:, 2 * HALF + low : 2 * HALF + low + PAIR]
        total = jnp.zeros((query.shape[0], PAIR), F32)
        for mask in masks:
            scores = dot_rows(query * (mask * 0.125).astype(BF16), key)
            weight = jnp.exp(scores - jnp.max(scores, axis=-1, keepdims=True))
            inverse = 1.0 / jnp.sum(weight, axis=-1, keepdims=True)
            total = total + dot((weight * inverse).astype(BF16), value * mask)
        attended[:, low : low + PAIR] = total.astype(BF16)
    part[...] = dot_rows(attended[...], out_w[...]).astype(BF16)


def units_ahead(
    x_ref, own, other, rows_ref, up_w, up_b, down_w, middle, second, hidden, slope, part
):
    for rows in chunks_of(x_ref):
        value = x_ref[rows, :] + (own[rows, :].astype(F32) + other[rows, :].astype(F32))
        value = value + rows_ref[3:4, :]
        middle[rows, :] = value
        normal = norm_parts(value)[0]
        second[rows, :] = (normal * rows_ref[1:2, :] + rows_ref[4:5, :]).astype(BF16)
    for low in range(0, UNITS, HALF):
        cols = slice(low, low + HALF)
        up_act = dot(second[...], up_w[:, cols]) + up_b[:, cols]
        cumulative, density = gelu_parts(up_act)
        hidden[:, cols] = (up_act * cumulative).astype(BF16)
        slope[:, cols] = (cumulative + up_act * density).astype(BF16)
    part[...] = dot_rows(hidden[...], down_w[...]).astype(BF16)


def units_back(g_ref, slope, up_w, down_w, down_in, up_in, part, g_sum, up_sum):
    total = jnp.zeros((1, WIDTH), F32)
    for rows in chunks_of(g_ref):
        value = g_ref[rows, :]
        total = total + jnp.sum(value, axis=0, keepdims=True)
        down_in[rows, :] = value.astype(BF16)
    g_sum[...] = total
    for low in range(0, UNITS, HALF):
        cols = slice(low, low + HALF)
        grad = dot(down_in[...], down_w[:, cols]) * slope[:, cols].astype(F32)
        grad = grad.astype(BF16)
        up_in[:, cols] = grad
        up_sum[:, cols] = jnp.sum(grad.astype(F32), axis=0, keepdims=True)
    part[...] = dot_rows(up_in[...], up_w[...]).astype(BF16)


def norm_chunk(values, gain_row, upstream):
    normal, inverse = norm_parts(values)
    gain_grad = jnp.sum(upstream * normal, axis=0, keepdims=True)
    shift_grad = jnp.sum(upstream, axis=0, keepdims=True)
    scaled = upstream * gain_row
    back = inverse * (
        scaled
        - jnp.mean(scaled, axis=-1, keepdims=True)
        - normal * jnp.mean(scaled * normal, axis=-1, keepdims=True)
    )
    return back, gain_grad, shift_grad


def attention_back(
    g_ref, own, other, middle, rows_ref, qkv_w, out_w, qkv,
    middle_g, out_in, proj_g, part, sums, proj_sum, attended_g,
):
    totals = [jnp.zeros((1, WIDTH), F32)] * 3
    for rows in chunks_of(g_ref):
        grad = own[rows, :].astype(F32) + other[rows, :].astype(F32)
        back, gain, shift = norm_chunk(middle[rows, :], rows_ref[1:2, :], grad)
        value = g_ref[rows, :] + back
        middle_g[rows, :] = value
        out_in[rows, :] = value.astype(BF16)
        bias = jnp.sum(value, axis=0, keepdims=True)
        totals = [t + v for t, v in zip(totals, (gain, shift, bias))]
    for k in range(3):
        sums[k : k + 1, :] = totals[k]
    attended_g[...] = dot(out_in[...], out_w[...]).astype(BF16)
    masks = pair_masks()
    for low in range(0, HALF, PAIR):
        spots = [slice(k * HALF + low, k * HALF + low + PAIR) for k in range(3)]
        query, key, value = (qkv[:, spot] for spot in spots)
        grad = attended_g[:, low : low + PAIR]
        found = [jnp.zeros((query.shape[0], PAIR), F32)] * 3
        for mask in masks:
            scaled = (mask * 0.125).astype(BF16)
            scores = dot_rows(key, query * scaled)
            weight = jnp.exp(scores - jnp.max(scores, axis=0, keepdims=True))
            probs = weight * (1.0 / jnp.sum(weight, axis=0, keepdims=True))
            prob_g = dot_rows(value, grad * mask)
            delta = jnp.sum(probs * prob_g, axis=0, keepdims=True)
            score_g = (probs * (prob_g - delta)).astype(BF16)
            found[0] = found[0] + dot_columns(score_g, key * scaled)
            found[1] = found[1] + dot(score_g, query * scaled)
            found[2] = found[2] + dot(probs.astype(BF16), grad * mask)
        for spot, values in zip(spots, found):
            values = values.astype(BF16)
            proj_g[:, spot] = values
            proj_sum[:, spot] = jnp.sum(values.astype(F32), axis=0, keepdims=True)
    part[...] = dot_rows(proj_g[...], qkv_w[...]).astype(BF16)


def stream_back(middle_g, own, other, x_ref, rows_ref, stream_g, sums):
    totals = [jnp.zeros((1, WIDTH), F32)] * 2
    for rows in chunks_of(x_ref):
        grad = own[rows, :].astype(F32) + other[rows, :].astype(F32)
        back, gain, shift = norm_chunk(x_ref[rows, :], rows_ref[0:1, :], grad)
        stream_g[rows, :] = middle_g[rows, :] + back
        totals = [t + v for t, v in zip(totals, (gain, shift))]
    for k in range(2):
        sums[k : k + 1, :] = totals[k]


def layer_ahead(stream, weights, shared, qv_b, up_b):
    qkv_w, out_w, up_w, down_w = weights
    length = stream.shape[0]
    bias = jnp.concatenate([qv_b[:1], jnp.zeros((1, HALF), F32), qv_b[1:]], axis=1)
    narrow, wide = ((length, WIDTH), BF16), ((length, UNITS), BF16)
    first, qkv, attended, part = call(
        attention_ahead,
        2,
        [narrow, ((length, COLS), BF16), ((length, HALF), BF16), narrow],
        stream, shared, qkv_w, bias, out_w,
    )
    middle, second, hidden, slope, down_part = call(
        units_ahead,
        4,
        [((length, WIDTH), F32), narrow, wide, wide, narrow],
        stream, part, trade(part), shared, up_w, up_b, down_w,
    )
    down_out = down_part.astype(F32) + trade(down_part).astype(F32)
    block_out = middle + down_out + shared[5:6]
    return block_out, (stream, first, qkv, attended, middle, second, hidden, slope)


def layer_back(upstream, stored, weights, shared, pending=None):
    qkv_w, out_w, up_w, down_w = weights
    stream, first, qkv, attended, middle, second, hidden, slope = stored
    length = stream.shape[0]
    narrow, wide = ((length, WIDTH), BF16), ((length, UNITS), BF16)
    down_in, up_in, part, down_bias_g, up_bias_g = call(
        units_back,
        4,
        [narrow, wide, narrow, ((1, WIDTH), F32), ((1, UNITS), F32)],
        upstream, slope, up_w, down_w,
    )
    axes = PHASES[2]
    if pending:
        sums, moving = pending
        moving = reduce_next(sums, after(moving, part), axes, 2)
    other = trade(part)
    down_g = dot_columns(down_in, hidden).astype(BF16)
    up_g = dot_columns(second, up_in).astype(BF16)
    middle_g, out_in, proj_g, part, middle_sums, proj_sums, _ = call(
        attention_back,
        5,
        [
            ((length, WIDTH), F32), narrow, ((length, COLS), BF16), narrow,
            ((3, WIDTH), F32), ((1, COLS), F32), ((length, HALF), BF16),
        ],
        upstream, part, other, middle, shared, qkv_w, out_w, qkv,
    )
    if pending:
        moving = reduce_next(sums, after(moving, part), axes, 1)
        pending = reduce_add(sums, moving, axes, 0)
    other = trade(part)
    out_g = dot_columns(out_in, attended).astype(BF16)
    qkv_g = dot_columns(first, proj_g).astype(BF16)
    stream_g, stream_sums = call(
        stream_back,
        1,
        [((length, WIDTH), F32), ((2, WIDTH), F32)],
        middle_g, part, other, stream, shared,
    )
    qv_g = jnp.concatenate([proj_sums[:, :HALF], proj_sums[:, 2 * HALF :]])
    shared_g = jnp.concatenate(
        [
            stream_sums[:1], middle_sums[:1], stream_sums[1:],
            middle_sums[2:], middle_sums[1:2], down_bias_g,
        ]
    )
    parts = grad_parts(qkv_g, out_g, up_g, down_g)
    return stream_g, (parts, reduce_first(parts, axes)), pending, shared_g, qv_g, up_bias_g


def whole_image(rows):
    rows = swap(rows)
    other = trade(rows)
    core = lax.axis_index("c")
    out = put(jnp.zeros((2,) + rows.shape, rows.dtype), rows, core)
    return put(out, other, 1 - core).reshape(-1, WIDTH)


def image_half(values):
    return swap(take(values.reshape(2, -1, WIDTH), lax.axis_index("c")))[None]


def body(
    tokens,
    cotangent,
    owner,
    norm_gains,
    shifts,
    qkv_weight,
    qv_bias,
    out_weight,
    up_weight,
    up_bias,
    down_weight,
):
    z, xl, y, xh = (lax.axis_index(name) for name in ("z", "xl", "y", "xh"))
    image_no = ((z * 2 + xl) * 4 + y) * 2 + xh
    live_flag = jnp.sum((owner == image_no).astype(F32))
    position = lax.broadcasted_iota(jnp.int32, (WIDTH, WIDTH), 1)
    lead, rest = position // 96, position % 96
    natural = lead * 96 + ((rest % 48) // ROWS) * 24 + (rest // 48) * ROWS + rest % ROWS
    reorder = (lax.broadcasted_iota(jnp.int32, (WIDTH, WIDTH), 0) == natural).astype(BF16)
    maps = small_maps()
    packed = pack_small(norm_gains, shifts, qv_bias, up_bias)
    weights, packed = fetch_weights(qkv_weight, out_weight, up_weight, down_weight, packed)
    shared, qv_b, up_b = fetch_small(packed, maps)
    stream = dot(whole_image(tokens[0]), reorder)
    cotangent, _ = lax.optimization_barrier((cotangent, weights[0][0]))
    upstream = dot(whole_image(cotangent[0]), reorder) * live_flag
    stored = []
    for number in range(LAYERS):
        stream, kept = layer_ahead(stream, weights[number], shared[number], qv_b[number], up_b[number])
        stored.append(kept)
    mixed_out = image_half(dot_rows((stream * live_flag).astype(BF16), reorder).astype(BF16))
    grads, shared_g, qv_g, up_g = ([None] * LAYERS for _ in range(4))
    pending = None
    for number in reversed(range(LAYERS)):
        upstream, pending, above, shared_g[number], qv_g[number], up_g[number] = layer_back(
            upstream, stored[number], weights[number], shared[number], pending
        )
        if above:
            grads[number + 1] = above
        if number:
            upstream, mixed_out = lax.optimization_barrier((upstream, mixed_out))
    sums, moving = pending
    for offset in (2, 1):
        moving = reduce_next(sums, moving, PHASES[2], offset)
    grads[0] = reduce_add(sums, moving, PHASES[2], 0)
    small = sum([shared_g, qv_g, up_g], [])
    (qkv_g, out_g, up_w_g, down_g), upstream, small = return_weights(grads, upstream, small)
    input_grad = image_half(dot_rows(upstream.astype(BF16), reorder).astype(BF16))
    gains_g, shifts_g, qv_bias_g, up_bias_g = return_small(
        small[:2], small[2:4], small[4:], maps
    )
    return (
        mixed_out,
        input_grad,
        gains_g,
        shifts_g,
        qkv_g,
        qv_bias_g,
        out_g,
        up_w_g,
        up_bias_g,
        down_g,
    )


def solution(mesh):
    parts = Mesh(mesh.devices.reshape(SIZES), AXES)
    return jax.shard_map(
        body,
        mesh=parts,
        in_specs=(
            P(REPLICA, "xh", None),
            P(REPLICA, "xh", None),
            P(),
            P(None, None, REPLICA),
            P(None, None, REPLICA),
            P(None, REPLICA, None, "xh"),
            P(None, None, "xh", REPLICA),
            P(None, "xh", REPLICA),
            P(None, REPLICA, "xh"),
            P(None, "xh", REPLICA),
            P(None, "xh", REPLICA),
        ),
        out_specs=(
            P(REPLICA, "xh", None),
            P(REPLICA, "xh", None),
            P(None, None, REPLICA),
            P(None, None, REPLICA),
            P(None, REPLICA, None, "xh"),
            P(None, None, "xh", REPLICA),
            P(None, "xh", REPLICA),
            P(None, REPLICA, "xh"),
            P(None, "xh", REPLICA),
            P(None, "xh", REPLICA),
        ),
        check_vma=False,
    )
```

```python
import math

import jax
import jax.numpy as jnp
from jax import lax
from jax.experimental import pallas as pl
from jax.experimental.pallas import tpu as pltpu
from jax.sharding import Mesh
from jax.sharding import PartitionSpec as P

HEAD = 64
LAYERS = 2
WIDTH = 768
HALF = WIDTH // 2
UNITS = 1536
COLS = 1152
ROWS = 12
F32 = jnp.float32
BF16 = jnp.bfloat16
epsilon = 1e-06

SIZES = (4, 2, 4, 2, 2)
AXES = ("z", "xl", "y", "c", "xh")
REPLICA = ("z", "xl", "y", "c")

RING = {"z": (0, 1, 2, 3), "y": (0, 1, 2, 3), "x": (0, 2, 1, 3)}
NAMES = {"z": "z", "y": "y", "x": ("xl", "xh")}


def hop(values, axis, steps):
    ring = RING[axis]
    return lax.ppermute(
        values, NAMES[axis], [(ring[i], ring[(i + steps) % 4]) for i in range(4)]
    )


def slot_of(axis, offset):
    if axis == "x":
        slot = (lax.axis_index("xl") + 2 * lax.axis_index("xh") + offset) % 4
        return (slot % 2) * 2 + slot // 2
    return (lax.axis_index(axis) + offset) % 4


def put(out, values, place):
    return lax.dynamic_update_slice(out, values[None], (place,) + (0,) * values.ndim)


def take(values, place):
    return lax.dynamic_index_in_dim(values, place, 0, keepdims=False)


def round_hop(values, axis):
    ring = RING[axis]
    pairs = []
    for core in range(2):
        for i in range(4):
            src, dst = ring[i], ring[(i + 1 - 2 * core) % 4]
            if axis == "x":
                spot = lambda at: (at // 2) * 4 + core * 2 + at % 2
            else:
                spot = lambda at: at * 2 + core
            pairs.append((spot(src), spot(dst)))
    names = ("xl", "c", "xh") if axis == "x" else (axis, "c")
    return lax.ppermute(values, names, pairs)


def core_slot(axis, offset):
    return slot_of(axis, offset * (1 - 2 * lax.axis_index("c")))


def together(values):
    return list(lax.optimization_barrier(tuple(values)))


def plus(first, *others):
    total = first.astype(F32)
    for other in others:
        total = total + other.astype(F32)
    return total.astype(BF16)


def assemble(pieces):
    out = jnp.zeros((4,) + pieces[0][1].shape, pieces[0][1].dtype)
    for place, block in pieces:
        out = put(out, block, place)
    return out


def after(values, *others):
    tied = lax.optimization_barrier((tuple(values), others))
    return list(tied[0])


def blocks_round(arrays, axes):
    found = [[v] for v in arrays]
    for _ in range(1, 4):
        arrays = [round_hop(v, axis) for v, axis in zip(arrays, axes)]
        for blocks, v in zip(found, arrays):
            blocks.append(v)
    return found


def slots_round(axis):
    return [core_slot(axis, -step) for step in range(4)]


def gather_round(arrays, axes):
    return [
        assemble(list(zip(slots_round(axis), blocks)))
        for axis, blocks in zip(axes, blocks_round(arrays, axes))
    ]


def reduce_first(arrays, axes):
    moving = [take(v, core_slot(axis, 3)) for v, axis in zip(arrays, axes)]
    return [round_hop(m, axis) for m, axis in zip(moving, axes)]


def reduce_add(arrays, moving, axes, offset):
    return [
        plus(take(v, core_slot(axis, offset)), m) for v, m, axis in zip(arrays, moving, axes)
    ]


def reduce_next(arrays, moving, axes, offset):
    moving = reduce_add(arrays, moving, axes, offset)
    return [round_hop(m, axis) for m, axis in zip(moving, axes)]


PHASES = (("x", "y", "z"), ("y", "z", "x"), ("z", "x", "y"))


SEGMENTS = (
    ((0, 0, 0, COLS),),
    ((1, 0, 0, HALF), (2, 0, HALF, WIDTH)),
    ((2, WIDTH, 0, WIDTH), (3, 0, WIDTH, HALF)),
    ((3, HALF, 0, COLS),),
)
SHAPES = (COLS, HALF, UNITS, UNITS)


def lay_out(slots, *refs):
    blocks, weights = refs[:12], refs[12:]
    for number, block in enumerate(blocks):
        slot = slots[number]
        for y in range(4):

            def go(block=block, slot=slot, y=y, part=number // 4):
                for which, low, start, width in SEGMENTS[y]:
                    weight, to = weights[which], slice(low, low + width)
                    come = slice(start, start + width)
                    if part == 0:
                        weight[slot, :, 0, :, to] = block[y, :, :, come]
                    elif part == 1:
                        weight[:, slot, 1, :, to] = block[:, y, :, come]
                    else:
                        for x in range(4):
                            weight[:, x, 2, :, to] = block[x, :, :, come]

            if number < 8:
                go()
            else:
                pl.when(slot == y)(go)


def gather_chips(slab):
    parts = together([slab[0], slab[1], slab[2]])
    parts = together(gather_round(parts, PHASES[0]))
    parts = together(gather_round(parts, PHASES[1]))
    slots = jnp.stack(sum([slots_round(axis) for axis in PHASES[2]], [])).astype(jnp.int32)
    layers, last = [], []
    for number in range(LAYERS):
        found = together([part[:, :, number] for part in parts] + last)[:3]
        found = blocks_round(found, PHASES[2])
        last = [blocks[3] for blocks in found]
        weights = pl.pallas_call(
            lay_out,
            in_specs=[pl.BlockSpec(memory_space=pltpu.SMEM)]
            + [pl.BlockSpec(memory_space=pltpu.VMEM)] * 12,
            out_specs=[pl.BlockSpec(memory_space=pltpu.VMEM)] * 4,
            out_shape=[jax.ShapeDtypeStruct((4, 4, 3, 16, n), BF16) for n in SHAPES],
            compiler_params=pltpu.CompilerParams(vmem_limit_bytes=40 * 2**20),
        )(slots, *sum(found, []))
        layers.append(tuple(w.reshape(WIDTH, w.shape[-1]) for w in weights))
    return layers


def ring_order(first, second, third):
    return together(
        [jnp.swapaxes(first, 1, 2), jnp.swapaxes(second, 0, 1), jnp.swapaxes(third, 0, 2)]
    )


def reduce_direct(arrays, axes):
    out = []
    for v, axis in zip(arrays, axes):
        mine, after, across, before = (take(v, slot_of(axis, n)) for n in range(4))
        out.append((mine, hop(after, axis, 1), hop(before, axis, -1), hop(across, axis, 2)))
    return [plus(*found) for found in out]


def reduce_chips(layers, stream_g):
    axes = PHASES[1]
    parts = together([jnp.stack(found, axis=2) for found in zip(*layers)])
    moving = reduce_first(parts, axes)
    (stream_g,) = after([stream_g], *moving)
    moving = reduce_next(parts, moving, axes, 2)
    moving = reduce_next(parts, moving, axes, 1)
    parts = together(reduce_add(parts, moving, axes, 0))
    return jnp.stack(reduce_direct(parts, PHASES[0])), stream_g


def turn(values, step):
    pairs = [
        (y * 4 + c * 2 + h, ((y + step) % 4) * 4 + h * 2 + c)
        for y in range(4)
        for c in range(2)
        for h in range(2)
    ]
    return lax.ppermute(values, ("y", "c", "xh"), pairs)


def swap(values):
    return lax.ppermute(values, ("c", "xh"), [(0, 0), (1, 2), (2, 1), (3, 3)])


def trade(values):
    return lax.ppermute(values, "c", [(0, 1), (1, 0)])


def fetch_weights(qkv_w, out_w, up_w, down_w):
    packed = jnp.concatenate(
        [
            qkv_w.reshape(LAYERS, ROWS, 3 * HALF),
            jnp.swapaxes(out_w, 1, 2),
            up_w,
            jnp.swapaxes(down_w, 1, 2),
        ],
        axis=2,
    ).reshape(LAYERS, ROWS, 4, COLS)
    packed = jnp.moveaxis(packed, 2, 0)
    slab = jnp.zeros((4, LAYERS, ROWS, COLS), BF16)
    y = lax.axis_index("y")
    for step in range(4):
        slab = put(slab, turn(take(packed, (y + step) % 4), step), (y - step) % 4)
    slab = jnp.moveaxis(slab, 0, 1).reshape(LAYERS, 3, 16, COLS)
    return gather_chips(jnp.moveaxis(slab, 1, 0))


def grad_parts(qkv_g, out_g, up_g, down_g):
    whole = jnp.stack(
        [
            qkv_g,
            jnp.concatenate([out_g, up_g[:, :WIDTH]], axis=1),
            jnp.concatenate([up_g[:, WIDTH:], down_g[:, :HALF]], axis=1),
            down_g[:, HALF:],
        ]
    ).reshape(4, 4, 4, 3, 16, COLS)
    return ring_order(*(jnp.moveaxis(whole[:, :, :, k], 0, 2) for k in range(3)))


def return_weights(layers, stream_g):
    slab, stream_g = reduce_chips(layers, stream_g)
    slab = jnp.moveaxis(slab, 0, 1).reshape(LAYERS, 4, ROWS, COLS)
    slab = jnp.moveaxis(slab, 1, 0)
    out = jnp.zeros((4, LAYERS, ROWS, COLS), BF16)
    y = lax.axis_index("y")
    for step in range(4):
        out = put(out, turn(take(slab, (y + step) % 4), step), (y - step) % 4)
    out = jnp.moveaxis(out, 0, 2).reshape(LAYERS, ROWS, 4 * COLS).astype(F32)
    grads = (
        out[:, :, :COLS].reshape(LAYERS, ROWS, 3, HALF),
        jnp.swapaxes(out[:, :, COLS : COLS + HALF], 1, 2),
        out[:, :, COLS + HALF : COLS + HALF + UNITS],
        jnp.swapaxes(out[:, :, COLS + HALF + UNITS :], 1, 2),
    )
    return grads, stream_g


def small_maps():
    core = lax.axis_index("c")

    def grid(columns):
        return (
            lax.broadcasted_iota(jnp.int32, (128, columns), 0),
            lax.broadcasted_iota(jnp.int32, (128, columns), 1),
        )

    device, f = grid(WIDTH)
    owner = (f // 96) * 8 + ((f % 48) // ROWS) * 2 + (f % 96) // 48
    whole = device // 2 == owner
    first = device == owner * 2
    device, f = grid(HALF)
    qv = device == (f // 6) * 2 + core
    device, f = grid(UNITS)
    up = device == (f // 24) * 2 + core

    def pick(rows, columns, period):
        row = lax.broadcasted_iota(jnp.int32, (rows, columns), 0)
        return (row == lax.broadcasted_iota(jnp.int32, (rows, columns), 1) % period).astype(F32)

    return (
        tuple(m.astype(BF16) for m in (first, whole, qv, up)),
        (pick(16, WIDTH, ROWS), pick(16, HALF, 6), pick(32, UNITS, 24)),
    )


def pack_small(gains, shifts, qv_b, up_b):

    def widen(values, width):
        return jnp.pad(values, ((0, 0),) * (values.ndim - 1) + ((0, width - values.shape[-1]),))

    return jnp.concatenate(
        [
            widen(jnp.concatenate([gains, shifts], axis=1), 16).reshape(-1),
            widen(qv_b.reshape(LAYERS, 2, 6), 16).reshape(-1),
            widen(up_b.reshape(LAYERS, 24), 32).reshape(-1),
            jnp.zeros((64,), BF16),
        ]
    )


def fetch_small(packed, maps):
    (first, _, qv_map, up_map), (pick, qv_pick, up_pick) = maps
    copies = jnp.broadcast_to(packed.reshape(1, 3, 128), (128, 3, 128))
    every = lax.all_to_all(copies, AXES, split_axis=0, concat_axis=0, tiled=True)
    every = every.reshape(128, 384)
    shared = dot_columns(every[:, :192], first).reshape(LAYERS, 6, 16, WIDTH)
    qv = dot_columns(every[:, 192:256], qv_map).reshape(LAYERS, 2, 16, HALF)
    up = dot_columns(every[:, 256:320], up_map).reshape(LAYERS, 1, 32, UNITS)
    return (
        jnp.sum(shared * pick, axis=2),
        jnp.sum(qv * qv_pick, axis=2),
        jnp.sum(up * up_pick, axis=2),
    )


def return_small(shared, qv, up, maps):
    (_, whole, qv_map, up_map), (pick, qv_pick, up_pick) = maps

    def spread(rows, table):
        rows = jnp.concatenate(rows)[:, None, :] * table
        return rows.reshape(-1, rows.shape[-1]).astype(BF16)

    chunks = jnp.concatenate(
        [
            0.5 * dot_rows(whole, spread(shared, pick)),
            dot_rows(qv_map, spread(qv, qv_pick)),
            dot_rows(up_map, spread(up, up_pick)),
            jnp.zeros((128, 64), F32),
        ],
        axis=1,
    ).reshape(128, 3, 128)
    mine = lax.all_to_all(chunks, AXES, split_axis=0, concat_axis=0, tiled=True)
    mine = jnp.sum(mine, axis=0).reshape(384)
    shared = mine[:192].reshape(LAYERS, 6, 16)[:, :, :ROWS]
    return (
        shared[:, :2],
        shared[:, 2:],
        mine[192:256].reshape(LAYERS, 2, 1, 16)[:, :, :, :6],
        mine[256:320].reshape(LAYERS, 1, 32)[:, :, :24],
    )


def norm_parts(values):
    average = jnp.mean(values, axis=-1, keepdims=True)
    centred = values - average
    spread = jnp.mean(centred * centred, axis=-1, keepdims=True)
    inverse = lax.rsqrt(spread + epsilon)
    return centred * inverse, inverse


def dot(a, b):
    return jnp.dot(a, b, preferred_element_type=F32)


def dot_rows(a, b):
    return lax.dot_general(a, b, (((1,), (1,)), ((), ())), preferred_element_type=F32)


def dot_columns(a, b):
    return lax.dot_general(a, b, (((0,), (0,)), ((), ())), preferred_element_type=F32)


def gelu_parts(up_act):
    cumulative = 0.5 * (1.0 + lax.erf(up_act * (1.0 / math.sqrt(2.0))))
    density = jnp.exp(-0.5 * up_act * up_act) * (1.0 / math.sqrt(2.0 * math.pi))
    return cumulative, density


CHUNK = 128
PAIR = 2 * HEAD


def call(kernel, flops, outs, *args):
    return pl.pallas_call(
        kernel,
        cost_estimate=pl.CostEstimate(
            flops=flops * 10**9,
            bytes_accessed=8 * 2**20,
            transcendentals=2**20,
        ),
        out_shape=[jax.ShapeDtypeStruct(shape, kind) for shape, kind in outs],
        compiler_params=pltpu.CompilerParams(vmem_limit_bytes=50 * 2**20),
    )(*args)


def chunks_of(ref):
    return [pl.ds(start, CHUNK) for start in range(0, ref.shape[0], CHUNK)]


def pair_masks():
    lane = lax.broadcasted_iota(jnp.int32, (1, PAIR), 1)
    return (lane < HEAD).astype(BF16), (lane >= HEAD).astype(BF16)


def attention_ahead(x_ref, rows_ref, qkv_w, bias, out_w, first, qkv, attended, part):
    for rows in chunks_of(x_ref):
        normal = norm_parts(x_ref[rows, :])[0]
        first[rows, :] = (normal * rows_ref[0:1, :] + rows_ref[2:3, :]).astype(BF16)
    qkv[...] = (dot(first[...], qkv_w[...]) + bias[...]).astype(BF16)
    masks = pair_masks()
    for low in range(0, HALF, PAIR):
        query = qkv[:, low : low + PAIR]
        key = qkv[:, HALF + low : HALF + low + PAIR]
        value = qkv[:, 2 * HALF + low : 2 * HALF + low + PAIR]
        total = jnp.zeros((query.shape[0], PAIR), F32)
        for mask in masks:
            scores = dot_rows(query * (mask * 0.125).astype(BF16), key)
            weight = jnp.exp(scores - jnp.max(scores, axis=-1, keepdims=True))
            inverse = 1.0 / jnp.sum(weight, axis=-1, keepdims=True)
            total = total + dot((weight * inverse).astype(BF16), value * mask)
        attended[:, low : low + PAIR] = total.astype(BF16)
    part[...] = dot_rows(attended[...], out_w[...]).astype(BF16)


def units_ahead(
    x_ref, own, other, rows_ref, up_w, up_b, down_w, middle, second, hidden, slope, part
):
    for rows in chunks_of(x_ref):
        value = x_ref[rows, :] + (own[rows, :].astype(F32) + other[rows, :].astype(F32))
        value = value + rows_ref[3:4, :]
        middle[rows, :] = value
        normal = norm_parts(value)[0]
        second[rows, :] = (normal * rows_ref[1:2, :] + rows_ref[4:5, :]).astype(BF16)
    for low in range(0, UNITS, HALF):
        cols = slice(low, low + HALF)
        up_act = dot(second[...], up_w[:, cols]) + up_b[:, cols]
        cumulative, density = gelu_parts(up_act)
        hidden[:, cols] = (up_act * cumulative).astype(BF16)
        slope[:, cols] = (cumulative + up_act * density).astype(BF16)
    part[...] = dot_rows(hidden[...], down_w[...]).astype(BF16)


def units_back(g_ref, slope, up_w, down_w, down_in, up_in, part, g_sum, up_sum):
    total = jnp.zeros((1, WIDTH), F32)
    for rows in chunks_of(g_ref):
        value = g_ref[rows, :]
        total = total + jnp.sum(value, axis=0, keepdims=True)
        down_in[rows, :] = value.astype(BF16)
    g_sum[...] = total
    for low in range(0, UNITS, HALF):
        cols = slice(low, low + HALF)
        grad = dot(down_in[...], down_w[:, cols]) * slope[:, cols].astype(F32)
        grad = grad.astype(BF16)
        up_in[:, cols] = grad
        up_sum[:, cols] = jnp.sum(grad.astype(F32), axis=0, keepdims=True)
    part[...] = dot_rows(up_in[...], up_w[...]).astype(BF16)


def norm_chunk(values, gain_row, upstream):
    normal, inverse = norm_parts(values)
    gain_grad = jnp.sum(upstream * normal, axis=0, keepdims=True)
    shift_grad = jnp.sum(upstream, axis=0, keepdims=True)
    scaled = upstream * gain_row
    back = inverse * (
        scaled
        - jnp.mean(scaled, axis=-1, keepdims=True)
        - normal * jnp.mean(scaled * normal, axis=-1, keepdims=True)
    )
    return back, gain_grad, shift_grad


def attention_back(
    g_ref, own, other, middle, rows_ref, qkv_w, out_w, qkv,
    middle_g, out_in, proj_g, part, sums, proj_sum, attended_g,
):
    totals = [jnp.zeros((1, WIDTH), F32)] * 3
    for rows in chunks_of(g_ref):
        grad = own[rows, :].astype(F32) + other[rows, :].astype(F32)
        back, gain, shift = norm_chunk(middle[rows, :], rows_ref[1:2, :], grad)
        value = g_ref[rows, :] + back
        middle_g[rows, :] = value
        out_in[rows, :] = value.astype(BF16)
        bias = jnp.sum(value, axis=0, keepdims=True)
        totals = [t + v for t, v in zip(totals, (gain, shift, bias))]
    for k in range(3):
        sums[k : k + 1, :] = totals[k]
    attended_g[...] = dot(out_in[...], out_w[...]).astype(BF16)
    masks = pair_masks()
    for low in range(0, HALF, PAIR):
        spots = [slice(k * HALF + low, k * HALF + low + PAIR) for k in range(3)]
        query, key, value = (qkv[:, spot] for spot in spots)
        grad = attended_g[:, low : low + PAIR]
        found = [jnp.zeros((query.shape[0], PAIR), F32)] * 3
        for mask in masks:
            scaled = (mask * 0.125).astype(BF16)
            scores = dot_rows(key, query * scaled)
            weight = jnp.exp(scores - jnp.max(scores, axis=0, keepdims=True))
            probs = weight * (1.0 / jnp.sum(weight, axis=0, keepdims=True))
            prob_g = dot_rows(value, grad * mask)
            delta = jnp.sum(probs * prob_g, axis=0, keepdims=True)
            score_g = (probs * (prob_g - delta)).astype(BF16)
            found[0] = found[0] + dot_columns(score_g, key * scaled)
            found[1] = found[1] + dot(score_g, query * scaled)
            found[2] = found[2] + dot(probs.astype(BF16), grad * mask)
        for spot, values in zip(spots, found):
            values = values.astype(BF16)
            proj_g[:, spot] = values
            proj_sum[:, spot] = jnp.sum(values.astype(F32), axis=0, keepdims=True)
    part[...] = dot_rows(proj_g[...], qkv_w[...]).astype(BF16)


def stream_back(middle_g, own, other, x_ref, rows_ref, stream_g, sums):
    totals = [jnp.zeros((1, WIDTH), F32)] * 2
    for rows in chunks_of(x_ref):
        grad = own[rows, :].astype(F32) + other[rows, :].astype(F32)
        back, gain, shift = norm_chunk(x_ref[rows, :], rows_ref[0:1, :], grad)
        stream_g[rows, :] = middle_g[rows, :] + back
        totals = [t + v for t, v in zip(totals, (gain, shift))]
    for k in range(2):
        sums[k : k + 1, :] = totals[k]


def layer_ahead(stream, weights, shared, qv_b, up_b):
    qkv_w, out_w, up_w, down_w = weights
    length = stream.shape[0]
    bias = jnp.concatenate([qv_b[:1], jnp.zeros((1, HALF), F32), qv_b[1:]], axis=1)
    narrow, wide = ((length, WIDTH), BF16), ((length, UNITS), BF16)
    first, qkv, attended, part = call(
        attention_ahead,
        2,
        [narrow, ((length, COLS), BF16), ((length, HALF), BF16), narrow],
        stream, shared, qkv_w, bias, out_w,
    )
    middle, second, hidden, slope, down_part = call(
        units_ahead,
        4,
        [((length, WIDTH), F32), narrow, wide, wide, narrow],
        stream, part, trade(part), shared, up_w, up_b, down_w,
    )
    down_out = down_part.astype(F32) + trade(down_part).astype(F32)
    block_out = middle + down_out + shared[5:6]
    return block_out, (stream, first, qkv, attended, middle, second, hidden, slope)


def layer_back(upstream, stored, weights, shared, pending=None):
    qkv_w, out_w, up_w, down_w = weights
    stream, first, qkv, attended, middle, second, hidden, slope = stored
    length = stream.shape[0]
    narrow, wide = ((length, WIDTH), BF16), ((length, UNITS), BF16)
    down_in, up_in, part, down_bias_g, up_bias_g = call(
        units_back,
        4,
        [narrow, wide, narrow, ((1, WIDTH), F32), ((1, UNITS), F32)],
        upstream, slope, up_w, down_w,
    )
    axes = PHASES[2]
    if pending:
        sums, moving = pending
        moving = reduce_next(sums, after(moving, upstream), axes, 2)
    other = trade(part)
    down_g = dot_columns(down_in, hidden).astype(BF16)
    up_g = dot_columns(second, up_in).astype(BF16)
    if pending:
        moving = reduce_next(sums, after(moving, part), axes, 1)
    middle_g, out_in, proj_g, part, middle_sums, proj_sums, _ = call(
        attention_back,
        5,
        [
            ((length, WIDTH), F32), narrow, ((length, COLS), BF16), narrow,
            ((3, WIDTH), F32), ((1, COLS), F32), ((length, HALF), BF16),
        ],
        upstream, part, other, middle, shared, qkv_w, out_w, qkv,
    )
    if pending:
        pending = reduce_add(sums, after(moving, part), axes, 0)
    other = trade(part)
    out_g = dot_columns(out_in, attended).astype(BF16)
    qkv_g = dot_columns(first, proj_g).astype(BF16)
    stream_g, stream_sums = call(
        stream_back,
        1,
        [((length, WIDTH), F32), ((2, WIDTH), F32)],
        middle_g, part, other, stream, shared,
    )
    qv_g = jnp.concatenate([proj_sums[:, :HALF], proj_sums[:, 2 * HALF :]])
    shared_g = jnp.concatenate(
        [
            stream_sums[:1], middle_sums[:1], stream_sums[1:],
            middle_sums[2:], middle_sums[1:2], down_bias_g,
        ]
    )
    parts = grad_parts(qkv_g, out_g, up_g, down_g)
    return stream_g, (parts, reduce_first(parts, axes)), pending, shared_g, qv_g, up_bias_g


def whole_image(rows):
    rows = swap(rows)
    other = trade(rows)
    core = lax.axis_index("c")
    out = put(jnp.zeros((2,) + rows.shape, rows.dtype), rows, core)
    return put(out, other, 1 - core).reshape(-1, WIDTH)


def image_half(values):
    return swap(take(values.reshape(2, -1, WIDTH), lax.axis_index("c")))[None]


def body(
    tokens,
    cotangent,
    owner,
    norm_gains,
    shifts,
    qkv_weight,
    qv_bias,
    out_weight,
    up_weight,
    up_bias,
    down_weight,
):
    z, xl, y, xh = (lax.axis_index(name) for name in ("z", "xl", "y", "xh"))
    image_no = ((z * 2 + xl) * 4 + y) * 2 + xh
    live_flag = jnp.sum((owner == image_no).astype(F32))
    position = lax.broadcasted_iota(jnp.int32, (WIDTH, WIDTH), 1)
    lead, rest = position // 96, position % 96
    natural = lead * 96 + ((rest % 48) // ROWS) * 24 + (rest // 48) * ROWS + rest % ROWS
    reorder = (lax.broadcasted_iota(jnp.int32, (WIDTH, WIDTH), 0) == natural).astype(BF16)
    maps = small_maps()
    packed = pack_small(norm_gains, shifts, qv_bias, up_bias)
    weights = fetch_weights(qkv_weight, out_weight, up_weight, down_weight)
    shared, qv_b, up_b = fetch_small(packed, maps)
    stream = dot(whole_image(tokens[0]), reorder)
    cotangent, _ = lax.optimization_barrier((cotangent, weights[0][0]))
    upstream = dot(whole_image(cotangent[0]), reorder) * live_flag
    stored = []
    for number in range(LAYERS):
        stream, kept = layer_ahead(stream, weights[number], shared[number], qv_b[number], up_b[number])
        stored.append(kept)
    mixed_out = image_half(dot_rows((stream * live_flag).astype(BF16), reorder).astype(BF16))
    grads, shared_g, qv_g, up_g = ([None] * LAYERS for _ in range(4))
    pending = None
    for number in reversed(range(LAYERS)):
        upstream, pending, above, shared_g[number], qv_g[number], up_g[number] = layer_back(
            upstream, stored[number], weights[number], shared[number], pending
        )
        if above:
            grads[number + 1] = above
        if number:
            upstream, mixed_out = lax.optimization_barrier((upstream, mixed_out))
    sums, moving = pending
    moving = reduce_next(sums, after(moving, upstream), PHASES[2], 2)
    moving = reduce_next(sums, moving, PHASES[2], 1)
    grads[0] = reduce_add(sums, moving, PHASES[2], 0)
    (qkv_g, out_g, up_w_g, down_g), upstream = return_weights(grads, upstream)
    input_grad = image_half(dot_rows(upstream.astype(BF16), reorder).astype(BF16))
    gains_g, shifts_g, qv_bias_g, up_bias_g = return_small(shared_g, qv_g, up_g, maps)
    return (
        mixed_out,
        input_grad,
        gains_g,
        shifts_g,
        qkv_g,
        qv_bias_g,
        out_g,
        up_w_g,
        up_bias_g,
        down_g,
    )


def solution(mesh):
    parts = Mesh(mesh.devices.reshape(SIZES), AXES)
    return jax.shard_map(
        body,
        mesh=parts,
        in_specs=(
            P(REPLICA, "xh", None),
            P(REPLICA, "xh", None),
            P(),
            P(None, None, REPLICA),
            P(None, None, REPLICA),
            P(None, REPLICA, None, "xh"),
            P(None, None, "xh", REPLICA),
            P(None, "xh", REPLICA),
            P(None, REPLICA, "xh"),
            P(None, "xh", REPLICA),
            P(None, "xh", REPLICA),
        ),
        out_specs=(
            P(REPLICA, "xh", None),
            P(REPLICA, "xh", None),
            P(None, None, REPLICA),
            P(None, None, REPLICA),
            P(None, REPLICA, None, "xh"),
            P(None, None, "xh", REPLICA),
            P(None, "xh", REPLICA),
            P(None, REPLICA, "xh"),
            P(None, "xh", REPLICA),
            P(None, "xh", REPLICA),
        ),
        check_vma=False,
    )
```

```python
import math

import jax
import jax.numpy as jnp
from jax import lax
from jax.experimental import pallas as pl
from jax.experimental.pallas import tpu as pltpu
from jax.sharding import Mesh
from jax.sharding import PartitionSpec as P

HEAD = 64
LAYERS = 2
WIDTH = 768
HALF = WIDTH // 2
UNITS = 1536
COLS = 1152
ROWS = 12
F32 = jnp.float32
BF16 = jnp.bfloat16
epsilon = 1e-06

SIZES = (4, 2, 4, 2, 2)
AXES = ("z", "xl", "y", "c", "xh")
REPLICA = ("z", "xl", "y", "c")

RING = {"z": (0, 1, 2, 3), "y": (0, 1, 2, 3), "x": (0, 2, 1, 3)}
NAMES = {"z": "z", "y": "y", "x": ("xl", "xh")}


def hop(values, axis, steps):
    ring = RING[axis]
    return lax.ppermute(
        values, NAMES[axis], [(ring[i], ring[(i + steps) % 4]) for i in range(4)]
    )


def slot_of(axis, offset):
    if axis == "x":
        slot = (lax.axis_index("xl") + 2 * lax.axis_index("xh") + offset) % 4
        return (slot % 2) * 2 + slot // 2
    return (lax.axis_index(axis) + offset) % 4


def put(out, values, place):
    return lax.dynamic_update_slice(out, values[None], (place,) + (0,) * values.ndim)


def take(values, place):
    return lax.dynamic_index_in_dim(values, place, 0, keepdims=False)


def round_hop(values, axis):
    ring = RING[axis]
    pairs = []
    for core in range(2):
        for i in range(4):
            src, dst = ring[i], ring[(i + 1 - 2 * core) % 4]
            if axis == "x":
                spot = lambda at: (at // 2) * 4 + core * 2 + at % 2
            else:
                spot = lambda at: at * 2 + core
            pairs.append((spot(src), spot(dst)))
    names = ("xl", "c", "xh") if axis == "x" else (axis, "c")
    return lax.ppermute(values, names, pairs)


def core_slot(axis, offset):
    return slot_of(axis, offset * (1 - 2 * lax.axis_index("c")))


def together(values):
    return list(lax.optimization_barrier(tuple(values)))


def plus(first, *others):
    total = first.astype(F32)
    for other in others:
        total = total + other.astype(F32)
    return total.astype(BF16)


def assemble(pieces):
    out = jnp.zeros((4,) + pieces[0][1].shape, pieces[0][1].dtype)
    for place, block in pieces:
        out = put(out, block, place)
    return out


def after(values, *others):
    tied = lax.optimization_barrier((tuple(values), others))
    return list(tied[0])


def blocks_round(arrays, axes):
    found = [[v] for v in arrays]
    for _ in range(1, 4):
        arrays = [round_hop(v, axis) for v, axis in zip(arrays, axes)]
        for blocks, v in zip(found, arrays):
            blocks.append(v)
    return found


def slots_round(axis):
    return [core_slot(axis, -step) for step in range(4)]


def gather_round(arrays, axes):
    return [
        assemble(list(zip(slots_round(axis), blocks)))
        for axis, blocks in zip(axes, blocks_round(arrays, axes))
    ]


def reduce_first(arrays, axes):
    moving = [take(v, core_slot(axis, 3)) for v, axis in zip(arrays, axes)]
    return [round_hop(m, axis) for m, axis in zip(moving, axes)]


def reduce_add(arrays, moving, axes, offset):
    return [
        plus(take(v, core_slot(axis, offset)), m) for v, m, axis in zip(arrays, moving, axes)
    ]


def reduce_next(arrays, moving, axes, offset):
    moving = reduce_add(arrays, moving, axes, offset)
    return [round_hop(m, axis) for m, axis in zip(moving, axes)]


PHASES = (("x", "y", "z"), ("y", "z", "x"), ("z", "x", "y"))


SEGMENTS = (
    ((0, 0, 0, COLS),),
    ((1, 0, 0, HALF), (2, 0, HALF, WIDTH)),
    ((2, WIDTH, 0, WIDTH), (3, 0, WIDTH, HALF)),
    ((3, HALF, 0, COLS),),
)
SHAPES = (COLS, HALF, UNITS, UNITS)


def lay_out(slots, *refs):
    blocks, weights = refs[:12], refs[12:]
    for number, block in enumerate(blocks):
        slot = slots[number]
        for y in range(4):

            def go(block=block, slot=slot, y=y, part=number // 4):
                for which, low, start, width in SEGMENTS[y]:
                    weight, to = weights[which], slice(low, low + width)
                    come = slice(start, start + width)
                    if part == 0:
                        weight[slot, :, 0, :, to] = block[y, :, :, come]
                    elif part == 1:
                        weight[:, slot, 1, :, to] = block[:, y, :, come]
                    else:
                        for x in range(4):
                            weight[:, x, 2, :, to] = block[x, :, :, come]

            if number < 8:
                go()
            else:
                pl.when(slot == y)(go)


def gather_chips(slab):
    parts = together([slab[0], slab[1], slab[2]])
    parts = together(gather_round(parts, PHASES[0]))
    parts = together(gather_round(parts, PHASES[1]))
    slots = jnp.stack(sum([slots_round(axis) for axis in PHASES[2]], [])).astype(jnp.int32)
    layers, last = [], []
    for number in range(LAYERS):
        found = together([part[:, :, number] for part in parts] + last)[:3]
        found = blocks_round(found, PHASES[2])
        last = [blocks[3] for blocks in found]
        weights = pl.pallas_call(
            lay_out,
            in_specs=[pl.BlockSpec(memory_space=pltpu.SMEM)]
            + [pl.BlockSpec(memory_space=pltpu.VMEM)] * 12,
            out_specs=[pl.BlockSpec(memory_space=pltpu.VMEM)] * 4,
            out_shape=[jax.ShapeDtypeStruct((4, 4, 3, 16, n), BF16) for n in SHAPES],
            compiler_params=pltpu.CompilerParams(vmem_limit_bytes=40 * 2**20),
        )(slots, *sum(found, []))
        layers.append(tuple(w.reshape(WIDTH, w.shape[-1]) for w in weights))
    return layers


def ring_order(first, second, third):
    return together(
        [jnp.swapaxes(first, 1, 2), jnp.swapaxes(second, 0, 1), jnp.swapaxes(third, 0, 2)]
    )


def reduce_direct(arrays, axes):
    out = []
    for v, axis in zip(arrays, axes):
        mine, after, across, before = (take(v, slot_of(axis, n)) for n in range(4))
        out.append((mine, hop(after, axis, 1), hop(before, axis, -1), hop(across, axis, 2)))
    return [plus(*found) for found in out]


def reduce_chips(layers, stream_g):
    axes = PHASES[1]
    parts = together([jnp.stack(found, axis=2) for found in zip(*layers)])
    moving = reduce_first(parts, axes)
    (stream_g,) = after([stream_g], *moving)
    moving = reduce_next(parts, moving, axes, 2)
    moving = reduce_next(parts, moving, axes, 1)
    parts = together(reduce_add(parts, moving, axes, 0))
    return jnp.stack(reduce_direct(parts, PHASES[0])), stream_g


def turn(values, step):
    pairs = [
        (y * 4 + c * 2 + h, ((y + step) % 4) * 4 + h * 2 + c)
        for y in range(4)
        for c in range(2)
        for h in range(2)
    ]
    return lax.ppermute(values, ("y", "c", "xh"), pairs)


def swap(values):
    return lax.ppermute(values, ("c", "xh"), [(0, 0), (1, 2), (2, 1), (3, 3)])


def trade(values):
    return lax.ppermute(values, "c", [(0, 1), (1, 0)])


def fetch_weights(qkv_w, out_w, up_w, down_w):
    packed = jnp.concatenate(
        [
            qkv_w.reshape(LAYERS, ROWS, 3 * HALF),
            jnp.swapaxes(out_w, 1, 2),
            up_w,
            jnp.swapaxes(down_w, 1, 2),
        ],
        axis=2,
    ).reshape(LAYERS, ROWS, 4, COLS)
    packed = jnp.moveaxis(packed, 2, 0)
    slab = jnp.zeros((4, LAYERS, ROWS, COLS), BF16)
    y = lax.axis_index("y")
    for step in range(4):
        slab = put(slab, turn(take(packed, (y + step) % 4), step), (y - step) % 4)
    slab = jnp.moveaxis(slab, 0, 1).reshape(LAYERS, 3, 16, COLS)
    return gather_chips(jnp.moveaxis(slab, 1, 0))


def grad_parts(qkv_g, out_g, up_g, down_g):
    whole = jnp.stack(
        [
            qkv_g,
            jnp.concatenate([out_g, up_g[:, :WIDTH]], axis=1),
            jnp.concatenate([up_g[:, WIDTH:], down_g[:, :HALF]], axis=1),
            down_g[:, HALF:],
        ]
    ).reshape(4, 4, 4, 3, 16, COLS)
    return ring_order(*(jnp.moveaxis(whole[:, :, :, k], 0, 2) for k in range(3)))


def return_weights(layers, stream_g):
    slab, stream_g = reduce_chips(layers, stream_g)
    slab = jnp.moveaxis(slab, 0, 1).reshape(LAYERS, 4, ROWS, COLS)
    slab = jnp.moveaxis(slab, 1, 0)
    out = jnp.zeros((4, LAYERS, ROWS, COLS), BF16)
    y = lax.axis_index("y")
    for step in range(4):
        out = put(out, turn(take(slab, (y + step) % 4), step), (y - step) % 4)
    out = jnp.moveaxis(out, 0, 2).reshape(LAYERS, ROWS, 4 * COLS).astype(F32)
    grads = (
        out[:, :, :COLS].reshape(LAYERS, ROWS, 3, HALF),
        jnp.swapaxes(out[:, :, COLS : COLS + HALF], 1, 2),
        out[:, :, COLS + HALF : COLS + HALF + UNITS],
        jnp.swapaxes(out[:, :, COLS + HALF + UNITS :], 1, 2),
    )
    return grads, stream_g


def small_maps():
    core = lax.axis_index("c")

    def grid(columns):
        return (
            lax.broadcasted_iota(jnp.int32, (128, columns), 0),
            lax.broadcasted_iota(jnp.int32, (128, columns), 1),
        )

    device, f = grid(WIDTH)
    owner = (f // 96) * 8 + ((f % 48) // ROWS) * 2 + (f % 96) // 48
    whole = device // 2 == owner
    first = device == owner * 2
    device, f = grid(HALF)
    qv = device == (f // 6) * 2 + core
    device, f = grid(UNITS)
    up = device == (f // 24) * 2 + core

    def pick(rows, columns, period):
        row = lax.broadcasted_iota(jnp.int32, (rows, columns), 0)
        return (row == lax.broadcasted_iota(jnp.int32, (rows, columns), 1) % period).astype(F32)

    return (
        tuple(m.astype(BF16) for m in (first, whole, qv, up)),
        (pick(16, WIDTH, ROWS), pick(16, HALF, 6), pick(32, UNITS, 24)),
    )


def pack_small(gains, shifts, qv_b, up_b):

    def widen(values, width):
        return jnp.pad(values, ((0, 0),) * (values.ndim - 1) + ((0, width - values.shape[-1]),))

    return jnp.concatenate(
        [
            widen(jnp.concatenate([gains, shifts], axis=1), 16).reshape(-1),
            widen(qv_b.reshape(LAYERS, 2, 6), 16).reshape(-1),
            widen(up_b.reshape(LAYERS, 24), 32).reshape(-1),
            jnp.zeros((64,), BF16),
        ]
    )


def fetch_small(packed, maps):
    (first, _, qv_map, up_map), (pick, qv_pick, up_pick) = maps
    copies = jnp.broadcast_to(packed.reshape(1, 3, 128), (128, 3, 128))
    every = lax.all_to_all(copies, AXES, split_axis=0, concat_axis=0, tiled=True)
    every = every.reshape(128, 384)
    shared = dot_columns(every[:, :192], first).reshape(LAYERS, 6, 16, WIDTH)
    qv = dot_columns(every[:, 192:256], qv_map).reshape(LAYERS, 2, 16, HALF)
    up = dot_columns(every[:, 256:320], up_map).reshape(LAYERS, 1, 32, UNITS)
    return (
        jnp.sum(shared * pick, axis=2),
        jnp.sum(qv * qv_pick, axis=2),
        jnp.sum(up * up_pick, axis=2),
    )


def return_small(shared, qv, up, maps):
    (_, whole, qv_map, up_map), (pick, qv_pick, up_pick) = maps

    def spread(rows, table):
        rows = jnp.concatenate(rows)[:, None, :] * table
        return rows.reshape(-1, rows.shape[-1]).astype(BF16)

    chunks = jnp.concatenate(
        [
            0.5 * dot_rows(whole, spread(shared, pick)),
            dot_rows(qv_map, spread(qv, qv_pick)),
            dot_rows(up_map, spread(up, up_pick)),
            jnp.zeros((128, 64), F32),
        ],
        axis=1,
    ).reshape(128, 3, 128)
    mine = lax.all_to_all(chunks, AXES, split_axis=0, concat_axis=0, tiled=True)
    mine = jnp.sum(mine, axis=0).reshape(384)
    shared = mine[:192].reshape(LAYERS, 6, 16)[:, :, :ROWS]
    return (
        shared[:, :2],
        shared[:, 2:],
        mine[192:256].reshape(LAYERS, 2, 1, 16)[:, :, :, :6],
        mine[256:320].reshape(LAYERS, 1, 32)[:, :, :24],
    )


def norm_parts(values):
    average = jnp.mean(values, axis=-1, keepdims=True)
    centred = values - average
    spread = jnp.mean(centred * centred, axis=-1, keepdims=True)
    inverse = lax.rsqrt(spread + epsilon)
    return centred * inverse, inverse


def dot(a, b):
    return jnp.dot(a, b, preferred_element_type=F32)


def dot_rows(a, b):
    return lax.dot_general(a, b, (((1,), (1,)), ((), ())), preferred_element_type=F32)


def dot_columns(a, b):
    return lax.dot_general(a, b, (((0,), (0,)), ((), ())), preferred_element_type=F32)


def gelu_parts(up_act):
    cumulative = 0.5 * (1.0 + lax.erf(up_act * (1.0 / math.sqrt(2.0))))
    density = jnp.exp(-0.5 * up_act * up_act) * (1.0 / math.sqrt(2.0 * math.pi))
    return cumulative, density


CHUNK = 128
PAIR = 2 * HEAD


def call(kernel, flops, outs, *args):
    return pl.pallas_call(
        kernel,
        cost_estimate=pl.CostEstimate(
            flops=flops * 10**9,
            bytes_accessed=8 * 2**20,
            transcendentals=2**20,
        ),
        out_shape=[jax.ShapeDtypeStruct(shape, kind) for shape, kind in outs],
        compiler_params=pltpu.CompilerParams(vmem_limit_bytes=50 * 2**20),
    )(*args)


def chunks_of(ref):
    return [pl.ds(start, CHUNK) for start in range(0, ref.shape[0], CHUNK)]


def pair_masks():
    lane = lax.broadcasted_iota(jnp.int32, (1, PAIR), 1)
    return (lane < HEAD).astype(BF16), (lane >= HEAD).astype(BF16)


def attention_ahead(x_ref, rows_ref, qkv_w, bias, out_w, first, qkv, attended, part):
    for rows in chunks_of(x_ref):
        normal = norm_parts(x_ref[rows, :])[0]
        first[rows, :] = (normal * rows_ref[0:1, :] + rows_ref[2:3, :]).astype(BF16)
    qkv[...] = (dot(first[...], qkv_w[...]) + bias[...]).astype(BF16)
    masks = pair_masks()
    for low in range(0, HALF, PAIR):
        query = qkv[:, low : low + PAIR]
        key = qkv[:, HALF + low : HALF + low + PAIR]
        value = qkv[:, 2 * HALF + low : 2 * HALF + low + PAIR]
        total = jnp.zeros((query.shape[0], PAIR), F32)
        for mask in masks:
            scores = dot_rows(query * (mask * 0.125).astype(BF16), key)
            weight = jnp.exp(scores - jnp.max(scores, axis=-1, keepdims=True))
            inverse = 1.0 / jnp.sum(weight, axis=-1, keepdims=True)
            total = total + dot((weight * inverse).astype(BF16), value * mask)
        attended[:, low : low + PAIR] = total.astype(BF16)
    part[...] = dot_rows(attended[...], out_w[...]).astype(BF16)


def units_ahead(
    x_ref, own, other, rows_ref, up_w, up_b, down_w, middle, second, hidden, slope, part
):
    for rows in chunks_of(x_ref):
        value = x_ref[rows, :] + (own[rows, :].astype(F32) + other[rows, :].astype(F32))
        value = value + rows_ref[3:4, :]
        middle[rows, :] = value
        normal = norm_parts(value)[0]
        second[rows, :] = (normal * rows_ref[1:2, :] + rows_ref[4:5, :]).astype(BF16)
    for low in range(0, UNITS, HALF):
        cols = slice(low, low + HALF)
        up_act = dot(second[...], up_w[:, cols]) + up_b[:, cols]
        cumulative, density = gelu_parts(up_act)
        hidden[:, cols] = (up_act * cumulative).astype(BF16)
        slope[:, cols] = (cumulative + up_act * density).astype(BF16)
    part[...] = dot_rows(hidden[...], down_w[...]).astype(BF16)


def units_back(g_ref, slope, up_w, down_w, down_in, up_in, part, g_sum, up_sum):
    total = jnp.zeros((1, WIDTH), F32)
    for rows in chunks_of(g_ref):
        value = g_ref[rows, :]
        total = total + jnp.sum(value, axis=0, keepdims=True)
        down_in[rows, :] = value.astype(BF16)
    g_sum[...] = total
    for low in range(0, UNITS, HALF):
        cols = slice(low, low + HALF)
        grad = dot(down_in[...], down_w[:, cols]) * slope[:, cols].astype(F32)
        grad = grad.astype(BF16)
        up_in[:, cols] = grad
        up_sum[:, cols] = jnp.sum(grad.astype(F32), axis=0, keepdims=True)
    part[...] = dot_rows(up_in[...], up_w[...]).astype(BF16)


def norm_chunk(values, gain_row, upstream):
    normal, inverse = norm_parts(values)
    gain_grad = jnp.sum(upstream * normal, axis=0, keepdims=True)
    shift_grad = jnp.sum(upstream, axis=0, keepdims=True)
    scaled = upstream * gain_row
    back = inverse * (
        scaled
        - jnp.mean(scaled, axis=-1, keepdims=True)
        - normal * jnp.mean(scaled * normal, axis=-1, keepdims=True)
    )
    return back, gain_grad, shift_grad


def attention_back(
    g_ref, own, other, middle, rows_ref, qkv_w, out_w, qkv,
    middle_g, out_in, proj_g, part, sums, proj_sum, attended_g,
):
    totals = [jnp.zeros((1, WIDTH), F32)] * 3
    for rows in chunks_of(g_ref):
        grad = own[rows, :].astype(F32) + other[rows, :].astype(F32)
        back, gain, shift = norm_chunk(middle[rows, :], rows_ref[1:2, :], grad)
        value = g_ref[rows, :] + back
        middle_g[rows, :] = value
        out_in[rows, :] = value.astype(BF16)
        bias = jnp.sum(value, axis=0, keepdims=True)
        totals = [t + v for t, v in zip(totals, (gain, shift, bias))]
    for k in range(3):
        sums[k : k + 1, :] = totals[k]
    attended_g[...] = dot(out_in[...], out_w[...]).astype(BF16)
    masks = pair_masks()
    for low in range(0, HALF, PAIR):
        spots = [slice(k * HALF + low, k * HALF + low + PAIR) for k in range(3)]
        query, key, value = (qkv[:, spot] for spot in spots)
        grad = attended_g[:, low : low + PAIR]
        found = [jnp.zeros((query.shape[0], PAIR), F32)] * 3
        for mask in masks:
            scaled = (mask * 0.125).astype(BF16)
            scores = dot_rows(key, query * scaled)
            weight = jnp.exp(scores - jnp.max(scores, axis=0, keepdims=True))
            probs = weight * (1.0 / jnp.sum(weight, axis=0, keepdims=True))
            prob_g = dot_rows(value, grad * mask)
            delta = jnp.sum(probs * prob_g, axis=0, keepdims=True)
            score_g = (probs * (prob_g - delta)).astype(BF16)
            found[0] = found[0] + dot_columns(score_g, key * scaled)
            found[1] = found[1] + dot(score_g, query * scaled)
            found[2] = found[2] + dot(probs.astype(BF16), grad * mask)
        for spot, values in zip(spots, found):
            values = values.astype(BF16)
            proj_g[:, spot] = values
            proj_sum[:, spot] = jnp.sum(values.astype(F32), axis=0, keepdims=True)
    part[...] = dot_rows(proj_g[...], qkv_w[...]).astype(BF16)


def stream_back(middle_g, own, other, x_ref, rows_ref, stream_g, sums):
    totals = [jnp.zeros((1, WIDTH), F32)] * 2
    for rows in chunks_of(x_ref):
        grad = own[rows, :].astype(F32) + other[rows, :].astype(F32)
        back, gain, shift = norm_chunk(x_ref[rows, :], rows_ref[0:1, :], grad)
        stream_g[rows, :] = middle_g[rows, :] + back
        totals = [t + v for t, v in zip(totals, (gain, shift))]
    for k in range(2):
        sums[k : k + 1, :] = totals[k]


def layer_ahead(stream, weights, shared, qv_b, up_b):
    qkv_w, out_w, up_w, down_w = weights
    length = stream.shape[0]
    bias = jnp.concatenate([qv_b[:1], jnp.zeros((1, HALF), F32), qv_b[1:]], axis=1)
    narrow, wide = ((length, WIDTH), BF16), ((length, UNITS), BF16)
    first, qkv, attended, part = call(
        attention_ahead,
        2,
        [narrow, ((length, COLS), BF16), ((length, HALF), BF16), narrow],
        stream, shared, qkv_w, bias, out_w,
    )
    middle, second, hidden, slope, down_part = call(
        units_ahead,
        4,
        [((length, WIDTH), F32), narrow, wide, wide, narrow],
        stream, part, trade(part), shared, up_w, up_b, down_w,
    )
    down_out = down_part.astype(F32) + trade(down_part).astype(F32)
    block_out = middle + down_out + shared[5:6]
    return block_out, (stream, first, qkv, attended, middle, second, hidden, slope)


def layer_back(upstream, stored, weights, shared, pending=None):
    qkv_w, out_w, up_w, down_w = weights
    stream, first, qkv, attended, middle, second, hidden, slope = stored
    length = stream.shape[0]
    narrow, wide = ((length, WIDTH), BF16), ((length, UNITS), BF16)
    if pending:
        sums, moving = pending
        upstream, *moving = together([upstream] + moving)
    down_in, up_in, part, down_bias_g, up_bias_g = call(
        units_back,
        4,
        [narrow, wide, narrow, ((1, WIDTH), F32), ((1, UNITS), F32)],
        upstream, slope, up_w, down_w,
    )
    axes = PHASES[2]
    if pending:
        moving = reduce_next(sums, moving, axes, 2)
    other = trade(part)
    down_g = dot_columns(down_in, hidden).astype(BF16)
    up_g = dot_columns(second, up_in).astype(BF16)
    if pending:
        moving = reduce_next(sums, after(moving, part), axes, 1)
    middle_g, out_in, proj_g, part, middle_sums, proj_sums, _ = call(
        attention_back,
        5,
        [
            ((length, WIDTH), F32), narrow, ((length, COLS), BF16), narrow,
            ((3, WIDTH), F32), ((1, COLS), F32), ((length, HALF), BF16),
        ],
        upstream, part, other, middle, shared, qkv_w, out_w, qkv,
    )
    if pending:
        pending = reduce_add(sums, after(moving, part), axes, 0)
    other = trade(part)
    out_g = dot_columns(out_in, attended).astype(BF16)
    qkv_g = dot_columns(first, proj_g).astype(BF16)
    stream_g, stream_sums = call(
        stream_back,
        1,
        [((length, WIDTH), F32), ((2, WIDTH), F32)],
        middle_g, part, other, stream, shared,
    )
    qv_g = jnp.concatenate([proj_sums[:, :HALF], proj_sums[:, 2 * HALF :]])
    shared_g = jnp.concatenate(
        [
            stream_sums[:1], middle_sums[:1], stream_sums[1:],
            middle_sums[2:], middle_sums[1:2], down_bias_g,
        ]
    )
    parts = grad_parts(qkv_g, out_g, up_g, down_g)
    return stream_g, (parts, reduce_first(parts, axes)), pending, shared_g, qv_g, up_bias_g


def whole_image(rows):
    rows = swap(rows)
    other = trade(rows)
    core = lax.axis_index("c")
    out = put(jnp.zeros((2,) + rows.shape, rows.dtype), rows, core)
    return put(out, other, 1 - core).reshape(-1, WIDTH)


def image_half(values):
    return swap(take(values.reshape(2, -1, WIDTH), lax.axis_index("c")))[None]


def body(
    tokens,
    cotangent,
    owner,
    norm_gains,
    shifts,
    qkv_weight,
    qv_bias,
    out_weight,
    up_weight,
    up_bias,
    down_weight,
):
    z, xl, y, xh = (lax.axis_index(name) for name in ("z", "xl", "y", "xh"))
    image_no = ((z * 2 + xl) * 4 + y) * 2 + xh
    live_flag = jnp.sum((owner == image_no).astype(F32))
    position = lax.broadcasted_iota(jnp.int32, (WIDTH, WIDTH), 1)
    lead, rest = position // 96, position % 96
    natural = lead * 96 + ((rest % 48) // ROWS) * 24 + (rest // 48) * ROWS + rest % ROWS
    reorder = (lax.broadcasted_iota(jnp.int32, (WIDTH, WIDTH), 0) == natural).astype(BF16)
    maps = small_maps()
    packed = pack_small(norm_gains, shifts, qv_bias, up_bias)
    weights = fetch_weights(qkv_weight, out_weight, up_weight, down_weight)
    shared, qv_b, up_b = fetch_small(packed, maps)
    stream = dot(whole_image(tokens[0]), reorder)
    cotangent, _ = lax.optimization_barrier((cotangent, weights[0][0]))
    upstream = dot(whole_image(cotangent[0]), reorder) * live_flag
    stored = []
    for number in range(LAYERS):
        stream, kept = layer_ahead(stream, weights[number], shared[number], qv_b[number], up_b[number])
        stored.append(kept)
        if number == 0:
            stream, upstream = lax.optimization_barrier((stream, upstream))
    mixed_out = image_half(dot_rows((stream * live_flag).astype(BF16), reorder).astype(BF16))
    grads, shared_g, qv_g, up_g = ([None] * LAYERS for _ in range(4))
    pending = None
    for number in reversed(range(LAYERS)):
        upstream, pending, above, shared_g[number], qv_g[number], up_g[number] = layer_back(
            upstream, stored[number], weights[number], shared[number], pending
        )
        if above:
            grads[number + 1] = above
        if number:
            upstream, mixed_out = lax.optimization_barrier((upstream, mixed_out))
    sums, moving = pending
    moving = reduce_next(sums, after(moving, upstream), PHASES[2], 2)
    moving = reduce_next(sums, moving, PHASES[2], 1)
    grads[0] = reduce_add(sums, moving, PHASES[2], 0)
    (qkv_g, out_g, up_w_g, down_g), upstream = return_weights(grads, upstream)
    input_grad = image_half(dot_rows(upstream.astype(BF16), reorder).astype(BF16))
    gains_g, shifts_g, qv_bias_g, up_bias_g = return_small(shared_g, qv_g, up_g, maps)
    return (
        mixed_out,
        input_grad,
        gains_g,
        shifts_g,
        qkv_g,
        qv_bias_g,
        out_g,
        up_w_g,
        up_bias_g,
        down_g,
    )


def solution(mesh):
    parts = Mesh(mesh.devices.reshape(SIZES), AXES)
    return jax.shard_map(
        body,
        mesh=parts,
        in_specs=(
            P(REPLICA, "xh", None),
            P(REPLICA, "xh", None),
            P(),
            P(None, None, REPLICA),
            P(None, None, REPLICA),
            P(None, REPLICA, None, "xh"),
            P(None, None, "xh", REPLICA),
            P(None, "xh", REPLICA),
            P(None, REPLICA, "xh"),
            P(None, "xh", REPLICA),
            P(None, "xh", REPLICA),
        ),
        out_specs=(
            P(REPLICA, "xh", None),
            P(REPLICA, "xh", None),
            P(None, None, REPLICA),
            P(None, None, REPLICA),
            P(None, REPLICA, None, "xh"),
            P(None, None, "xh", REPLICA),
            P(None, "xh", REPLICA),
            P(None, REPLICA, "xh"),
            P(None, "xh", REPLICA),
            P(None, "xh", REPLICA),
        ),
        check_vma=False,
    )
```
